32 devices in a mesh: seq: 4 (over z), exp: 8 (over y, x, core).
Axes of the slice: x: 2, y: 2, z: 4, core: 2. Of those that a mesh axis runs over, the one named last changes fastest.
Arguments:
- tokens: bfloat16 [16, 512, 2048], P('exp', 'seq'), may hold values from -6 to 6
- cotangent: bfloat16 [16, 512, 2048], P('exp', 'seq'), may hold values from -6 to 6
- lengths: int32 [16], P('exp'), may hold values from 128 to 512, as said below
- adapter_choice: int32 [16, 8], P('exp'), may hold values from 0 to 1, as said below
- expert_ids: int32 [8, 4, 2, 128, 8], P('exp', 'seq'), may hold values from 0 to 31, all different within a row; in each aligned block of 256 rows (0 to 255, 256 to 511, ..., all dimensions but the last counted through in order) at most 96 rows name the same one
- gate_weights: float32 [8, 4, 2, 128, 8], P('exp', 'seq'), may hold values from 0.0625 to 0.1875
- attn_gain: float32 [2048], replicated, may hold values from 0.5 to 1.5
- moe_gain: float32 [2048], replicated, may hold values from 0.5 to 1.5
- query_gain: float32 [128], replicated, may hold values from 1 to 2
- key_gain: float32 [128], replicated, may hold values from 1 to 2
- w_qkv: bfloat16 [3, 2048, 2048], replicated, may hold values from -0.125 to 0.125
- w_out: bfloat16 [2048, 2048], replicated, may hold values from -0.5 to 0.5
- expert_gate: bfloat16 [32, 2048, 1024], P('exp'), may hold values from -0.125 to 0.125
- expert_up: bfloat16 [32, 2048, 1024], P('exp'), may hold values from -0.125 to 0.125
- expert_down: bfloat16 [32, 1024, 2048], P('exp'), may hold values from -1 to 1
- adapt_down: float32 [8, 4, 2048, 16], P(None, None, 'exp'), may hold values from -0.125 to 0.125
- first_down: float32 [8, 4, 2048, 16], P(None, None, 'exp'), may hold values from -1024 to 1024
- second_down: float32 [8, 4, 2048, 16], P(None, None, 'exp'), may hold values from 36864 to 147456
- adapt_up: float32 [8, 4, 16, 2048], P(None, None, None, 'exp'), may hold values from -1.5 to 1.5
- first_up: float32 [8, 4, 16, 2048], P(None, None, None, 'exp'), may hold values from -192 to 192
- second_up: float32 [8, 4, 16, 2048], P(None, None, None, 'exp'), may hold values from 1024 to 4096
Outputs:
- output: bfloat16 [16, 512, 2048], P('exp', 'seq')
- grad_input: float32 [16, 512, 2048], P('exp', 'seq')
- new_first_down: float32 [8, 4, 2048, 16], P(None, None, 'exp')
- new_second_down: float32 [8, 4, 2048, 16], P(None, None, 'exp')
- new_down: float32 [8, 4, 2048, 16], P(None, None, 'exp')
- new_first_up: float32 [8, 4, 16, 2048], P(None, None, None, 'exp')
- new_second_up: float32 [8, 4, 16, 2048], P(None, None, None, 'exp')
- new_up: float32 [8, 4, 16, 2048], P(None, None, None, 'exp')
The draws below stay inside these ranges and needn't reach their ends.
Inputs may be any that keep to these rules, and one draw needn't show every extreme that they name: `lengths`: in each group of 2 sequences that share an index of exp, one, drawn from the seed, has length 512; the others are at least 128. `adapter_choice`: each row holds a single 1. `expert_ids`: each token names 8 different experts. Among the 256 tokens of one device (one index of exp and of seq) no expert is named more than 96 times, a bound that some block reaches.
All inputs are finite; a program needn't handle non-finite values.
Results may differ from the reference program's by a relative error of at most 0.025.
Values may be sent and summed in bfloat16 or wider, within the bound.
No kernel may reach another device: no remote copies, remote signals or barrier semaphores. Data moves between devices by JAX's collectives and lax.ppermute only.
A program may use at most 384 MiB of HBM per device.

```python
import math
import jax
import jax.numpy as jnp
import numpy as np
from jax import lax

D = 2048
HEADS = 16
HEAD = 128
FF = 1024
TOP = 8
RANK = 16
SETS = 8
SEQ_GRP = 2
SHARD = 128
STEP = 5
EXPERTS = 32
GROUPS = 8
SPLITS = 4
SEQS = 16
LENGTH = 512
TOK_DEV = 256
CAP = 96


def draw_lengths(key, part):
    key = jax.random.fold_in(key, 11)
    full_key, other_key = jax.random.split(key)
    group_total = SEQS // SEQ_GRP
    chosen = jax.random.randint(full_key, (group_total, 1), 0, SEQ_GRP)
    others = jax.random.randint(other_key, (group_total, SEQ_GRP), LENGTH // 4, LENGTH + 1)
    member = jnp.arange(SEQ_GRP, dtype=jnp.int32)[None, :]
    return jnp.where(member == chosen, LENGTH, others).reshape(SEQS).astype(jnp.int32)


def draw_adapter_choice(key, part):
    key = jax.random.fold_in(key, 23)
    picked = jax.random.randint(key, (SEQS,), 0, SETS)
    return (picked[:, None] == jnp.arange(SETS, dtype=jnp.int32)[None, :]).astype(jnp.int32)


def steps_of(key, dims, shards, low, largest):
    factor_of = 1.0
    for dim, blocks in shards:
        steps = jax.random.uniform(jax.random.fold_in(jax.random.fold_in(key, 6), dim), (blocks,), jnp.float32, low / len(shards), largest / len(shards))
        factor_of = factor_of * jnp.repeat(jnp.exp(steps), dims[dim] // blocks).reshape((-1,) + (1,) * (len(dims) - 1 - dim))
    return factor_of


def shared_out(key, own, number, rows, amount, top, limit, skew):
    order = jax.random.permutation(key, amount)
    packed, common = portions_of(amount, rows * top, limit, skew, True), portions_of(amount, rows * top, limit, skew, False)
    places = jnp.arange(amount)

    def named(sizes, rotation):
        used = int((sizes > 0).sum())
        fixed = max(1, used // 4)
        passed = fixed + (places - fixed + rotation * (used - fixed)) % max(1, amount - fixed)
        return jnp.zeros((amount,), jnp.int32).at[order[jnp.where(places < fixed, places, passed)]].set(jnp.asarray(sizes, jnp.int32))

    sizes = jnp.where(number % 4 == 0, named(packed, number // 4), named(common, number - number // 4 - 1))
    mixed = jax.random.permutation(jax.random.fold_in(own, 3), amount)
    source_of, taker = mixed[0:amount // 2 * 2:2], mixed[1:amount // 2 * 2:2]
    room = jnp.minimum(sizes[source_of] - 1, limit - sizes[taker]) // 2
    room = jnp.where((source_of == order[0]) | (taker == order[0]) | (sizes[taker] == 0), 0, jnp.maximum(room, 0))
    passed = jax.random.randint(jax.random.fold_in(own, 4), (amount // 2,), 0, 1 << 20) % (room + 1)
    sizes = sizes.at[source_of].add(-passed).at[taker].add(passed)
    members = jnp.searchsorted(jnp.cumsum(sizes), jnp.arange(rows * top), side="right").astype(jnp.int32)
    grid = members.reshape(top, rows).T
    grid = grid[jax.random.permutation(jax.random.fold_in(own, 1), rows)]
    rotation = jax.random.randint(jax.random.fold_in(own, 2), (rows, 1), 0, top)
    return jnp.take_along_axis(grid, (jnp.arange(top)[None, :] + rotation) % top, axis=1)


def portions_of(count, total, reach, slope, full):
    weights = [(1 << 20) // math.isqrt(standing ** slope) + 1 for standing in range(1, count + 1)]
    largest = reach if full else min(reach, max(-(-total // count), total * weights[0] // sum(weights)))
    least = 1 if total - largest >= count - 1 else 0
    counts, spare = [largest] + [least] * (count - 1), total - largest - least * (count - 1)
    while spare > 0:
        movable = [i for i in range(1, count) if counts[i] < largest] or [i for i in range(1, count) if counts[i] < reach]
        pool, remaining = sum([weights[i] for i in movable]), spare
        for i in movable:
            extra = min(reach - counts[i], max(1, remaining * weights[i] // pool), spare)
            counts[i] = counts[i] + extra
            spare = spare - extra
    return np.array(counts)


def bell_draw(rng, shape, scale, reach, cuts=(), kind=jnp.bfloat16):
    array = jax.random.normal(rng, shape, jnp.float32) * scale
    if len(cuts) > 0:
        array = steps_of(rng, shape, cuts, -0.22, 0.18) * array
    return jnp.clip(array, min=-reach, max=reach).astype(kind)


def setup_inputs(seed: int = 0) -> dict:
    streams_of = jax.random.split(jax.random.key(seed), 22)
    tokens = bell_draw(streams_of[0], (SEQS, LENGTH, D), 1.0, 6.0, ((0, 8), (1, 4)))
    cotangent = bell_draw(streams_of[1], (SEQS, LENGTH, D), 1.0, 6.0, ((0, 8), (1, 4)))
    lengths = draw_lengths(jax.random.fold_in(streams_of[21], 71), 0)
    adapter_choice = draw_adapter_choice(jax.random.fold_in(streams_of[21], 71), 0)
    expert_ids_keys = jax.random.split(jax.random.fold_in(streams_of[4], 1), GROUPS * SPLITS * SEQ_GRP * SHARD // TOK_DEV)
    expert_ids_turns = jax.random.permutation(jax.random.fold_in(streams_of[4], 3), GROUPS * SPLITS * SEQ_GRP * SHARD // TOK_DEV)
    expert_ids = jax.vmap(lambda own, number: shared_out(jax.random.fold_in(streams_of[4], 2), own, number, TOK_DEV, EXPERTS, TOP, CAP, 1))(expert_ids_keys, expert_ids_turns).reshape((GROUPS, SPLITS, SEQ_GRP, SHARD, TOP))
    gate_weights = jnp.clip(0.0625 + 0.125 * jax.random.uniform(streams_of[5], (GROUPS, SPLITS, SEQ_GRP, SHARD, TOP), jnp.float32) ** steps_of(streams_of[5], (GROUPS, SPLITS, SEQ_GRP, SHARD, TOP), ((0, 8), (1, 4)), -0.2, 0.2), 0.0625, 0.1875)
    attn_gain = jnp.clip(1.0 + 0.1 * jax.random.normal(streams_of[6], (D,), jnp.float32), 0.5, 1.5)
    moe_gain = jnp.clip(1.0 + 0.1 * jax.random.normal(streams_of[7], (D,), jnp.float32), 0.5, 1.5)
    query_gain = jnp.clip(jax.random.uniform(streams_of[8], (HEAD,), jnp.float32, 1.0, 2.0), 1.0, 2.0)
    key_gain = jnp.clip(jax.random.uniform(streams_of[9], (HEAD,), jnp.float32, 1.0, 2.0), 1.0, 2.0)
    w_qkv = bell_draw(streams_of[10], (3, D, D), D ** -0.5, 0.125)
    w_out = bell_draw(streams_of[11], (D, D), (D // 16) ** -0.5, 0.5)
    expert_gate = bell_draw(streams_of[12], (EXPERTS, D, FF), D ** -0.5, 0.125, ((0, 8),))
    expert_up = bell_draw(streams_of[13], (EXPERTS, D, FF), D ** -0.5, 0.125, ((0, 8),))
    expert_down = bell_draw(streams_of[14], (EXPERTS, FF, D), (FF // 32) ** -0.5, 1.0, ((0, 8),))
    adapt_down = bell_draw(streams_of[15], (SETS, 4, D, RANK), D ** -0.5, 0.125, ((2, 8),), jnp.float32)
    first_down = bell_draw(streams_of[16], (SETS, 4, D, RANK), (6 * (SEQS * LENGTH // SETS) ** 0.5), 1024.0, ((2, 8),), jnp.float32)
    second_down = jnp.clip(jnp.exp(math.log(147456.0) - 1.3862944 * jax.random.uniform(streams_of[17], (SETS, 4, D, RANK), jnp.float32) ** steps_of(streams_of[17], (SETS, 4, D, RANK), ((2, 8),), -0.2, 0.2)), 36864.0, 147456.0)
    adapt_up = bell_draw(streams_of[18], (SETS, 4, RANK, D), RANK ** -0.5, 1.5, ((3, 8),), jnp.float32)
    first_up = bell_draw(streams_of[19], (SETS, 4, RANK, D), ((SEQS * LENGTH // SETS) ** 0.5), 192.0, ((3, 8),), jnp.float32)
    second_up = jnp.clip(jnp.exp(math.log(4096.0) - 1.3862944 * jax.random.uniform(streams_of[20], (SETS, 4, RANK, D), jnp.float32) ** steps_of(streams_of[20], (SETS, 4, RANK, D), ((3, 8),), -0.2, 0.2)), 1024.0, 4096.0)
    return dict(tokens=tokens, cotangent=cotangent, lengths=lengths, adapter_choice=adapter_choice, expert_ids=expert_ids, gate_weights=gate_weights, attn_gain=attn_gain, moe_gain=moe_gain, query_gain=query_gain, key_gain=key_gain, w_qkv=w_qkv, w_out=w_out, expert_gate=expert_gate, expert_up=expert_up, expert_down=expert_down, adapt_down=adapt_down, first_down=first_down, second_down=second_down, adapt_up=adapt_up, first_up=first_up, second_up=second_up)


NORM_EPS = 1e-05
ROPE_BASE = 50000.0
ADAPTER_SCALE = 0.5
BETA_FIRST = 0.5
BETA_SECOND = 0.5
RATE_DOWN = 0.02
RATE_UP = 0.2
WEIGHT_DECAY = 0.01
ADAM_EPS = 1e-08
MASKED = -1e+30
HIGHEST = lax.Precision.HIGHEST

@jax.custom_vjp
def low(v):
    return lax.optimization_barrier(v.astype(jnp.bfloat16)).astype(jnp.float32)

@jax.custom_vjp
def low_back(v):
    return v

def low_keep(v):
    return (low(v), None)

def low_pass(kept, grad):
    return (grad,)

def back_keep(v):
    return (v, None)

def back_low(kept, grad):
    return (low(grad),)
low.defvjp(low_keep, low_pass)
low_back.defvjp(back_keep, back_low)

def rms_norm(values, gain):
    return values * lax.rsqrt(lax.optimization_barrier(jnp.mean(values * values, axis=-1, keepdims=True)) + NORM_EPS) * gain

def rope_tables(positions):
    half_size = HEAD // 2
    frequency = ROPE_BASE ** (-(2.0 / HEAD) * jnp.arange(half_size, dtype=jnp.float32))
    angles = positions.astype(jnp.float32)[:, None] * frequency[None, :]
    return (jnp.cos(angles), jnp.sin(angles))

def rotate(values, cosine_table, sine_table):
    half_size = HEAD // 2
    front_half = values[..., :half_size]
    back_half = values[..., half_size:]
    cosine_wide = cosine_table[:, None, :]
    sine_wide = sine_table[:, None, :]
    return jnp.concatenate([front_half * cosine_wide - back_half * sine_wide, back_half * cosine_wide + front_half * sine_wide], axis=-1)

def silu_value(values):
    return values * jax.nn.sigmoid(values)

def attention_group(inputs, down_rows, up_rows, seq_lengths, weights):
    attn_gain, query_gain, key_gain, w_qkv, w_out = weights
    group_size = inputs.shape[0]
    normed = low(rms_norm(inputs, attn_gain))
    down_rows = low(down_rows)
    up_rows = low(up_rows)

    def project(source, which_proj, weight):
        base_term = jnp.einsum('gld,de->gle', source, weight, precision=HIGHEST)
        middle = low_back(low(jnp.einsum('gld,gdr->glr', source, down_rows[:, which_proj], precision=HIGHEST)))
        return base_term + ADAPTER_SCALE * jnp.einsum('glr,gre->gle', middle, up_rows[:, which_proj], precision=HIGHEST)

    def split_heads(values):
        return values.reshape(group_size, LENGTH, HEADS, HEAD)
    cosine_table, sine_table = rope_tables(jnp.arange(LENGTH, dtype=jnp.int32))
    queries = low(rotate(rms_norm(split_heads(low_back(project(normed, 0, w_qkv[0]))), query_gain), cosine_table, sine_table))
    key_rows = low(rotate(rms_norm(split_heads(low_back(project(normed, 1, w_qkv[1]))), key_gain), cosine_table, sine_table))
    value_rows = low(low_back(split_heads(project(normed, 2, w_qkv[2]))))
    live_keys = jnp.arange(LENGTH, dtype=jnp.int32)[None, :] < seq_lengths[:, None]
    block_rows = min(512, LENGTH)
    query_blocks = jnp.moveaxis(queries.reshape(group_size, LENGTH // block_rows, block_rows, HEADS, HEAD), 1, 0)

    def attend(query_block):
        raw_scores = low_back(jnp.einsum('gqhe,gkhe->ghqk', query_block, key_rows, precision=HIGHEST) * HEAD ** (-0.5))
        masked = jnp.where(live_keys[:, None, None, :], raw_scores, MASKED)
        exponent = jnp.exp(masked - lax.optimization_barrier(jnp.max(masked, axis=-1, keepdims=True)))
        soft_weights = exponent / lax.optimization_barrier(jnp.sum(exponent, axis=-1, keepdims=True))
        return jnp.einsum('ghqk,gkhe->gqhe', low(soft_weights), value_rows, precision=HIGHEST)
    attended = jnp.moveaxis(lax.map(jax.checkpoint(attend), query_blocks), 0, 1).reshape(group_size, LENGTH, D)
    attended = low_back(low(attended))
    return inputs + low_back(project(attended, 3, w_out))

def expert_block(normed_rows, chosen, block_gates, w_gate, w_up, w_down):
    flat_chosen = chosen.reshape(TOK_DEV * TOP)
    match_table = (flat_chosen[:, None] == jnp.arange(EXPERTS, dtype=jnp.int32)[None, :]).astype(jnp.int32)
    slot_rank = lax.optimization_barrier(jnp.sum((jnp.cumsum(match_table, axis=0) - match_table) * match_table, axis=1))
    slot_index = (flat_chosen * CAP + slot_rank).astype(jnp.int32)
    buffer = jnp.zeros((EXPERTS * CAP, D), jnp.float32).at[slot_index].set(jnp.repeat(normed_rows, TOP, axis=0))
    buffer = low_back(buffer).reshape(EXPERTS, CAP, D)
    gate_act = low_back(jnp.einsum('ecd,edf->ecf', buffer, w_gate, precision=HIGHEST))
    up_act = low_back(jnp.einsum('ecd,edf->ecf', buffer, w_up, precision=HIGHEST))
    hidden = low(silu_value(gate_act) * up_act)
    produced = low_back(low(jnp.einsum('ecf,efd->ecd', hidden, w_down, precision=HIGHEST)))
    returned = produced.reshape(EXPERTS * CAP, D)[slot_index].reshape(TOK_DEV, TOP, D)
    return lax.optimization_barrier(jnp.sum(block_gates[:, :, None] * returned, axis=1))

def layer_forward(inputs, adapt_down, adapt_up, lengths, choice_rows, expert_ids, gate_weights, weights, moe_gain, w_gate, w_up, w_down):
    down_sel = jnp.einsum('sk,kpdr->spdr', choice_rows, adapt_down, precision=HIGHEST)
    up_sel = jnp.einsum('sk,kprd->sprd', choice_rows, adapt_up, precision=HIGHEST)
    group_total = SEQS // SEQ_GRP

    def by_group(values):
        return values.reshape((group_total, SEQ_GRP) + values.shape[1:])

    def group_step(carry_in, pieces):
        return (carry_in, jax.checkpoint(attention_group)(pieces[0], pieces[1], pieces[2], pieces[3], weights))
    zero_carry = jnp.zeros((), jnp.float32)
    spare_carry, mixed = lax.scan(group_step, zero_carry, (by_group(inputs), by_group(down_sel), by_group(up_sel), by_group(lengths)))
    block_total = GROUPS * SPLITS
    blocked = jnp.transpose(mixed.reshape(GROUPS, SEQ_GRP, SPLITS, SHARD, D), (0, 2, 1, 3, 4)).reshape(block_total, TOK_DEV, D)
    moe_in = low(rms_norm(blocked, moe_gain))

    def moe_step(carry_in, pieces):
        return (carry_in, jax.checkpoint(expert_block)(pieces[0], pieces[1], pieces[2], w_gate, w_up, w_down))
    spare_moe, added = lax.scan(moe_step, zero_carry, (moe_in, expert_ids.reshape(block_total, TOK_DEV, TOP), gate_weights.reshape(block_total, TOK_DEV, TOP)))
    result = blocked + added
    return jnp.transpose(result.reshape(GROUPS, SPLITS, SEQ_GRP, SHARD, D), (0, 2, 1, 3, 4)).reshape(SEQS, LENGTH, D)

def adam_update(weight, gradient, first, second, step_rate):
    new_first = BETA_FIRST * first + (1.0 - BETA_FIRST) * gradient
    new_second = BETA_SECOND * second + (1.0 - BETA_SECOND) * gradient * gradient
    first_hat = new_first / (1.0 - BETA_FIRST ** STEP)
    second_hat = new_second / (1.0 - BETA_SECOND ** STEP)
    new_weight = weight - step_rate * (first_hat / (jnp.sqrt(second_hat) + ADAM_EPS) + WEIGHT_DECAY * weight)
    return (new_first, new_second, new_weight)

def reference(tokens, cotangent, lengths, adapter_choice, expert_ids, gate_weights, attn_gain, moe_gain, query_gain, key_gain, w_qkv, w_out, expert_gate, expert_up, expert_down, adapt_down, first_down, second_down, adapt_up, first_up, second_up):
    weights = (attn_gain, query_gain, key_gain, w_qkv.astype(jnp.float32), w_out.astype(jnp.float32))
    choice_rows = adapter_choice.astype(jnp.float32)
    w_gate = expert_gate.astype(jnp.float32)
    w_up = expert_up.astype(jnp.float32)
    w_down = expert_down.astype(jnp.float32)

    def forward(inputs, down_all, up_all):
        return layer_forward(inputs, down_all, up_all, lengths, choice_rows, expert_ids, gate_weights, weights, moe_gain, w_gate, w_up, w_down)
    output, pullback = jax.vjp(forward, tokens.astype(jnp.float32), adapt_down, adapt_up)
    live_mask = (jnp.arange(LENGTH, dtype=jnp.int32)[None, :] < lengths[:, None]).astype(jnp.float32)
    grad_input, grad_down, grad_up = pullback(cotangent.astype(jnp.float32) * live_mask[:, :, None])
    new_first_down, new_second_down, new_down = adam_update(adapt_down, grad_down, first_down, second_down, RATE_DOWN)
    new_first_up, new_second_up, new_up = adam_update(adapt_up, grad_up, first_up, second_up, RATE_UP)
    return (output.astype(jnp.bfloat16), grad_input, new_first_down, new_second_down, new_down, new_first_up, new_second_up, new_up)
```

```python
import functools

import jax
import jax.numpy as jnp
from jax import lax
from jax.experimental import pallas as pl
from jax.experimental.pallas import tpu as pltpu
from jax.sharding import PartitionSpec as P

HEAD = 128
STEP = 5

NORM_EPS = 1e-05
ROPE_BASE = 50000.0
ADAPTER_SCALE = 0.5
BETA_FIRST = 0.5
BETA_SECOND = 0.5
RATE_DOWN = 0.02
RATE_UP = 0.2
WEIGHT_DECAY = 0.01
ADAM_EPS = 1e-08
MASKED = -1e30
SCORE_SCALE = HEAD ** (-0.5)

F32 = jnp.float32
BF16 = jnp.bfloat16
VMEM_LIMIT = 60 * 1024 * 1024


def dot_nn(a, b):
    return lax.dot_general(a, b, (((1,), (0,)), ((), ())), preferred_element_type=F32)


def dot_nt(a, b):
    return lax.dot_general(a, b, (((1,), (1,)), ((), ())), preferred_element_type=F32)


def dot_tn(a, b):
    return lax.dot_general(a, b, (((0,), (0,)), ((), ())), preferred_element_type=F32)


def inverse_rms(values):
    return lax.rsqrt(jnp.mean(values * values, axis=-1, keepdims=True) + NORM_EPS)


def norm_back(values, gain, upstream):
    inverse = inverse_rms(values)
    scaled = upstream * gain
    return inverse * scaled - values * (inverse * inverse * inverse) * jnp.mean(
        values * scaled, axis=-1, keepdims=True
    )


def sigmoid(values):
    return 1.0 / (1.0 + jnp.exp(-values))


def adam_update(weight, gradient, first, second, step_rate):
    new_first = BETA_FIRST * first + (1.0 - BETA_FIRST) * gradient
    new_second = BETA_SECOND * second + (1.0 - BETA_SECOND) * gradient * gradient
    first_hat = new_first / (1.0 - BETA_FIRST**STEP)
    second_hat = new_second / (1.0 - BETA_SECOND**STEP)
    new_weight = weight - step_rate * (
        first_hat / (jnp.sqrt(second_hat) + ADAM_EPS) + WEIGHT_DECAY * weight
    )
    return (new_first, new_second, new_weight)


def shape_of(shape, dtype):
    return jax.ShapeDtypeStruct(shape, dtype)


def whole_block(shape):
    rank = len(shape)
    return pl.BlockSpec(tuple(shape), lambda *_: (0,) * rank)


def kernel_call(
    body, name, grid, in_specs, out_specs, out_shape, scratch=(), prefetch=0, flops=0, moved=0
):
    return pl.pallas_call(
        body,
        grid_spec=pltpu.PrefetchScalarGridSpec(
            num_scalar_prefetch=prefetch,
            grid=grid,
            in_specs=in_specs,
            out_specs=out_specs,
            scratch_shapes=list(scratch),
        ),
        out_shape=out_shape,
        name=name,
        cost_estimate=pl.CostEstimate(
            flops=int(flops), bytes_accessed=int(moved), transcendentals=0
        ),
        compiler_params=pltpu.CompilerParams(vmem_limit_bytes=VMEM_LIMIT),
    )


def swap(values, mask):
    count = lax.axis_size("exp")
    return lax.ppermute(values, "exp", [(i, i ^ mask) for i in range(count)])


def by_relative(stacked):
    count = lax.axis_size("exp")
    return jnp.take(stacked, lax.axis_index("exp") ^ jnp.arange(count), axis=0)


def gather_rows(rows):
    count = lax.axis_size("exp")
    if count != 8:
        everything = by_relative(lax.all_gather(rows, "exp"))
        return [(m, 0, everything[m]) for m in range(count)]
    half = rows.shape[0] // 2
    by_x = swap(rows, 2)
    by_y = swap(rows, 4)
    far_front = swap(by_x[:half], 4)
    far_back = swap(by_y[half:], 2)
    pieces = [(0, 0, rows), (2, 0, by_x), (4, 0, by_y), (6, 0, far_front), (6, half, far_back)]
    return pieces + [(m + 1, first, swap(array, 1)) for m, first, array in pieces]


def stack_pieces(pieces):
    count = lax.axis_size("exp")
    ordered = []
    for m in range(count):
        own = sorted(
            [(first, index) for index, (at, first, _) in enumerate(pieces) if at == m]
        )
        ordered.append(jnp.concatenate([pieces[index][2] for _, index in own], axis=0))
    return jnp.stack(ordered)


def add_low(a, b):
    return (a.astype(F32) + b.astype(F32)).astype(BF16)


def scatter_sum(parts):
    count = lax.axis_size("exp")
    if count != 8:
        sent = by_relative(jnp.stack(parts))
        came = lax.all_to_all(sent, "exp", 0, 0)
        return [(0, came[i]) for i in range(count)]
    half = parts[0].shape[0] // 2
    paired = {m: add_low(parts[m], swap(parts[m + 1], 1)) for m in (6, 4, 2)}
    beside = swap(parts[1], 1)
    far_front = swap(paired[6][:half], 2)
    far_back = swap(paired[6][half:], 4)
    x_front = swap(paired[2][:half], 2)
    y_back = swap(paired[4][half:], 4)
    y_front = swap(add_low(paired[4][:half], far_front), 4)
    x_back = swap(add_low(paired[2][half:], far_back), 2)
    return [
        (0, parts[0]),
        (0, beside),
        (0, x_front),
        (half, y_back),
        (0, y_front),
        (half, x_back),
    ]


def project_first(tokens, gain, w_qkv, groups, splits):
    rows, width = tokens.shape
    part = width // splits
    shard = rows // groups

    def body(tok_ref, gain_ref, w_ref, *outs):
        normed_ref = outs[groups]

        @pl.when((pl.program_id(0) == 0) & (pl.program_id(1) == 0))
        def _():
            values = tok_ref[...].astype(F32)
            normed_ref[...] = (values * inverse_rms(values) * gain_ref[...]).astype(BF16)

        result = dot_nn(normed_ref[...], w_ref[0])
        for g in range(groups):
            outs[g][0, 0] = result[g * shard : (g + 1) * shard].astype(BF16)

    return kernel_call(
        body,
        "project_first",
        (3, splits),
        [
            whole_block((rows, width)),
            whole_block((1, width)),
            pl.BlockSpec((1, width, part), lambda p, j: (p, 0, j)),
        ],
        [pl.BlockSpec((1, 1, shard, part), lambda p, j: (j, p, 0, 0))] * groups
        + [whole_block((rows, width))],
        [shape_of((splits, 3, shard, part), BF16)] * groups + [shape_of((rows, width), BF16)],
        flops=6 * rows * width * width,
        moved=6 * width * width,
    )(tokens, gain, w_qkv)


def pick_sets(stacked, picks, groups):
    count, kinds, _, projections, rank, part = stacked.shape

    def body(pick_ref, in_ref, out_ref):
        out_ref[0] = in_ref[0, :, 0]

    return kernel_call(
        body,
        "pick_sets",
        (groups, count),
        [
            pl.BlockSpec(
                (1, kinds, 1, projections, rank, part),
                lambda g, j, s: (j ^ s[groups], 0, s[g], 0, 0, 0),
            )
        ],
        pl.BlockSpec((1, kinds, projections, rank, part), lambda g, j, s: (g, 0, 0, 0, j)),
        shape_of((groups, kinds, projections, rank, count * part), BF16),
        prefetch=1,
        moved=8 * groups * count * projections * rank * part,
    )(picks, stacked)


def wide_mids(mids, which, rank):
    splits = mids.shape[0]
    return jnp.concatenate(
        [mids[z, which * rank : (which + 1) * rank, :] for z in range(splits)], axis=1
    )


def rotate(values, cosine, sine):
    return values * cosine + pltpu.roll(values, HEAD // 2, 1) * sine


def rotate_back(values, cosine, sine):
    return values * cosine - pltpu.roll(values, HEAD // 2, 1) * sine


def softmax_rows(queries, keys, length):
    total = keys.shape[0]
    scores = dot_nt(queries, keys) * SCORE_SCALE
    live = lax.broadcasted_iota(jnp.int32, (1, total), 1) < length
    scores = jnp.where(live, scores, MASKED)
    exponent = jnp.exp(scores - jnp.max(scores, axis=-1, keepdims=True))
    return exponent / jnp.sum(exponent, axis=-1, keepdims=True)


def attend(length, raw, mids, ups, query_gain, key_gain, cosine, sine):
    splits, _, shard, part = raw.shape
    rank = ups.shape[1]
    total = splits * shard
    heads = part // HEAD

    def body(
        len_ref, raw_ref, mid_ref, up_ref, qg_ref, kg_ref, cos_ref, sin_ref,
        att_ref, q_ref, k_ref, v_ref, rq_ref, rk_ref,
    ):
        mid = mid_ref[...]

        def full(which):
            base = raw_ref[:, which].reshape(total, HEAD).astype(F32)
            return base + ADAPTER_SCALE * dot_tn(wide_mids(mid, which, rank), up_ref[which])

        raw_q, raw_k, raw_v = full(0), full(1), full(2)
        rq_ref[0] = raw_q
        rk_ref[0] = raw_k
        cosine, sine = cos_ref[...], sin_ref[...]
        queries = rotate(raw_q * inverse_rms(raw_q) * qg_ref[...], cosine, sine).astype(BF16)
        keys = rotate(raw_k * inverse_rms(raw_k) * kg_ref[...], cosine, sine).astype(BF16)
        values = raw_v.astype(BF16)
        q_ref[0] = queries
        k_ref[0] = keys
        v_ref[0] = values
        weights = softmax_rows(queries, keys, len_ref[0]).astype(BF16)
        att_ref[...] = dot_nn(weights, values).astype(BF16).reshape(splits, shard, HEAD)

    head_block = pl.BlockSpec((1, total, HEAD), lambda h, s: (h, 0, 0))
    return kernel_call(
        body,
        "attend",
        (heads,),
        [
            pl.BlockSpec((splits, 3, shard, HEAD), lambda h, s: (0, 0, 0, h)),
            whole_block(mids.shape),
            pl.BlockSpec((3, rank, HEAD), lambda h, s: (0, 0, h)),
            whole_block((1, HEAD)),
            whole_block((1, HEAD)),
            whole_block((total, HEAD)),
            whole_block((total, HEAD)),
        ],
        [pl.BlockSpec((splits, shard, HEAD), lambda h, s: (0, 0, h))] + [head_block] * 5,
        [shape_of((splits, shard, part), BF16)]
        + [shape_of((heads, total, HEAD), BF16)] * 3
        + [shape_of((heads, total, HEAD), F32)] * 2,
        prefetch=1,
        flops=4 * heads * total * total * HEAD,
        moved=heads * total * HEAD * 24 + 4 * heads * total * total,
    )(length, raw, mids, ups, query_gain, key_gain, cosine, sine)


def attend_back(length, grads, q, k, v, raw_q, raw_k, query_gain, key_gain, cosine, sine):
    splits, shard, part = grads.shape
    total = splits * shard
    heads = part // HEAD

    def body(
        len_ref, grad_ref, q_ref, k_ref, v_ref, rq_ref, rk_ref, qg_ref, kg_ref, cos_ref, sin_ref,
        out_ref,
    ):
        queries, keys, values = q_ref[0], k_ref[0], v_ref[0]
        grad = grad_ref[...].reshape(total, HEAD)
        weights = softmax_rows(queries, keys, len_ref[0])
        grad_probs = dot_nt(grad, values)
        inner = jnp.sum(weights * grad_probs, axis=-1, keepdims=True)
        grad_scores = (weights * (grad_probs - inner)).astype(BF16)
        grad_q = dot_nn(grad_scores, keys) * SCORE_SCALE
        grad_k = dot_tn(grad_scores, queries) * SCORE_SCALE
        grad_v = dot_tn(weights.astype(BF16), grad)
        cosine, sine = cos_ref[...], sin_ref[...]
        grad_q = norm_back(rq_ref[0], qg_ref[...], rotate_back(grad_q, cosine, sine))
        grad_k = norm_back(rk_ref[0], kg_ref[...], rotate_back(grad_k, cosine, sine))
        for which, value in enumerate((grad_q, grad_k, grad_v)):
            out_ref[:, which] = value.astype(BF16).reshape(splits, shard, HEAD)

    head_block = pl.BlockSpec((1, total, HEAD), lambda h, s: (h, 0, 0))
    return kernel_call(
        body,
        "attend_back",
        (heads,),
        [pl.BlockSpec((splits, shard, HEAD), lambda h, s: (0, 0, h))]
        + [head_block] * 5
        + [
            whole_block((1, HEAD)),
            whole_block((1, HEAD)),
            whole_block((total, HEAD)),
            whole_block((total, HEAD)),
        ],
        pl.BlockSpec((splits, 3, shard, HEAD), lambda h, s: (0, 0, 0, h)),
        shape_of((splits, 3, shard, part), BF16),
        prefetch=1,
        flops=10 * heads * total * total * HEAD,
        moved=heads * total * HEAD * 24 + 8 * heads * total * total,
    )(length, grads, q, k, v, raw_q, raw_k, query_gain, key_gain, cosine, sine)


def project_out(attended, w_out, down, up, tokens, gain):
    splits, shard, part = attended.shape
    width = splits * part
    rank = down.shape[0]
    block = min(512, width)
    steps = width // block

    def body(att_ref, w_ref, down_ref, up_ref, tok_ref, gain_ref, mixed_ref, moe_ref, mid_ref, att):
        step = pl.program_id(0)

        @pl.when(step == 0)
        def _():
            for z in range(splits):
                att[:, z * part : (z + 1) * part] = att_ref[z]
            mid_ref[...] = dot_nt(down_ref[...], att[...]).astype(BF16)

        columns = pl.ds(pl.multiple_of(step * block, block), block)
        mixed_ref[:, columns] = (
            tok_ref[:, columns].astype(F32)
            + dot_nn(att[...], w_ref[...])
            + ADAPTER_SCALE * dot_tn(mid_ref[...], up_ref[:, columns])
        )

        @pl.when(step == steps - 1)
        def _():
            values = mixed_ref[...]
            moe_ref[...] = (values * inverse_rms(values) * gain_ref[...]).astype(BF16)

    return kernel_call(
        body,
        "project_out",
        (steps,),
        [
            whole_block(attended.shape),
            pl.BlockSpec((width, block), lambda i: (0, i)),
            whole_block((rank, width)),
            whole_block((rank, width)),
            whole_block((shard, width)),
            whole_block((1, width)),
        ],
        [whole_block((shard, width)), whole_block((shard, width)), whole_block((rank, shard))],
        [
            shape_of((shard, width), F32),
            shape_of((shard, width), BF16),
            shape_of((rank, shard), BF16),
        ],
        scratch=[pltpu.VMEM((shard, width), BF16)],
        flops=2 * shard * width * width,
        moved=2 * width * width,
    )(attended, w_out, down, up, tokens, gain)


def one_hot(slot_row, capacity):
    tokens = slot_row.shape[1]
    index = lax.broadcasted_iota(jnp.int32, (capacity, tokens), 0).astype(F32)
    return index == slot_row


def load_pieces(pieces, refs, target, sem, shard):
    copies = []
    for index, (ref, (g, m, first, count)) in enumerate(zip(refs, pieces)):
        copies.append(
            pltpu.make_async_copy(
                ref, target.at[m, pl.ds(g * shard + first, count)], sem.at[index]
            )
        )
    for copy in copies:
        copy.start()
    for copy in copies:
        copy.wait()


def piece_list(gathered):
    places, arrays = [], []
    for g, pieces in enumerate(gathered):
        for m, first, array in pieces:
            places.append((g, m, first, array.shape[0]))
            arrays.append(array)
    return places, arrays


def expert_grad_hidden(gathered, meta, expert_down, capacity):
    places, arrays = piece_list(gathered)
    shard = sum(place[3] for place in places if place[:2] == (0, 0))
    experts, hidden, width = expert_down.shape
    count = meta.shape[0]
    tokens = meta.shape[-1]
    rows = count * capacity

    def body(meta_ref, w_ref, *rest):
        refs, (out_ref, held, picked, sem) = rest[: len(arrays)], rest[len(arrays) :]
        expert = pl.program_id(0)

        @pl.when(expert == 0)
        def _():
            load_pieces(places, refs, held, sem, shard)

        for m in range(count):
            named = one_hot(meta_ref[m, 0, pl.ds(expert, 1)], capacity)
            weight = jnp.sum(
                jnp.where(named, meta_ref[m, 1, pl.ds(expert, 1)], 0.0), axis=1, keepdims=True
            )
            picked[m * capacity : (m + 1) * capacity] = (
                weight * dot_nn(named.astype(BF16), held[m])
            ).astype(BF16)
        out_ref[0] = dot_nt(picked[...], w_ref[0]).astype(BF16)

    return kernel_call(
        body,
        "expert_grad_hidden",
        (experts,),
        [
            whole_block(meta.shape),
            pl.BlockSpec((1, hidden, width), lambda e: (e, 0, 0)),
        ]
        + [pl.BlockSpec(memory_space=pl.ANY)] * len(arrays),
        pl.BlockSpec((1, rows, hidden), lambda e: (e, 0, 0)),
        shape_of((experts, rows, hidden), BF16),
        scratch=[
            pltpu.VMEM((count, tokens, width), BF16),
            pltpu.VMEM((rows, width), BF16),
            pltpu.SemaphoreType.DMA((len(arrays),)),
        ],
        flops=2 * experts * rows * (hidden + tokens) * width,
        moved=2 * experts * hidden * width + 2 * count * tokens * width,
    )(meta, expert_down, *arrays)


def expert_middle(gathered, meta, expert_gate, expert_up, grad_hidden, capacity):
    places, arrays = piece_list(gathered)
    shard = sum(place[3] for place in places if place[:2] == (0, 0))
    experts, width, hidden = expert_gate.shape
    count = meta.shape[0]
    tokens = meta.shape[-1]
    rows = count * capacity
    block = min(512, hidden)
    steps = hidden // block
    chunk = 256 if rows % 256 == 0 else rows

    def body(meta_ref, gate_ref, up_ref, gh_ref, *rest):
        refs, (h_ref, gx_ref, held, picked, total, sem) = rest[: len(arrays)], rest[len(arrays) :]
        expert, step = pl.program_id(0), pl.program_id(1)

        @pl.when((expert == 0) & (step == 0))
        def _():
            load_pieces(places, refs, held, sem, shard)

        @pl.when(step == 0)
        def _():
            for m in range(count):
                named = one_hot(meta_ref[m, 0, pl.ds(expert, 1)], capacity)
                picked[m * capacity : (m + 1) * capacity] = dot_nn(
                    named.astype(BF16), held[m]
                ).astype(BF16)

        for c in range(rows // chunk):
            at = slice(c * chunk, (c + 1) * chunk)
            x = picked[at]
            gate = dot_nn(x, gate_ref[0])
            up = dot_nn(x, up_ref[0])
            sigma = sigmoid(gate)
            value = gate * sigma
            grad = gh_ref[0, at].astype(F32)
            h_ref[0, at] = (value * up).astype(BF16)
            grad_gate = (grad * up * (sigma * (1.0 + gate * (1.0 - sigma)))).astype(BF16)
            grad_up = (grad * value).astype(BF16)
            grad_x = dot_nt(grad_gate, gate_ref[0]) + dot_nt(grad_up, up_ref[0])

            @pl.when(step == 0)
            def _():
                total[at] = grad_x

            @pl.when((step > 0) & (step < steps - 1))
            def _():
                total[at] += grad_x

            @pl.when(step == steps - 1)
            def _():
                gx_ref[0, at] = (total[at] + grad_x).astype(BF16)

    return kernel_call(
        body,
        "expert_middle",
        (experts, steps),
        [
            whole_block(meta.shape),
            pl.BlockSpec((1, width, block), lambda e, f: (e, 0, f)),
            pl.BlockSpec((1, width, block), lambda e, f: (e, 0, f)),
            pl.BlockSpec((1, rows, block), lambda e, f: (e, 0, f)),
        ]
        + [pl.BlockSpec(memory_space=pl.ANY)] * len(arrays),
        [
            pl.BlockSpec((1, rows, block), lambda e, f: (e, 0, f)),
            pl.BlockSpec((1, rows, width), lambda e, f: (e, 0, 0)),
        ],
        [shape_of((experts, rows, hidden), BF16), shape_of((experts, rows, width), BF16)],
        scratch=[
            pltpu.VMEM((count, tokens, width), BF16),
            pltpu.VMEM((rows, width), BF16),
            pltpu.VMEM((rows, width), F32),
            pltpu.SemaphoreType.DMA((len(arrays),)),
        ],
        flops=2 * experts * rows * (4 * hidden + tokens) * width,
        moved=4 * experts * hidden * width + 4 * experts * rows * width,
    )(meta, expert_gate, expert_up, grad_hidden, *arrays)


def expert_produce(hidden_rows, meta, expert_down, capacity):
    experts, hidden, width = expert_down.shape
    count = meta.shape[0]
    rows = count * capacity

    def body(meta_ref, h_ref, w_ref, out_ref):
        expert = pl.program_id(0)
        result = dot_nn(h_ref[0], w_ref[0])
        for m in range(count):
            named = one_hot(meta_ref[m, 0, pl.ds(expert, 1)], capacity)
            weight = jnp.sum(
                jnp.where(named, meta_ref[m, 1, pl.ds(expert, 1)], 0.0), axis=1, keepdims=True
            )
            at = slice(m * capacity, (m + 1) * capacity)
            out_ref[0, at] = (weight * result[at]).astype(BF16)

    return kernel_call(
        body,
        "expert_produce",
        (experts,),
        [
            whole_block(meta.shape),
            pl.BlockSpec((1, rows, hidden), lambda e: (e, 0, 0)),
            pl.BlockSpec((1, hidden, width), lambda e: (e, 0, 0)),
        ],
        pl.BlockSpec((1, rows, width), lambda e: (e, 0, 0)),
        shape_of((experts, rows, width), BF16),
        flops=2 * experts * rows * hidden * width,
        moved=2 * experts * hidden * width + 2 * experts * rows * width,
    )(meta, hidden_rows, expert_down)


def combine(slot_rows, meta, members, capacity, groups):
    experts, rows, width = slot_rows.shape
    tokens = meta.shape[-1]
    shard = tokens // groups
    block = min(512, width)
    size = len(members)
    start = members[0]
    depth = experts * capacity

    def body(meta_ref, in_ref, *rest):
        outs, named = rest[:-1], rest[-1]

        @pl.when(pl.program_id(0) == 0)
        def _():
            for i, m in enumerate(members):
                for e in range(experts):
                    named[i, e * capacity : (e + 1) * capacity] = one_hot(
                        meta_ref[m, 0, e : e + 1], capacity
                    ).astype(BF16)

        for i in range(size):
            held = in_ref[:, i * capacity : (i + 1) * capacity].reshape(depth, block)
            result = dot_tn(named[i], held).astype(BF16)
            for g in range(groups):
                outs[i * groups + g][...] = result[g * shard : (g + 1) * shard]

    result = kernel_call(
        body,
        "combine",
        (width // block,),
        [
            whole_block(meta.shape),
            pl.BlockSpec((experts, size * capacity, block), lambda c: (0, start // size, c)),
        ],
        [pl.BlockSpec((shard, block), lambda c: (0, c))] * (size * groups),
        [shape_of((shard, width), BF16)] * (size * groups),
        scratch=[pltpu.VMEM((size, depth, tokens), BF16)],
        flops=2 * size * depth * tokens * width,
        moved=2 * size * (depth + tokens) * width,
    )(meta, slot_rows)
    return [result[i * groups : (i + 1) * groups] for i in range(size)]


def combine_all(slot_rows, meta, capacity, groups):
    count = meta.shape[0]
    parts = {}
    for start in reversed(range(0, count, 2)):
        for m, part in zip(
            (start, start + 1), combine(slot_rows, meta, (start, start + 1), capacity, groups)
        ):
            parts[m] = part
    return [[parts[m][g] for m in range(count)] for g in range(groups)]


def project_out_back(pieces, mixed, upstream, gain, w_out, down, up, attended, mid):
    splits, shard, part = attended.shape
    width = splits * part
    rank = down.shape[0]
    places = [(first, array.shape[0]) for first, array in pieces]

    def body(mixed_ref, up_stream_ref, gain_ref, w_ref, down_ref, up_ref, att_ref, mid_ref, *rest):
        refs = rest[: len(places)]
        gm_ref, out_ref, gdown_ref, gup_ref, low, small = rest[len(places) :]
        step = pl.program_id(0)

        @pl.when(step == 0)
        def _():
            gm_ref[...] = jnp.zeros((shard, width), F32)
            for ref, (first, count) in zip(refs, places):
                gm_ref[first : first + count] += ref[...].astype(F32)
            grad = up_stream_ref[...].astype(F32) + norm_back(
                mixed_ref[...], gain_ref[...], gm_ref[...]
            )
            gm_ref[...] = grad
            low[...] = grad.astype(BF16)
            small[...] = (ADAPTER_SCALE * dot_nt(up_ref[...], low[...])).astype(BF16)
            gup_ref[...] = (ADAPTER_SCALE * dot_nn(mid_ref[...], low[...])).astype(BF16)

        columns = pl.ds(pl.multiple_of(step * part, part), part)
        out_ref[0] = (
            dot_nt(low[...], w_ref[...]) + dot_tn(small[...], down_ref[:, columns])
        ).astype(BF16)
        gdown_ref[...] = dot_nn(small[...], att_ref[0]).astype(BF16)

    return kernel_call(
        body,
        "project_out_back",
        (splits,),
        [
            whole_block((shard, width)),
            whole_block((shard, width)),
            whole_block((1, width)),
            pl.BlockSpec((part, width), lambda j: (j, 0)),
            whole_block((rank, width)),
            whole_block((rank, width)),
            pl.BlockSpec((1, shard, part), lambda j: (j, 0, 0)),
            whole_block((rank, shard)),
        ]
        + [whole_block((count, width)) for _, count in places],
        [
            whole_block((shard, width)),
            pl.BlockSpec((1, shard, part), lambda j: (j, 0, 0)),
            pl.BlockSpec((rank, part), lambda j: (0, j)),
            whole_block((rank, width)),
        ],
        [
            shape_of((shard, width), F32),
            shape_of((splits, shard, part), BF16),
            shape_of((rank, width), BF16),
            shape_of((rank, width), BF16),
        ],
        scratch=[pltpu.VMEM((shard, width), BF16), pltpu.VMEM((rank, shard), BF16)],
        flops=2 * shard * width * width,
        moved=2 * width * width,
    )(mixed, upstream, gain, w_out, down, up, attended, mid, *[array for _, array in pieces])


def adapter_grads(grads, normed, mids, downs_ups):
    groups = len(grads)
    splits, _, shard, part = grads[0].shape
    width = splits * part
    rank = downs_ups.shape[3]

    def body(normed_ref, mid_ref, up_ref, *rest):
        refs = rest[:groups]
        small_ref, gdown_ref, gup_ref, low = rest[groups:]
        for g in range(groups):
            for z in range(splits):
                low[:, z * part : (z + 1) * part] = refs[g][z, 0]
            small = (ADAPTER_SCALE * dot_nt(up_ref[g, 0, 0], low[...])).astype(BF16)
            small_ref[g, 0] = small
            gdown_ref[g, 0] = dot_nn(small, normed_ref[g * shard : (g + 1) * shard]).astype(BF16)
            gup_ref[g, 0] = (ADAPTER_SCALE * dot_nn(mid_ref[g, 0], low[...])).astype(BF16)

    wide = pl.BlockSpec((groups, 1, rank, width), lambda p: (0, p, 0, 0))
    return kernel_call(
        body,
        "adapter_grads",
        (3,),
        [
            whole_block(normed.shape),
            pl.BlockSpec((groups, 1, rank, shard), lambda p: (0, p, 0, 0)),
            pl.BlockSpec((groups, 1, 1, rank, width), lambda p: (0, 1, p, 0, 0)),
        ]
        + [pl.BlockSpec((splits, 1, shard, part), lambda p: (0, p, 0, 0))] * groups,
        [pl.BlockSpec((groups, 1, rank, shard), lambda p: (0, p, 0, 0)), wide, wide],
        [
            shape_of((groups, 3, rank, shard), BF16),
            shape_of((groups, 3, rank, width), BF16),
            shape_of((groups, 3, rank, width), BF16),
        ],
        scratch=[pltpu.VMEM((shard, width), BF16)],
        flops=18 * groups * shard * rank * width,
        moved=6 * groups * shard * width,
    )(normed, mids, downs_ups, *grads)


def project_first_back(grads, smalls, downs_ups, w_qkv, tokens, gain, grad_mixed):
    groups = len(grads)
    splits, _, shard, part = grads[0].shape
    width = splits * part
    rank = downs_ups.shape[3]
    rows = groups * shard
    block = min(512, width)
    steps = width // block

    def body(small_ref, down_ref, w_ref, tok_ref, gain_ref, *rest):
        mixed_refs, refs = rest[:groups], rest[groups : 2 * groups]
        out_ref, low, total = rest[2 * groups :]
        which, step = pl.program_id(0), pl.program_id(1)

        @pl.when(step == 0)
        def _():
            for g in range(groups):
                for z in range(splits):
                    low[g * shard : (g + 1) * shard, z * part : (z + 1) * part] = refs[g][z, 0]

        columns = pl.ds(pl.multiple_of(step * block, block), block)
        result = dot_nt(low[...], w_ref[0])
        small = jnp.concatenate(
            [dot_tn(small_ref[g, 0], down_ref[g, 0, 0]) for g in range(groups)], axis=0
        )

        @pl.when(which == 0)
        def _():
            total[:, columns] = result + small

        @pl.when(which > 0)
        def _():
            total[:, columns] += result + small

        @pl.when((which == 2) & (step == steps - 1))
        def _():
            back = norm_back(tok_ref[...].astype(F32), gain_ref[...], total[...])
            for g in range(groups):
                out_ref[g] = mixed_refs[g][...] + back[g * shard : (g + 1) * shard]

    return kernel_call(
        body,
        "project_first_back",
        (3, steps),
        [
            pl.BlockSpec((groups, 1, rank, shard), lambda p, i: (0, p, 0, 0)),
            pl.BlockSpec((groups, 1, 1, rank, block), lambda p, i: (0, 0, p, 0, i)),
            pl.BlockSpec((1, block, width), lambda p, i: (p, i, 0)),
            whole_block((rows, width)),
            whole_block((1, width)),
        ]
        + [whole_block((shard, width))] * groups
        + [pl.BlockSpec((splits, 1, shard, part), lambda p, i: (0, p, 0, 0))] * groups,
        whole_block((groups, shard, width)),
        shape_of((groups, shard, width), F32),
        scratch=[pltpu.VMEM((rows, width), BF16), pltpu.VMEM((rows, width), F32)],
        flops=6 * rows * width * width,
        moved=6 * width * width,
    )(smalls, downs_ups, w_qkv, tokens, gain, *grad_mixed, *grads)


def local(
    tokens,
    cotangent,
    lengths,
    adapter_choice,
    expert_ids,
    gate_weights,
    attn_gain,
    moe_gain,
    query_gain,
    key_gain,
    w_qkv,
    w_out,
    expert_gate,
    expert_up,
    expert_down,
    adapt_down,
    first_down,
    second_down,
    adapt_up,
    first_up,
    second_up,
):
    groups, shard, width = tokens.shape
    splits = lax.axis_size("seq")
    devices = lax.axis_size("exp")
    here = lax.axis_index("seq")
    total = shard * splits
    part = width // splits
    rows = groups * shard
    sets, projections, slice_width, rank = adapt_down.shape
    local_experts = expert_gate.shape[0]
    experts = local_experts * devices
    top = expert_ids.shape[-1]
    capacity = 3 * rows * top // (2 * experts)

    flat_tokens = tokens.reshape(rows, width)
    gain_row = attn_gain.reshape(1, width)
    moe_row = moe_gain.reshape(1, width)
    query_row = query_gain.reshape(1, HEAD)
    key_row = key_gain.reshape(1, HEAD)

    positions = here * shard + jnp.arange(shard, dtype=jnp.int32)
    own_live = positions[None, :] < lengths[:, None]
    upstream = jnp.where(own_live[:, :, None], cotangent, jnp.zeros((), BF16))

    frequency = ROPE_BASE ** (-(2.0 / HEAD) * jnp.arange(HEAD // 2, dtype=F32))
    angles = jnp.arange(total, dtype=F32)[:, None] * frequency[None, :]
    cosine, sine = jnp.cos(angles), jnp.sin(angles)
    cosine = jnp.concatenate([cosine, cosine], axis=1)
    sine = jnp.concatenate([-sine, sine], axis=1)

    first = project_first(flat_tokens, gain_row, w_qkv, groups, splits)
    normed = first[groups]
    raw = [lax.all_to_all(first[g], "seq", 0, 0) for g in range(groups)]

    packed = jnp.stack([jnp.swapaxes(adapt_down.astype(BF16), 2, 3), adapt_up.astype(BF16)])
    stacked = stack_pieces(gather_rows(packed.reshape(-1, slice_width)))
    stacked = stacked.reshape(devices, 2, sets, projections, rank, slice_width)
    chosen = jnp.sum(adapter_choice * jnp.arange(sets, dtype=jnp.int32)[None, :], axis=1)
    picks = jnp.concatenate([chosen, lax.axis_index("exp").reshape(1)]).astype(jnp.int32)
    factors = pick_sets(stacked, picks, groups)
    mids = jnp.einsum(
        "gsd,gprd->gprs",
        normed.reshape(groups, shard, width),
        factors[:, 0, :3],
        preferred_element_type=F32,
    ).astype(BF16)
    all_mids = lax.all_gather(mids.reshape(groups, 3 * rank, shard), "seq")
    own_ups = lax.dynamic_slice_in_dim(factors[:, 1, :3], here * part, part, axis=3)

    ids = expert_ids.reshape(rows, top)
    gates = gate_weights.reshape(rows, top)
    named = ids.T[:, None, :] == jnp.arange(experts, dtype=jnp.int32)[None, :, None]
    gate_table = jnp.sum(jnp.where(named, gates.T[:, None, :], 0.0), axis=0)
    mask = jnp.any(named, axis=0)
    earlier = jnp.arange(rows)[:, None] < jnp.arange(rows)[None, :]
    ranks = jnp.dot(mask.astype(BF16), earlier.astype(BF16), preferred_element_type=F32)
    slots = jnp.where(mask, ranks, -1.0)
    meta = jnp.stack([slots, gate_table]).reshape(2, devices, local_experts, rows)
    meta = by_relative(lax.all_to_all(jnp.swapaxes(meta, 0, 1), "exp", 0, 0))

    cot_rows = [gather_rows(upstream[g]) for g in range(groups)]
    grad_hidden = expert_grad_hidden(cot_rows, meta, expert_down, capacity)

    saved, attended, mixed, mid_out, moe_rows = [], [], [], [], []
    for g in range(groups):
        att, *kept = attend(
            lengths[g : g + 1],
            raw[g],
            all_mids[:, g],
            own_ups[g],
            query_row,
            key_row,
            cosine,
            sine,
        )
        saved.append(kept)
        attended.append(lax.all_to_all(att, "seq", 0, 0))
        out_mixed, moe_in, mid = project_out(
            attended[g], w_out, factors[g, 0, 3], factors[g, 1, 3], tokens[g], moe_row
        )
        mixed.append(out_mixed)
        mid_out.append(mid)
        moe_rows.append(gather_rows(moe_in))

    hidden, grad_slots = expert_middle(
        moe_rows, meta, expert_gate, expert_up, grad_hidden, capacity
    )
    grad_parts = combine_all(grad_slots, meta, capacity, groups)
    grad_pieces = [scatter_sum(grad_parts[g]) for g in range(groups)]

    produced = expert_produce(hidden, meta, expert_down, capacity)
    out_parts = combine_all(produced, meta, capacity, groups)
    out_pieces = [scatter_sum(out_parts[g]) for g in range(groups)]

    grad_mixed, grad_raw, out_grads = [], [], []
    for g in range(groups):
        gm, grad_att, gdown, gup = project_out_back(
            grad_pieces[g],
            mixed[g],
            upstream[g],
            moe_row,
            w_out,
            factors[g, 0, 3],
            factors[g, 1, 3],
            attended[g],
            mid_out[g],
        )
        grad_mixed.append(gm)
        out_grads.append(jnp.stack([gdown, gup]))
        grad_att = lax.all_to_all(grad_att, "seq", 0, 0)
        back = attend_back(
            lengths[g : g + 1], grad_att, *saved[g], query_row, key_row, cosine, sine
        )
        grad_raw.append(lax.all_to_all(back, "seq", 0, 0))

    outputs = []
    for g in range(groups):
        sums = [mixed[g]]
        for first_row, array in out_pieces[g]:
            after = shard - first_row - array.shape[0]
            sums.append(jnp.pad(array.astype(F32), ((first_row, after), (0, 0))))
        outputs.append(functools.reduce(jnp.add, sums).astype(BF16))
    output = jnp.stack(outputs)

    smalls, grad_down, grad_up = adapter_grads(grad_raw, normed, mids, factors)
    grad_input = project_first_back(
        grad_raw, smalls, factors, w_qkv, flat_tokens, gain_row, grad_mixed
    )

    per_first = jnp.stack([grad_down, grad_up], axis=1)
    per_all = jnp.concatenate([per_first, jnp.stack(out_grads)[:, :, None]], axis=2)
    per_all = per_all.reshape(groups, 2, 4, rank, devices, slice_width)
    came = lax.all_to_all(jnp.moveaxis(per_all, 4, 0), "exp", 0, 0)
    choices = lax.all_gather(adapter_choice.astype(BF16), "exp")
    in_sets = jnp.einsum(
        "dgk,dgcprw->kcprw", choices, came, preferred_element_type=F32
    ).astype(BF16)
    pieces = in_sets.reshape(splits, -1, slice_width)
    pieces = lax.all_to_all(pieces, "seq", 0, 0)
    summed = jnp.sum(pieces.astype(F32), axis=0).astype(BF16)
    summed = lax.all_gather(summed, "seq", axis=0, tiled=True)
    summed = summed.reshape(sets, 2, 4, rank, slice_width).astype(F32)
    shard_down = jnp.swapaxes(summed[:, 0], 2, 3)
    shard_up = summed[:, 1]
    new_first_down, new_second_down, new_down = adam_update(
        adapt_down, shard_down, first_down, second_down, RATE_DOWN
    )
    new_first_up, new_second_up, new_up = adam_update(
        adapt_up, shard_up, first_up, second_up, RATE_UP
    )
    return (
        output,
        grad_input,
        new_first_down,
        new_second_down,
        new_down,
        new_first_up,
        new_second_up,
        new_up,
    )


def solution(mesh):
    in_specs = (
        P("exp", "seq", None),
        P("exp", "seq", None),
        P("exp"),
        P("exp", None),
        P("exp", "seq", None, None, None),
        P("exp", "seq", None, None, None),
        P(),
        P(),
        P(),
        P(),
        P(),
        P(),
        P("exp", None, None),
        P("exp", None, None),
        P("exp", None, None),
        P(None, None, "exp", None),
        P(None, None, "exp", None),
        P(None, None, "exp", None),
        P(None, None, None, "exp"),
        P(None, None, None, "exp"),
        P(None, None, None, "exp"),
    )
    out_specs = (
        P("exp", "seq", None),
        P("exp", "seq", None),
        P(None, None, "exp", None),
        P(None, None, "exp", None),
        P(None, None, "exp", None),
        P(None, None, None, "exp"),
        P(None, None, None, "exp"),
        P(None, None, None, "exp"),
    )
    return jax.shard_map(local, mesh=mesh, in_specs=in_specs, out_specs=out_specs, check_vma=False)
```

```python
import functools

import jax
import jax.numpy as jnp
from jax import lax
from jax.experimental import pallas as pl
from jax.experimental.pallas import tpu as pltpu
from jax.sharding import PartitionSpec as P

HEAD = 128
STEP = 5

NORM_EPS = 1e-05
ROPE_BASE = 50000.0
ADAPTER_SCALE = 0.5
BETA_FIRST = 0.5
BETA_SECOND = 0.5
RATE_DOWN = 0.02
RATE_UP = 0.2
WEIGHT_DECAY = 0.01
ADAM_EPS = 1e-08
MASKED = -1e30
SCORE_SCALE = HEAD ** (-0.5)

F32 = jnp.float32
BF16 = jnp.bfloat16
VMEM_LIMIT = 62 * 1024 * 1024
COST_SHARE = 0.01


def dot_nn(a, b):
    return lax.dot_general(a, b, (((1,), (0,)), ((), ())), preferred_element_type=F32)


def dot_nt(a, b):
    return lax.dot_general(a, b, (((1,), (1,)), ((), ())), preferred_element_type=F32)


def dot_tn(a, b):
    return lax.dot_general(a, b, (((0,), (0,)), ((), ())), preferred_element_type=F32)


def inverse_rms(values):
    return lax.rsqrt(jnp.mean(values * values, axis=-1, keepdims=True) + NORM_EPS)


def norm_back(values, gain, upstream):
    inverse = inverse_rms(values)
    scaled = upstream * gain
    return inverse * scaled - values * (inverse * inverse * inverse) * jnp.mean(
        values * scaled, axis=-1, keepdims=True
    )


def sigmoid(values):
    return 0.5 + 0.5 * jnp.tanh(0.5 * values)


def adam_update(weight, gradient, first, second, step_rate):
    new_first = BETA_FIRST * first + (1.0 - BETA_FIRST) * gradient
    new_second = BETA_SECOND * second + (1.0 - BETA_SECOND) * gradient * gradient
    first_hat = new_first / (1.0 - BETA_FIRST**STEP)
    second_hat = new_second / (1.0 - BETA_SECOND**STEP)
    new_weight = weight - step_rate * (
        first_hat / (jnp.sqrt(second_hat) + ADAM_EPS) + WEIGHT_DECAY * weight
    )
    return (new_first, new_second, new_weight)


def shape_of(shape, dtype):
    return jax.ShapeDtypeStruct(shape, dtype)


def whole_block(shape):
    rank = len(shape)
    return pl.BlockSpec(tuple(shape), lambda *_: (0,) * rank)


def kernel_call(
    body, name, grid, in_specs, out_specs, out_shape, scratch=(), prefetch=0, flops=0, moved=0,
    aliases=None,
):
    return pl.pallas_call(
        body,
        grid_spec=pltpu.PrefetchScalarGridSpec(
            num_scalar_prefetch=prefetch,
            grid=grid,
            in_specs=in_specs,
            out_specs=out_specs,
            scratch_shapes=list(scratch),
        ),
        out_shape=out_shape,
        input_output_aliases=aliases or {},
        name=name,
        cost_estimate=pl.CostEstimate(
            flops=int(flops * COST_SHARE), bytes_accessed=int(moved * COST_SHARE), transcendentals=0
        ),
        compiler_params=pltpu.CompilerParams(vmem_limit_bytes=VMEM_LIMIT),
    )


def swap(values, mask):
    count = lax.axis_size("exp")
    return lax.ppermute(values, "exp", [(i, i ^ mask) for i in range(count)])


def shift(values, distance):
    count = lax.axis_size("seq")
    return lax.ppermute(values, "seq", [(i, (i + distance) % count) for i in range(count)])


def shift_order():
    count = lax.axis_size("seq")
    return sorted(range(1, count), key=lambda r: -min(r, count - r))


def forward_seq(pieces):
    if not isinstance(pieces, (list, tuple)):
        return lax.all_to_all(pieces, "seq", 0, 0)
    came = {r: shift(pieces[r], r) for r in shift_order()}
    return [pieces[0]] + [came[r] for r in range(1, len(pieces))]


def backward_seq(pieces):
    if not isinstance(pieces, (list, tuple)):
        return lax.all_to_all(pieces, "seq", 0, 0)
    came = {r: shift(pieces[r], -r) for r in shift_order()}
    return [pieces[0]] + [came[r] for r in range(1, len(pieces))]


def tell_all(values, axis):
    count = lax.axis_size(axis)
    return lax.all_to_all(jnp.broadcast_to(values[None], (count,) + values.shape), axis, 0, 0)


def by_distance(stacked):
    count = lax.axis_size("seq")
    order = (lax.axis_index("seq") - jnp.arange(count)) % count
    return jnp.take(stacked, order, axis=0)


def by_relative(stacked):
    count = lax.axis_size("exp")
    return jnp.take(stacked, lax.axis_index("exp") ^ jnp.arange(count), axis=0)


WAYS = ((2, 4), (4, 2))


def gather_rows(rows, before_far, before_last):
    count = lax.axis_size("exp")
    if count != 8:
        everything = by_relative(lax.all_gather(rows, "exp"))
        return [[everything[m]] for m in range(count)]
    half = rows.shape[0] // 2
    by_x = swap(rows, 2)
    by_y = swap(rows, 4)
    far = lax.optimization_barrier(((by_x[:half], by_y[half:]), before_far))[0]
    far = [swap(far[0], 4), swap(far[1], 2)]
    found = [[rows], [swap(rows, 1)], [by_x], [swap(by_x, 1)], [by_y], [swap(by_y, 1)], far]
    return found + [[swap(block, 1) for block in after(far, before_last)]]


def add_low(*values):
    return functools.reduce(jnp.add, [value.astype(F32) for value in values]).astype(BF16)


def after(values, *first):
    return lax.optimization_barrier((values, first))[0]


ANYWHERE = pl.BlockSpec(memory_space=pl.ANY)


def group_block(shape, group):
    rank = len(shape) - 1
    return pl.BlockSpec((None,) + tuple(shape[1:]), lambda *_: (group,) + (0,) * rank)


def is_list(pieces):
    return isinstance(pieces, (list, tuple))


def piece_shape(pieces):
    if is_list(pieces):
        return len(pieces), pieces[0].shape
    return pieces.shape[0], pieces.shape[1:]


def piece_arrays(pieces, splits):
    return list(pieces) if is_list(pieces) else [pieces] * splits


def piece_specs(pieces, block, index):
    if is_list(pieces):
        return [pl.BlockSpec(block, index)] * len(pieces)
    return [
        pl.BlockSpec((None,) + tuple(block), lambda *at, r=r: (r,) + tuple(index(*at)))
        for r in range(pieces.shape[0])
    ]


def out_specs_of(listed, splits, block, index):
    if listed:
        return [pl.BlockSpec(block, index)] * splits
    return [pl.BlockSpec((splits,) + tuple(block), lambda *at: (0,) + tuple(index(*at)))]


def out_shapes_of(listed, splits, shape, dtype):
    if listed:
        return [shape_of(shape, dtype)] * splits
    return [shape_of((splits,) + tuple(shape), dtype)]


def out_refs_of(listed, refs):
    return list(refs) if listed else [refs[0].at[r] for r in range(refs[0].shape[0])]


def out_pieces_of(listed, results):
    return list(results) if listed else results[0]


def project_first(place, tokens, gain, w_qkv, groups, splits, listed):
    rows, width = tokens.shape
    part = width // splits
    shard = rows // groups
    counts = [splits if listed[g] else 1 for g in range(groups)]
    total = sum(counts)

    def body(place_ref, tok_ref, gain_ref, w_ref, *rest):
        outs = rest[:total]
        parts_ref, normed_ref, held, sem = rest[total:]
        which = pl.program_id(0)

        def owner(r):
            return lax.rem(place_ref[0] + r, splits)

        def copy(p, r):
            columns = pl.ds(pl.multiple_of(owner(r) * part, part), part)
            return pltpu.make_async_copy(
                w_ref.at[p, :, columns],
                held.at[p, :, pl.ds(r * part, part)],
                sem.at[p, r],
            )

        @pl.when(which == 0)
        def _():
            for p in range(3):
                for r in range(splits):
                    copy(p, r).start()
            values = tok_ref[...].astype(F32)
            low = (values * inverse_rms(values) * gain_ref[...]).astype(BF16)
            normed_ref[...] = low
            for z in range(splits):
                for g in range(groups):
                    parts_ref[z, g] = low[
                        g * shard : (g + 1) * shard, z * part : (z + 1) * part
                    ]

        for r in range(splits):
            copy(which, r).wait()
            result = dot_nn(normed_ref[...], held[which, :, r * part : (r + 1) * part])
            first = 0
            for g in range(groups):
                low = result[g * shard : (g + 1) * shard].astype(BF16)
                if listed[g]:
                    outs[first + r][0] = low
                else:
                    outs[first][owner(r), 0] = low
                first += counts[g]

    specs, shapes = [], []
    for g in range(groups):
        specs += out_specs_of(listed[g], splits, (1, shard, part), lambda p, s: (p, 0, 0))
        shapes += out_shapes_of(listed[g], splits, (3, shard, part), BF16)
    result = kernel_call(
        body,
        "project_first",
        (3,),
        [whole_block((rows, width)), whole_block((1, width)), ANYWHERE],
        specs + [whole_block((splits, groups, shard, part)), whole_block((rows, width))],
        shapes
        + [shape_of((splits, groups, shard, part), BF16), shape_of((rows, width), BF16)],
        scratch=[
            pltpu.VMEM((3, width, width), BF16),
            pltpu.SemaphoreType.DMA((3, splits)),
        ],
        prefetch=1,
        flops=6 * rows * width * width,
        moved=6 * width * width,
    )(place, tokens, gain, w_qkv)
    outs, first = [], 0
    for g in range(groups):
        outs.append(out_pieces_of(listed[g], result[first : first + counts[g]]))
        first += counts[g]
    return outs, result[total], result[total + 1]


def pick_sets(gathered, picks, groups, sets, sections, normed=None):
    count, _, part = gathered.shape
    width = count * part
    shard = normed.shape[0] // groups if normed is not None else 0
    number = len(sections)

    def body(pick_ref, in_ref, *rest):
        normed_ref = rest[0] if shard else None
        outs = rest[1:] if shard else rest
        outs, sem = outs[:-1], outs[-1]
        copies = []
        for g in range(groups):
            for i, (first, own) in enumerate(sections):
                for e in range(count):
                    copies.append(
                        pltpu.make_async_copy(
                            in_ref.at[e, pl.ds(pl.multiple_of(first + pick_ref[g] * own, own), own)],
                            outs[i].at[g, :, pl.ds(e * part, part)],
                            sem.at[(g * number + i) * count + e],
                        )
                    )
        for copy in copies:
            copy.start()
        for copy in copies:
            copy.wait()
        if shard:
            for g in range(groups):
                outs[number][g] = dot_nt(
                    outs[0][g], normed_ref[g * shard : (g + 1) * shard]
                ).astype(BF16)

    shapes = [(groups, own, width) for _, own in sections]
    if shard:
        shapes.append((groups, sections[0][1], shard))
    return kernel_call(
        body,
        "pick_sets",
        (1,),
        [ANYWHERE] + ([whole_block(normed.shape)] if shard else []),
        [whole_block(shape) for shape in shapes],
        [shape_of(shape, BF16) for shape in shapes],
        scratch=[pltpu.SemaphoreType.DMA((groups * number * count,))],
        prefetch=1,
        moved=4 * groups * width * sum(own for _, own in sections),
    )(picks, gathered, *([normed] if shard else []))


def route(ids, gates, choice, devices, local_experts):
    top, tokens = ids.shape
    experts = devices * local_experts

    def body(ids_ref, gates_ref, choice_ref, out_ref):
        expert = lax.broadcasted_iota(jnp.int32, (experts, tokens), 0)
        weights = jnp.zeros((experts, tokens), F32)
        named = jnp.zeros((experts, tokens), F32)
        for k in range(top):
            hit = expert == ids_ref[k : k + 1]
            weights = jnp.where(hit, gates_ref[k : k + 1], weights)
            named = jnp.where(hit, 1.0, named)
        earlier = lax.broadcasted_iota(jnp.int32, (tokens, tokens), 0) < lax.broadcasted_iota(
            jnp.int32, (tokens, tokens), 1
        )
        ranks = dot_nn(named.astype(BF16), jnp.where(earlier, 1.0, 0.0).astype(BF16))
        slots = jnp.where(named > 0.0, ranks, -1.0)
        for d in range(devices):
            out_ref[d, 0] = slots[d * local_experts : (d + 1) * local_experts]
            out_ref[d, 1] = weights[d * local_experts : (d + 1) * local_experts]
            out_ref[d, 2] = jnp.broadcast_to(choice_ref[...], (local_experts, tokens))

    shape = (devices, 3, local_experts, tokens)
    return kernel_call(
        body,
        "route",
        (1,),
        [whole_block(ids.shape), whole_block(gates.shape), whole_block(choice.shape)],
        whole_block(shape),
        shape_of(shape, F32),
        moved=12 * experts * tokens,
    )(ids, gates, choice)


def rotate(values, cosine, sine):
    return values * cosine + pltpu.roll(values, HEAD // 2, 1) * sine


def rotate_back(values, cosine, sine):
    return values * cosine - pltpu.roll(values, HEAD // 2, 1) * sine


def softmax_rows(queries, keys, live):
    scores = jnp.where(live, dot_nt(queries, keys) * SCORE_SCALE, MASKED)
    exponent = jnp.exp(scores - jnp.max(scores, axis=-1, keepdims=True))
    return exponent * (1.0 / jnp.sum(exponent, axis=-1, keepdims=True))


def attend(length, raw, mids, ups, query_gain, key_gain, positions, cosine, sine):
    listed = is_list(raw)
    splits, (_, shard, part) = piece_shape(raw)
    rank = ups.shape[1]
    total = splits * shard
    heads = part // HEAD

    def body(len_ref, up_ref, qg_ref, kg_ref, pos_ref, cos_ref, sin_ref, *rest):
        raw_refs, mid_ref = rest[:splits], rest[splits]
        att_refs = out_refs_of(listed, rest[splits + 1 : -5])
        q_ref, k_ref, v_ref, rq_ref, rk_ref = rest[-5:]

        def full(which):
            base = jnp.concatenate([ref[which] for ref in raw_refs], axis=0).astype(F32)
            mid = jnp.concatenate(
                [mid_ref[r, which * rank : (which + 1) * rank] for r in range(splits)], axis=1
            )
            return base + ADAPTER_SCALE * dot_tn(mid, up_ref[which])

        raw_q, raw_k, raw_v = full(0), full(1), full(2)
        rq_ref[0] = raw_q
        rk_ref[0] = raw_k
        cosine, sine = cos_ref[...], sin_ref[...]
        queries = rotate(raw_q * inverse_rms(raw_q) * qg_ref[...], cosine, sine).astype(BF16)
        keys = rotate(raw_k * inverse_rms(raw_k) * kg_ref[...], cosine, sine).astype(BF16)
        values = raw_v.astype(BF16)
        q_ref[0] = queries
        k_ref[0] = keys
        v_ref[0] = values
        weights = softmax_rows(queries, keys, pos_ref[...] < len_ref[0]).astype(BF16)
        result = dot_nn(weights, values).astype(BF16)
        for r in range(splits):
            att_refs[r][...] = result[r * shard : (r + 1) * shard]

    head_block = pl.BlockSpec((1, total, HEAD), lambda h, s: (h, 0, 0))
    result = kernel_call(
        body,
        "attend",
        (heads,),
        [
            pl.BlockSpec((3, rank, HEAD), lambda h, s: (0, 0, h)),
            whole_block((1, HEAD)),
            whole_block((1, HEAD)),
            whole_block((1, total)),
            whole_block((total, HEAD)),
            whole_block((total, HEAD)),
        ]
        + piece_specs(raw, (3, shard, HEAD), lambda h, s: (0, 0, h))
        + [whole_block(mids.shape)],
        out_specs_of(listed, splits, (shard, HEAD), lambda h, s: (0, h)) + [head_block] * 5,
        out_shapes_of(listed, splits, (shard, part), BF16)
        + [shape_of((heads, total, HEAD), BF16)] * 3
        + [shape_of((heads, total, HEAD), F32)] * 2,
        prefetch=1,
        flops=4 * heads * total * total * HEAD,
        moved=heads * total * HEAD * 24 + 4 * heads * total * total,
    )(length, ups, query_gain, key_gain, positions, cosine, sine, *piece_arrays(raw, splits), mids)
    return out_pieces_of(listed, result[:-5]), result[-5:]


def attend_back(length, grads, group, saved, mids, rank, query_gain, key_gain, positions, cosine, sine):
    listed = False
    splits, _, shard, part = grads.shape
    total = splits * shard
    heads = part // HEAD

    def body(len_ref, qg_ref, kg_ref, pos_ref, cos_ref, sin_ref, *rest):
        grad_refs, mid_ref = rest[:splits], rest[splits]
        q_ref, k_ref, v_ref, rq_ref, rk_ref = rest[splits + 1 : splits + 6]
        out_refs = out_refs_of(listed, rest[splits + 6 : -1])
        gup_ref = rest[-1]
        queries, keys, values = q_ref[0], k_ref[0], v_ref[0]
        grad = jnp.concatenate([ref[...] for ref in grad_refs], axis=0)
        weights = softmax_rows(queries, keys, pos_ref[...] < len_ref[0])
        grad_probs = dot_nt(grad, values)
        inner = jnp.sum(weights * grad_probs, axis=-1, keepdims=True)
        grad_scores = (weights * (grad_probs - inner)).astype(BF16)
        grad_q = dot_nn(grad_scores, keys) * SCORE_SCALE
        grad_k = dot_tn(grad_scores, queries) * SCORE_SCALE
        grad_v = dot_tn(weights.astype(BF16), grad)
        cosine, sine = cos_ref[...], sin_ref[...]
        grad_q = norm_back(rq_ref[0], qg_ref[...], rotate_back(grad_q, cosine, sine))
        grad_k = norm_back(rk_ref[0], kg_ref[...], rotate_back(grad_k, cosine, sine))

        for which, value in enumerate((grad_q, grad_k, grad_v)):
            low = value.astype(BF16)
            for r in range(splits):
                out_refs[r][which] = low[r * shard : (r + 1) * shard]
            mid = jnp.concatenate(
                [mid_ref[r, which * rank : (which + 1) * rank] for r in range(splits)], axis=1
            )
            gup_ref[which * rank : (which + 1) * rank] = (
                ADAPTER_SCALE * dot_nn(mid, low)
            ).astype(BF16)

    head_block = pl.BlockSpec((1, total, HEAD), lambda h, s: (h, 0, 0))
    result = kernel_call(
        body,
        "attend_back",
        (heads,),
        [
            whole_block((1, HEAD)),
            whole_block((1, HEAD)),
            whole_block((1, total)),
            whole_block((total, HEAD)),
            whole_block((total, HEAD)),
        ]
        + [
            pl.BlockSpec((None, None, shard, HEAD), lambda h, s, r=r: (r, group, 0, h))
            for r in range(splits)
        ]
        + [whole_block(mids.shape)]
        + [head_block] * 5,
        out_specs_of(listed, splits, (3, shard, HEAD), lambda h, s: (0, 0, h))
        + [pl.BlockSpec((3 * rank, HEAD), lambda h, s: (0, h))],
        out_shapes_of(listed, splits, (3, shard, part), BF16)
        + [shape_of((3 * rank, part), BF16)],
        prefetch=1,
        flops=10 * heads * total * total * HEAD,
        moved=heads * total * HEAD * 24 + 8 * heads * total * total,
    )(length, query_gain, key_gain, positions, cosine, sine, *[grads] * splits, mids, *saved)
    return out_pieces_of(listed, result[:-1]), result[-1]


def project_out(attended, w_out, down, up, tokens, gain):
    splits, groups, shard, part = attended.shape
    width = splits * part
    rank = down.shape[1]
    rows = groups * shard

    def body(att_ref, w_ref, down_ref, up_ref, tok_ref, gain_ref, *rest):
        mixed_ref, moe_ref, mid_ref, att, held, sem = rest
        copies = [
            pltpu.make_async_copy(
                w_ref.at[pl.ds(i * part, part)], held.at[pl.ds(i * part, part)], sem.at[i]
            )
            for i in range(splits)
        ]
        for copy in copies:
            copy.start()
        adapter = []
        for g in range(groups):
            at = slice(g * shard, (g + 1) * shard)
            for z in range(splits):
                att[at, z * part : (z + 1) * part] = att_ref[z, g]
            mid = dot_nt(down_ref[g], att[at]).astype(BF16)
            mid_ref[g] = mid
            adapter.append(
                tok_ref[g].astype(F32) + ADAPTER_SCALE * dot_tn(mid, up_ref[g])
            )
        total = jnp.concatenate(adapter, axis=0)
        for i, copy in enumerate(copies):
            copy.wait()
            total += dot_nn(att[:, i * part : (i + 1) * part], held[i * part : (i + 1) * part])
        moe_ref[...] = (total * inverse_rms(total) * gain_ref[...]).astype(BF16)
        for g in range(groups):
            mixed_ref[g] = total[g * shard : (g + 1) * shard]

    return kernel_call(
        body,
        "project_out",
        (1,),
        [
            whole_block(attended.shape),
            ANYWHERE,
            whole_block(down.shape),
            whole_block(up.shape),
            whole_block(tokens.shape),
            whole_block((1, width)),
        ],
        [
            whole_block((groups, shard, width)),
            whole_block((rows, width)),
            whole_block((groups, rank, shard)),
        ],
        [
            shape_of((groups, shard, width), F32),
            shape_of((rows, width), BF16),
            shape_of((groups, rank, shard), BF16),
        ],
        scratch=[
            pltpu.VMEM((rows, width), BF16),
            pltpu.VMEM((width, width), BF16),
            pltpu.SemaphoreType.DMA((splits,)),
        ],
        flops=2 * rows * width * width,
        moved=2 * width * width,
    )(attended, w_out, down, up, tokens, gain)


def one_hot(slot_row, capacity):
    tokens = slot_row.shape[1]
    index = lax.broadcasted_iota(jnp.int32, (capacity, tokens), 0).astype(F32)
    return index == slot_row


def pick_rows(sources, meta_ref, ring, sem, picked, capacity, weigh, begin=0):
    count = meta_ref.shape[0]
    experts = picked.shape[0]
    slots = ring.shape[0]

    def copies(m):
        found = sources(m)
        size = ring.shape[1] // len(found)
        return [
            pltpu.make_async_copy(
                ref, ring.at[m % slots, pl.ds(i * size, size)], sem.at[m, i]
            )
            for i, ref in enumerate(found)
        ]

    for m in range(slots):
        for copy in copies(m):
            copy.start()
    for m in range(count):
        named = jnp.concatenate(
            [one_hot(meta_ref[m, 0, e : e + 1], capacity) for e in range(begin, begin + experts)], axis=0
        )
        for copy in copies(m):
            copy.wait()
        result = dot_nn(named.astype(BF16), ring[m % slots])
        if weigh:
            weights = jnp.concatenate(
                [
                    jnp.broadcast_to(meta_ref[m, 1, e : e + 1], (capacity, named.shape[1]))
                    for e in range(begin, begin + experts)
                ],
                axis=0,
            )
            result = result * jnp.sum(jnp.where(named, weights, 0.0), axis=1, keepdims=True)
        low = result.astype(BF16)
        for e in range(experts):
            picked[e, m * capacity : (m + 1) * capacity] = low[e * capacity : (e + 1) * capacity]
        if m + slots < count:
            for copy in copies(m + slots):
                copy.start()


def expert_grad_hidden(place, gathered, meta, expert_down, capacity, begin, end):
    _, hidden, width = expert_down.shape
    experts = end - begin
    count = meta.shape[0]
    tokens = meta.shape[-1]
    rows = count * capacity

    def body(place_ref, meta_ref, w_ref, rows_ref, *rest):
        out_ref, ring, picked, sem = rest[-4:]
        expert = pl.program_id(0)

        @pl.when(expert == 0)
        def _():
            pick_rows(
                lambda m: [rows_ref.at[place_ref[1] ^ m]],
                meta_ref, ring, sem, picked, capacity, True, begin,
            )

        out_ref[0] = dot_nt(picked[expert], w_ref[0]).astype(BF16)

    return kernel_call(
        body,
        "expert_grad_hidden",
        (experts,),
        [
            whole_block(meta.shape),
            pl.BlockSpec((1, hidden, width), lambda e, s: (e + begin, 0, 0)),
            ANYWHERE,
        ],
        pl.BlockSpec((1, rows, hidden), lambda e, s: (e, 0, 0)),
        shape_of((experts, rows, hidden), BF16),
        scratch=[
            pltpu.VMEM((4, tokens, width), BF16),
            pltpu.VMEM((experts, rows, width), BF16),
            pltpu.SemaphoreType.DMA((count, 1)),
        ],
        prefetch=1,
        flops=2 * experts * rows * (hidden + tokens) * width,
        moved=2 * experts * hidden * width + 2 * count * tokens * width,
    )(place, meta, expert_down, gathered)


def combine_rows(meta_ref, picked, m, capacity):
    experts, _, width = picked.shape
    named = jnp.concatenate(
        [one_hot(meta_ref[m, 0, e : e + 1], capacity) for e in range(experts)], axis=0
    )
    named = jnp.where(named, 1.0, 0.0).T.astype(BF16)
    held = jnp.concatenate(
        [picked[e, m * capacity : (m + 1) * capacity] for e in range(experts)], axis=0
    )
    return dot_nn(named, held)


def send_combined(meta_ref, picked, ring, sem, capacity, targets):
    count = meta_ref.shape[0]
    tokens = ring.shape[1]
    slots = ring.shape[0]
    waiting = {}
    for i, m in enumerate(reversed(range(count))):
        for copy in waiting.pop(i - slots, []):
            copy.wait()
        ring[i % slots] = combine_rows(meta_ref, picked, m, capacity).astype(BF16)
        found = targets(m)
        size = tokens // len(found)
        waiting[i] = [
            pltpu.make_async_copy(
                ring.at[i % slots, pl.ds(b * size, size)], ref, sem.at[i % slots, b]
            )
            for b, ref in enumerate(found)
        ]
        for copy in waiting[i]:
            copy.start()
    for copies in waiting.values():
        for copy in copies:
            copy.wait()


def expert_middle(gathered, meta, expert_gate, expert_up, grad_hiddens, capacity):
    experts, width, hidden = expert_gate.shape
    count = meta.shape[0]
    tokens = meta.shape[-1]
    rows = count * capacity
    chunk = 256 if rows % 256 == 0 else rows
    numbers = [len(found) for found in gathered]
    arrays = [array for found in gathered for array in found]

    half = grad_hiddens[0].shape[0]

    def body(meta_ref, gate_ref, up_ref, front_ref, back_ref, *rest):
        refs, (h_ref, gx_ref, ring, picked, sem) = rest[: len(arrays)], rest[len(arrays) :]
        expert = pl.program_id(0)

        @pl.when(expert == 0)
        def _():
            pick_rows(
                lambda m: refs[sum(numbers[:m]) : sum(numbers[: m + 1])],
                meta_ref, ring, sem, picked, capacity, False,
            )

        for c in range(rows // chunk):
            at = slice(c * chunk, (c + 1) * chunk)
            x = picked[expert, at]
            gate = dot_nn(x, gate_ref[0])
            up = dot_nn(x, up_ref[0])
            sigma = sigmoid(gate)
            value = gate * sigma
            grad = jnp.where(expert < half, front_ref[0, at], back_ref[0, at]).astype(F32)
            h_ref[0, at] = (value * up).astype(BF16)
            grad_gate = (grad * up * (sigma + value * (1.0 - sigma))).astype(BF16)
            grad_up = (grad * value).astype(BF16)
            gx_ref[0, at] = (
                dot_nt(grad_gate, gate_ref[0]) + dot_nt(grad_up, up_ref[0])
            ).astype(BF16)

    return kernel_call(
        body,
        "expert_middle",
        (experts,),
        [
            whole_block(meta.shape),
            pl.BlockSpec((1, width, hidden), lambda e: (e, 0, 0)),
            pl.BlockSpec((1, width, hidden), lambda e: (e, 0, 0)),
            pl.BlockSpec((1, rows, hidden), lambda e: (jnp.minimum(e, half - 1), 0, 0)),
            pl.BlockSpec((1, rows, hidden), lambda e: (jnp.maximum(e - half, 0), 0, 0)),
        ]
        + [ANYWHERE] * len(arrays),
        [
            pl.BlockSpec((1, rows, hidden), lambda e: (e, 0, 0)),
            pl.BlockSpec((1, rows, width), lambda e: (e, 0, 0)),
        ],
        [shape_of((experts, rows, hidden), BF16), shape_of((experts, rows, width), BF16)],
        scratch=[
            pltpu.VMEM((2, tokens, width), BF16),
            pltpu.VMEM((experts, rows, width), BF16),
            pltpu.SemaphoreType.DMA((count, max(numbers))),
        ],
        flops=2 * experts * rows * (4 * hidden + tokens) * width,
        moved=4 * experts * hidden * width + 4 * experts * rows * width,
    )(meta, expert_gate, expert_up, *grad_hiddens, *arrays)


def combine(place, slot_rows, meta, capacity, groups, paired):
    experts, _, width = slot_rows.shape
    count = meta.shape[0]
    tokens = meta.shape[-1]
    depth = experts * capacity
    last = count - 1
    even = [m for m in range(count) if m % 2 == 0]

    def body(place_ref, meta_ref, in_ref, *rest):
        outs, (ring, sem) = rest[:-2], rest[-2:]
        step = pl.program_id(0)

        def copies(i):
            m = last - i
            if not paired:
                targets = [outs[0].at[place_ref[1] ^ m]]
            elif m % 2:
                targets = [outs[-1].at[m // 2]]
            else:
                targets = outs[m // 2 * groups : (m // 2 + 1) * groups]
            size = tokens // len(targets)
            return [
                pltpu.make_async_copy(
                    ring.at[i % 2, pl.ds(b * size, size)], ref, sem.at[i % 2, b]
                )
                for b, ref in enumerate(targets)
            ]

        for i in range(2, count):

            @pl.when(step == i)
            def _():
                for copy in copies(i - 2):
                    copy.wait()

        named = jnp.concatenate(
            [one_hot(meta_ref[0, 0, e : e + 1], capacity) for e in range(experts)], axis=0
        )
        named = jnp.where(named, 1.0, 0.0).T.astype(BF16)
        ring[lax.rem(step, 2)] = dot_nn(named, in_ref[...].reshape(depth, width)).astype(BF16)
        for i in range(count):

            @pl.when(step == i)
            def _():
                for copy in copies(i):
                    copy.start()

        @pl.when(step == count - 1)
        def _():
            for i in range(count - 2, count):
                for copy in copies(i):
                    copy.wait()

    if paired:
        shapes = [shape_of((tokens // groups, width), BF16)] * (len(even) * groups)
        shapes.append(shape_of((count // 2, tokens, width), BF16))
    else:
        shapes = [shape_of((count, tokens, width), BF16)]
    result = kernel_call(
        body,
        "combine",
        (count,),
        [
            pl.BlockSpec((1,) + meta.shape[1:], lambda i, s: (last - i, 0, 0, 0)),
            pl.BlockSpec((experts, capacity, width), lambda i, s: (0, last - i, 0)),
        ],
        [ANYWHERE] * len(shapes),
        shapes,
        scratch=[
            pltpu.VMEM((2, tokens, width), BF16),
            pltpu.SemaphoreType.DMA((2, groups)),
        ],
        prefetch=1,
        flops=2 * count * depth * tokens * width,
        moved=2 * count * (depth + tokens) * width,
    )(place, meta, slot_rows)
    if not paired:
        return result[0], None
    return {m: result[i * groups : (i + 1) * groups] for i, m in enumerate(even)}, result[-1]


def expert_produce(place, hidden_rows, meta, expert_down, capacity, first, last, before=None):
    experts, hidden, width = expert_down.shape
    count = meta.shape[0]
    tokens = meta.shape[-1]
    rows = count * capacity
    held = before.shape[0] if before is not None else 0

    def body(place_ref, meta_ref, h_ref, w_ref, *rest):
        expert = pl.program_id(0) + first
        result = dot_nn(h_ref[0], w_ref[0])
        if held:
            before_ref, out_ref, ring, made, sem, before_sem = rest
            copy = pltpu.make_async_copy(before_ref, made.at[pl.ds(0, held)], before_sem)

            @pl.when(expert == first)
            def _():
                copy.start()

        else:
            (out_ref,) = rest
        for m in range(count):
            named = one_hot(meta_ref[m, 0, pl.ds(expert, 1)], capacity)
            weight = jnp.sum(
                jnp.where(named, meta_ref[m, 1, pl.ds(expert, 1)], 0.0), axis=1, keepdims=True
            )
            at = slice(m * capacity, (m + 1) * capacity)
            value = (weight * result[at]).astype(BF16)
            if held:
                made[expert, at] = value
            else:
                out_ref[0, at] = value

        if held:

            @pl.when(expert == last - 1)
            def _():
                copy.wait()
                send_combined(
                    meta_ref, made, ring, sem, capacity, lambda m: [out_ref.at[place_ref[1] ^ m]]
                )

    out_spec, shape = ANYWHERE, shape_of((count, tokens, width), BF16)
    if not held:
        out_spec = pl.BlockSpec((1, rows, width), lambda e, s: (e, 0, 0))
        shape = shape_of((last - first, rows, width), BF16)
    return kernel_call(
        body,
        "expert_produce",
        (last - first,),
        [
            whole_block(meta.shape),
            pl.BlockSpec((1, rows, hidden), lambda e, s: (e + first, 0, 0)),
            pl.BlockSpec((1, hidden, width), lambda e, s: (e + first, 0, 0)),
        ]
        + ([ANYWHERE] if held else []),
        out_spec,
        shape,
        scratch=[
            pltpu.VMEM((2, tokens, width), BF16),
            pltpu.VMEM((experts, rows, width), BF16),
            pltpu.SemaphoreType.DMA((2, 1)),
            pltpu.SemaphoreType.DMA,
        ]
        if held
        else [],
        prefetch=1,
        flops=2 * (last - first) * rows * hidden * width,
        moved=2 * experts * hidden * width + 2 * experts * rows * width,
    )(place, meta, hidden_rows, expert_down, *([before] if held else []))


def project_out_back(pieces, mixed, upstream, gain, w_out, down, up, attended, mids):
    splits, groups, shard, part = attended.shape
    width = splits * part
    rank = down.shape[1]
    rows = groups * shard
    number = len(pieces[0])

    def body(up_stream_ref, gain_ref, w_ref, down_ref, up_ref, mixed_ref, att_ref, mid_ref, *rest):
        refs, rest = rest[: groups * number], rest[groups * number :]
        gm_ref, gdown_ref, gup_ref, out_ref, low, held, sem = rest
        copies = [
            pltpu.make_async_copy(w_ref.at[pl.ds(z * part, part)], held.at[z], sem.at[z])
            for z in range(splits)
        ]
        for copy in copies:
            copy.start()
        smalls = []
        for g in range(groups):
            total = refs[g * number][...].astype(F32)
            for ref in refs[g * number + 1 : (g + 1) * number]:
                total += ref[...].astype(F32)
            grad = up_stream_ref[g].astype(F32) + norm_back(mixed_ref[g], gain_ref[...], total)
            gm_ref[g] = grad
            grad = grad.astype(BF16)
            low[g * shard : (g + 1) * shard] = grad
            small = (ADAPTER_SCALE * dot_nt(up_ref[g], grad)).astype(BF16)
            smalls.append(small)
            gup_ref[g] = (ADAPTER_SCALE * dot_nn(mid_ref[g], grad)).astype(BF16)
        for z in range(splits):
            columns = slice(z * part, (z + 1) * part)
            copies[z].wait()
            result = dot_nt(low[...], held[z])
            for g in range(groups):
                out_ref[z, g] = (
                    result[g * shard : (g + 1) * shard] + dot_tn(smalls[g], down_ref[g, :, columns])
                ).astype(BF16)
                gdown_ref[g, :, columns] = dot_nn(smalls[g], att_ref[z, g]).astype(BF16)

    return kernel_call(
        body,
        "project_out_back",
        (1,),
        [
            whole_block(upstream.shape),
            whole_block((1, width)),
            ANYWHERE,
            whole_block(down.shape),
            whole_block(up.shape),
            whole_block(mixed.shape),
            whole_block(attended.shape),
            whole_block(mids.shape),
        ]
        + [whole_block((shard, width))] * (groups * number),
        [
            whole_block((groups, shard, width)),
            whole_block((groups, rank, width)),
            whole_block((groups, rank, width)),
            whole_block(attended.shape),
        ],
        [
            shape_of((groups, shard, width), F32),
            shape_of((groups, rank, width), BF16),
            shape_of((groups, rank, width), BF16),
            shape_of(attended.shape, BF16),
        ],
        scratch=[
            pltpu.VMEM((rows, width), BF16),
            pltpu.VMEM((splits, part, width), BF16),
            pltpu.SemaphoreType.DMA((splits,)),
        ],
        flops=2 * rows * width * width,
        moved=2 * width * width,
    )(
        upstream, gain, w_out, down, up, mixed, attended, mids,
        *[array for found in pieces for array in found],
    )


def adapter_grads(place, group, grads, normed, ups, devices):
    listed = is_list(grads)
    splits, (_, shard, part) = piece_shape(grads)
    width = splits * part
    own = ups.shape[1]
    rank = own // 3
    slice_width = width // devices

    def body(place_ref, normed_ref, up_ref, *rest):
        refs, (small_ref, down_ref, low) = rest[:splits], rest[splits:]
        for which in range(3):
            for r in range(splits):
                owner = lax.rem(place_ref[0] + r, splits) if listed else r
                low[:, pl.ds(pl.multiple_of(owner * part, part), part)] = refs[r][which]
            at = slice(which * rank, (which + 1) * rank)
            small = (ADAPTER_SCALE * dot_nt(up_ref[at], low[...])).astype(BF16)
            small_ref[at] = small
            result = dot_nn(small, normed_ref[...]).astype(BF16)
            for e in range(devices):
                down_ref[e, at] = result[:, e * slice_width : (e + 1) * slice_width]

    return kernel_call(
        body,
        "adapter_grads",
        (1,),
        [
            pl.BlockSpec((shard, width), lambda i, s: (group, 0)),
            group_block(ups.shape, group),
        ]
        + piece_specs(grads, (3, shard, part), lambda i, s: (0, 0, 0)),
        [whole_block((own, shard)), whole_block((devices, own, slice_width))],
        [shape_of((own, shard), BF16), shape_of((devices, own, slice_width), BF16)],
        scratch=[pltpu.VMEM((shard, width), BF16)],
        prefetch=1,
        flops=12 * shard * rank * width,
        moved=6 * shard * width,
    )(place, normed, ups, *piece_arrays(grads, splits))


def project_first_back(place, grads, smalls, downs, w_qkv, tokens, gain, grad_mixed):
    groups = len(grads)
    listed = [is_list(pieces) for pieces in grads]
    splits, (_, shard, part) = piece_shape(grads[0])
    width = splits * part
    rows = groups * shard

    rank = downs.shape[1] // 3

    def body(place_ref, down_ref, w_ref, tok_ref, gain_ref, mixed_ref, *rest):
        small_refs, refs = rest[:groups], rest[groups : groups + groups * splits]
        out_ref, low, total, held, sem = rest[groups + groups * splits :]
        which = pl.program_id(0)

        def copy(p):
            return pltpu.make_async_copy(w_ref.at[p], held.at[p], sem.at[p])

        @pl.when(which == 0)
        def _():
            for p in range(3):
                copy(p).start()

        for g in range(groups):
            for r in range(splits):
                owner = lax.rem(place_ref[0] + r, splits) if listed[g] else r
                low[
                    g * shard : (g + 1) * shard, pl.ds(pl.multiple_of(owner * part, part), part)
                ] = refs[g * splits + r][0]
        at = pl.ds(pl.multiple_of(which * rank, rank), rank)
        small = jnp.concatenate(
            [dot_tn(small_refs[g][at], down_ref[g, at]) for g in range(groups)], axis=0
        )
        copy(which).wait()
        result = dot_nt(low[...], held[which]) + small

        @pl.when(which == 0)
        def _():
            total[...] = result

        @pl.when(which == 1)
        def _():
            total[...] += result

        @pl.when(which == 2)
        def _():
            back = norm_back(tok_ref[...].astype(F32), gain_ref[...], total[...] + result)
            for g in range(groups):
                out_ref[g] = mixed_ref[g] + back[g * shard : (g + 1) * shard]

    return kernel_call(
        body,
        "project_first_back",
        (3,),
        [
            whole_block(downs.shape),
            ANYWHERE,
            whole_block((rows, width)),
            whole_block((1, width)),
            whole_block(grad_mixed.shape),
        ]
        + [whole_block((3 * rank, shard))] * groups
        + [
            spec
            for pieces in grads
            for spec in piece_specs(pieces, (1, shard, part), lambda p, s: (p, 0, 0))
        ],
        whole_block((groups, shard, width)),
        shape_of((groups, shard, width), F32),
        scratch=[
            pltpu.VMEM((rows, width), BF16),
            pltpu.VMEM((rows, width), F32),
            pltpu.VMEM((3, width, width), BF16),
            pltpu.SemaphoreType.DMA((3,)),
        ],
        prefetch=1,
        flops=6 * rows * width * width,
        moved=6 * width * width,
    )(
        place, downs, w_qkv, tokens, gain, grad_mixed, *smalls,
        *[piece for pieces in grads for piece in piece_arrays(pieces, splits)],
    )


def local(
    tokens,
    cotangent,
    lengths,
    adapter_choice,
    expert_ids,
    gate_weights,
    attn_gain,
    moe_gain,
    query_gain,
    key_gain,
    w_qkv,
    w_out,
    expert_gate,
    expert_up,
    expert_down,
    adapt_down,
    first_down,
    second_down,
    adapt_up,
    first_up,
    second_up,
):
    groups, shard, width = tokens.shape
    splits = lax.axis_size("seq")
    devices = lax.axis_size("exp")
    here = lax.axis_index("seq")
    total = shard * splits
    part = width // splits
    rows = groups * shard
    sets, projections, slice_width, rank = adapt_down.shape
    local_experts = expert_gate.shape[0]
    experts = local_experts * devices
    top = expert_ids.shape[-1]
    capacity = 3 * rows * top // (2 * experts)
    listed = [False] * groups

    position = lax.axis_index("exp")
    place = jnp.stack([here, position]).astype(jnp.int32)
    flat_tokens = tokens.reshape(rows, width)
    gain_row = attn_gain.reshape(1, width)
    moe_row = moe_gain.reshape(1, width)
    query_row = query_gain.reshape(1, HEAD)
    key_row = key_gain.reshape(1, HEAD)

    own_positions = here * shard + jnp.arange(shard, dtype=jnp.int32)
    own_live = own_positions[None, :] < lengths[:, None]
    upstream = jnp.where(own_live[:, :, None], cotangent, jnp.zeros((), BF16))
    down_rows = jnp.swapaxes(adapt_down.astype(BF16), 2, 3)
    adapter_rows = jnp.concatenate(
        [
            down_rows[:, :3].reshape(-1, slice_width),
            down_rows[:, 3].reshape(-1, slice_width),
            adapt_up[:, :3].astype(BF16).reshape(-1, slice_width),
            adapt_up[:, 3].astype(BF16).reshape(-1, slice_width),
        ]
    )
    all_adapters = lax.all_gather(adapter_rows, "exp")

    base, _, normed = project_first(
        place, after(flat_tokens, adapter_rows), gain_row, w_qkv, groups, splits, listed
    )
    raw = [forward_seq(base[0])]
    cot_rows = lax.all_gather(after(upstream, normed).reshape(rows, width), "exp")

    own = 3 * rank
    chosen = jnp.sum(adapter_choice * jnp.arange(sets, dtype=jnp.int32)[None, :], axis=1)
    sections = [
        (0, own), (sets * own, rank), (sets * (own + rank), own), (sets * (2 * own + rank), rank),
    ]
    downs, out_downs, ups, out_ups, mids = pick_sets(
        all_adapters, chosen, groups, sets, sections, normed
    )
    all_mids = by_distance(jnp.stack(forward_seq([mids] * splits)))
    raw[0], all_mids = lax.optimization_barrier((raw[0], all_mids))
    for g in range(1, groups):
        raw.append(forward_seq(after(base[g], raw[g - 1])))
    own_ups = lax.dynamic_slice_in_dim(ups, here * part, part, axis=2)
    own_ups = own_ups.reshape(groups, 3, rank, part)

    blocks = jnp.arange(splits, dtype=jnp.int32)
    frequency = ROPE_BASE ** (-(2.0 / HEAD) * jnp.arange(HEAD // 2, dtype=F32))
    tables = []
    for g in range(groups):
        positions = blocks[:, None] * shard + jnp.arange(shard, dtype=jnp.int32)[None, :]
        angles = after(positions, raw[0]).reshape(total, 1).astype(F32) * frequency[None, :]
        cosine, sine = jnp.cos(angles), jnp.sin(angles)
        tables.append(
            (
                positions.reshape(1, total),
                jnp.concatenate([cosine, cosine], axis=1),
                jnp.concatenate([-sine, sine], axis=1),
            )
        )

    saved, heads_rows = [], []
    for g in range(groups):
        if g:
            raw[g] = after(raw[g], heads_rows)
        att, kept = attend(
            lengths[g : g + 1],
            raw[g],
            all_mids[:, g],
            own_ups[g],
            query_row,
            key_row,
            *tables[g],
        )
        saved.append(kept)
        heads_rows.append(att)
    attended = lax.all_to_all(jnp.stack(heads_rows, axis=1), "seq", 0, 0)
    mixed, moe_rows, mid_out = project_out(
        attended, w_out, out_downs, out_ups, tokens, moe_row
    )

    ids, gates = after((expert_ids, gate_weights), attended)
    ids = ids.reshape(rows, top).T
    gates = gates.reshape(rows, top).T
    choice = adapter_choice.astype(F32).reshape(1, groups * sets)
    choice = jnp.pad(choice, ((0, 0), (0, rows - groups * sets)))
    meta = lax.all_to_all(route(ids, gates, choice, devices, local_experts), "exp", 0, 0)
    choices = meta[:, 2, 0, : groups * sets].reshape(devices, groups, sets).astype(BF16)
    meta = by_relative(meta)

    half = local_experts // 2
    grad_front = expert_grad_hidden(
        place, cot_rows, after(meta, moe_rows), expert_down, capacity, 0, half
    )
    grad_back = expert_grad_hidden(
        place, cot_rows, after(meta, grad_front), expert_down, capacity, half, local_experts
    )
    gathered = gather_rows(moe_rows, grad_front, grad_back)

    paired = devices == 8 and groups == 2
    hidden, grad_slots = expert_middle(
        gathered, meta, expert_gate, expert_up, (grad_front, grad_back), capacity
    )
    parts, others = combine(place, grad_slots, meta, capacity, groups, paired)
    if paired:
        beside = swap(others, 1).reshape(devices // 2, groups, shard, width)
        far_sums = [add_low(parts[6][g], beside[3][g]) for g in range(groups)]
        near_sums = [add_low(parts[WAYS[g][0]][g], beside[WAYS[g][0] // 2][g]) for g in range(groups)]
        far_sums, near_sums = lax.optimization_barrier((far_sums, near_sums))
        far = [swap(far_sums[g], WAYS[g][0]) for g in range(groups)]
        near = [swap(near_sums[g], WAYS[g][0]) for g in range(groups)]
        produced = expert_produce(
            place, after(hidden, far_sums), meta, expert_down, capacity, 0, half
        )
        far, produced = lax.optimization_barrier((far, produced))
        joined_sums = [
            add_low(parts[WAYS[g][1]][g], beside[WAYS[g][1] // 2][g], far[g]) for g in range(groups)
        ]
        joined = [swap(joined_sums[g], WAYS[g][1]) for g in range(groups)]
        grad_pieces = [
            [parts[0][g], beside[0][g], near[g], joined[g]] for g in range(groups)
        ]
        produced = after(produced, joined_sums)
    else:
        summed = lax.psum_scatter(parts, "exp").reshape(groups, shard, width)
        grad_pieces = [[summed[g]] for g in range(groups)]
        produced = expert_produce(place, hidden, meta, expert_down, capacity, 0, half)
    out_parts = expert_produce(
        place, hidden, meta, expert_down, capacity, half, local_experts, produced
    )
    grad_pieces = after(grad_pieces, out_parts)
    grad_mixed, grad_out_downs, grad_out_ups, grad_att = project_out_back(
        grad_pieces, mixed, upstream, moe_row, w_out, out_downs, out_ups, attended, mid_out
    )
    out_sum = lax.psum_scatter(after(out_parts, grad_mixed), "exp").reshape(groups, shard, width)
    grad_att = lax.all_to_all(grad_att, "seq", 0, 0)
    grad_raw, gups = [], []
    for g in range(groups):
        if g:
            grad_att = after(grad_att, gups)
        back, gup = attend_back(
            lengths[g : g + 1],
            grad_att,
            g,
            saved[g],
            all_mids[:, g],
            rank,
            query_row,
            key_row,
            *tables[g],
        )
        gups.append(gup)
        grad_raw.append(forward_seq(after(back, grad_raw) if g else back))

    gups = jnp.stack(after(gups, grad_raw[0]))
    wide_ups = lax.dynamic_update_slice_in_dim(
        jnp.zeros((groups, own, width), BF16), gups, here * part, axis=2
    )
    early = jnp.concatenate([grad_out_downs, wide_ups, grad_out_ups], axis=1)
    early = jnp.moveaxis(early.reshape(groups, -1, devices, slice_width), 2, 0)
    output = (mixed + after(out_sum, gups).astype(F32)).astype(BF16)

    smalls, late = [], []
    for g in range(groups):
        small, down = adapter_grads(place, g, grad_raw[g], normed, ups, devices)
        smalls.append(small)
        late.append(down)
    late = jnp.concatenate([jnp.stack(late, axis=1), early], axis=2)
    late = lax.all_to_all(late, "exp", 0, 0)
    grad_input = project_first_back(
        place, grad_raw, smalls, downs, w_qkv, after(flat_tokens, output), gain_row, grad_mixed
    )
    late = after(late, grad_input)
    pieces = jnp.einsum("dgk,dgrw->krw", choices, late, preferred_element_type=F32)
    pieces = pieces.astype(BF16)
    pieces = pieces.reshape(splits, -1, slice_width)
    order = (here + jnp.arange(splits)) % splits
    pieces = list(jnp.take(pieces, order, axis=0))
    summed = add_low(*forward_seq(pieces))
    in_sets = by_distance(jnp.stack(forward_seq([summed] * splits)))
    in_sets = in_sets.reshape(sets, 2, projections, rank, slice_width).astype(F32)
    shard_down = jnp.swapaxes(in_sets[:, 0], 2, 3)
    shard_up = in_sets[:, 1]
    new_first_down, new_second_down, new_down = adam_update(
        adapt_down, shard_down, first_down, second_down, RATE_DOWN
    )
    new_first_up, new_second_up, new_up = adam_update(
        adapt_up, shard_up, first_up, second_up, RATE_UP
    )
    return (
        output,
        grad_input,
        new_first_down,
        new_second_down,
        new_down,
        new_first_up,
        new_second_up,
        new_up,
    )


def solution(mesh):
    in_specs = (
        P("exp", "seq", None),
        P("exp", "seq", None),
        P("exp"),
        P("exp", None),
        P("exp", "seq", None, None, None),
        P("exp", "seq", None, None, None),
        P(),
        P(),
        P(),
        P(),
        P(),
        P(),
        P("exp", None, None),
        P("exp", None, None),
        P("exp", None, None),
        P(None, None, "exp", None),
        P(None, None, "exp", None),
        P(None, None, "exp", None),
        P(None, None, None, "exp"),
        P(None, None, None, "exp"),
        P(None, None, None, "exp"),
    )
    out_specs = (
        P("exp", "seq", None),
        P("exp", "seq", None),
        P(None, None, "exp", None),
        P(None, None, "exp", None),
        P(None, None, "exp", None),
        P(None, None, None, "exp"),
        P(None, None, None, "exp"),
        P(None, None, None, "exp"),
    )
    return jax.shard_map(local, mesh=mesh, in_specs=in_specs, out_specs=out_specs, check_vma=False)
```

```python
import functools

import jax
import jax.numpy as jnp
from jax import lax
from jax.experimental import pallas as pl
from jax.experimental.pallas import tpu as pltpu
from jax.sharding import PartitionSpec as P

HEAD = 128
STEP = 5

NORM_EPS = 1e-05
ROPE_BASE = 50000.0
ADAPTER_SCALE = 0.5
BETA_FIRST = 0.5
BETA_SECOND = 0.5
RATE_DOWN = 0.02
RATE_UP = 0.2
WEIGHT_DECAY = 0.01
ADAM_EPS = 1e-08
MASKED = -1e30
SCORE_SCALE = HEAD ** (-0.5)

F32 = jnp.float32
BF16 = jnp.bfloat16
VMEM_LIMIT = 62 * 1024 * 1024
COST_SHARE = 0.01


def dot_nn(a, b):
    return lax.dot_general(a, b, (((1,), (0,)), ((), ())), preferred_element_type=F32)


def dot_nt(a, b):
    return lax.dot_general(a, b, (((1,), (1,)), ((), ())), preferred_element_type=F32)


def dot_tn(a, b):
    return lax.dot_general(a, b, (((0,), (0,)), ((), ())), preferred_element_type=F32)


def inverse_rms(values):
    return lax.rsqrt(jnp.mean(values * values, axis=-1, keepdims=True) + NORM_EPS)


def norm_back(values, gain, upstream):
    inverse = inverse_rms(values)
    scaled = upstream * gain
    return inverse * scaled - values * (inverse * inverse * inverse) * jnp.mean(
        values * scaled, axis=-1, keepdims=True
    )


def sigmoid(values):
    return 0.5 + 0.5 * jnp.tanh(0.5 * values)


def adam_update(weight, gradient, first, second, step_rate):
    new_first = BETA_FIRST * first + (1.0 - BETA_FIRST) * gradient
    new_second = BETA_SECOND * second + (1.0 - BETA_SECOND) * gradient * gradient
    first_hat = new_first / (1.0 - BETA_FIRST**STEP)
    second_hat = new_second / (1.0 - BETA_SECOND**STEP)
    new_weight = weight - step_rate * (
        first_hat / (jnp.sqrt(second_hat) + ADAM_EPS) + WEIGHT_DECAY * weight
    )
    return (new_first, new_second, new_weight)


def shape_of(shape, dtype):
    return jax.ShapeDtypeStruct(shape, dtype)


def whole_block(shape):
    rank = len(shape)
    return pl.BlockSpec(tuple(shape), lambda *_: (0,) * rank)


def kernel_call(
    body, name, grid, in_specs, out_specs, out_shape, scratch=(), prefetch=0, flops=0, moved=0,
    aliases=None,
):
    return pl.pallas_call(
        body,
        grid_spec=pltpu.PrefetchScalarGridSpec(
            num_scalar_prefetch=prefetch,
            grid=grid,
            in_specs=in_specs,
            out_specs=out_specs,
            scratch_shapes=list(scratch),
        ),
        out_shape=out_shape,
        input_output_aliases=aliases or {},
        name=name,
        cost_estimate=pl.CostEstimate(
            flops=int(flops * COST_SHARE), bytes_accessed=int(moved * COST_SHARE), transcendentals=0
        ),
        compiler_params=pltpu.CompilerParams(vmem_limit_bytes=VMEM_LIMIT),
    )


def swap(values, mask):
    count = lax.axis_size("exp")
    return lax.ppermute(values, "exp", [(i, i ^ mask) for i in range(count)])


def shift(values, distance):
    count = lax.axis_size("seq")
    return lax.ppermute(values, "seq", [(i, (i + distance) % count) for i in range(count)])


def shift_order():
    count = lax.axis_size("seq")
    return sorted(range(1, count), key=lambda r: -min(r, count - r))


def forward_seq(pieces):
    if not isinstance(pieces, (list, tuple)):
        return lax.all_to_all(pieces, "seq", 0, 0)
    came = {r: shift(pieces[r], r) for r in shift_order()}
    return [pieces[0]] + [came[r] for r in range(1, len(pieces))]


def backward_seq(pieces):
    if not isinstance(pieces, (list, tuple)):
        return lax.all_to_all(pieces, "seq", 0, 0)
    came = {r: shift(pieces[r], -r) for r in shift_order()}
    return [pieces[0]] + [came[r] for r in range(1, len(pieces))]


def tell_all(values, axis):
    count = lax.axis_size(axis)
    return lax.all_to_all(jnp.broadcast_to(values[None], (count,) + values.shape), axis, 0, 0)


def by_distance(stacked):
    count = lax.axis_size("seq")
    order = (lax.axis_index("seq") - jnp.arange(count)) % count
    return jnp.take(stacked, order, axis=0)


def by_relative(stacked):
    count = lax.axis_size("exp")
    return jnp.take(stacked, lax.axis_index("exp") ^ jnp.arange(count), axis=0)


WAYS = ((2, 4), (4, 2))


def gather_rows(rows):
    count = lax.axis_size("exp")
    if count != 8 or len(rows) != 2:
        everything = by_relative(lax.all_gather(jnp.concatenate(rows), "exp"))
        return [[everything[m]] for m in range(count)]
    near = {2: [None, None], 4: [None, None], 6: [None, None]}
    for g, (first, _) in enumerate(WAYS):
        near[first][g] = swap(rows[g], first)
    for g, (_, second) in enumerate(WAYS):
        near[second][g] = swap(rows[g], second)
    for g, (first, second) in enumerate(WAYS):
        near[6][g] = swap(near[first][g], second)
    found = [list(rows), [swap(block, 1) for block in rows]]
    for m in (2, 4, 6):
        found += [near[m], [swap(block, 1) for block in near[m]]]
    return found


def add_low(*values):
    return functools.reduce(jnp.add, [value.astype(F32) for value in values]).astype(BF16)


def after(values, *first):
    return lax.optimization_barrier((values, first))[0]


ANYWHERE = pl.BlockSpec(memory_space=pl.ANY)


def group_block(shape, group):
    rank = len(shape) - 1
    return pl.BlockSpec((None,) + tuple(shape[1:]), lambda *_: (group,) + (0,) * rank)


def is_list(pieces):
    return isinstance(pieces, (list, tuple))


def piece_shape(pieces):
    if is_list(pieces):
        return len(pieces), pieces[0].shape
    return pieces.shape[0], pieces.shape[1:]


def piece_arrays(pieces, splits):
    return list(pieces) if is_list(pieces) else [pieces] * splits


def piece_specs(pieces, block, index):
    if is_list(pieces):
        return [pl.BlockSpec(block, index)] * len(pieces)
    return [
        pl.BlockSpec((None,) + tuple(block), lambda *at, r=r: (r,) + tuple(index(*at)))
        for r in range(pieces.shape[0])
    ]


def out_specs_of(listed, splits, block, index):
    if listed:
        return [pl.BlockSpec(block, index)] * splits
    return [pl.BlockSpec((splits,) + tuple(block), lambda *at: (0,) + tuple(index(*at)))]


def out_shapes_of(listed, splits, shape, dtype):
    if listed:
        return [shape_of(shape, dtype)] * splits
    return [shape_of((splits,) + tuple(shape), dtype)]


def out_refs_of(listed, refs):
    return list(refs) if listed else [refs[0].at[r] for r in range(refs[0].shape[0])]


def out_pieces_of(listed, results):
    return list(results) if listed else results[0]


def project_first(place, tokens, gain, w_qkv, groups, splits, listed):
    rows, width = tokens.shape
    part = width // splits
    shard = rows // groups
    counts = [splits if listed[g] else 1 for g in range(groups)]
    total = sum(counts)

    def body(place_ref, tok_ref, gain_ref, w_ref, *rest):
        outs = rest[:total]
        parts_ref, normed_ref, held, sem = rest[total:]
        which = pl.program_id(0)

        def owner(r):
            return lax.rem(place_ref[0] + r, splits)

        def copy(p, r):
            columns = pl.ds(pl.multiple_of(owner(r) * part, part), part)
            return pltpu.make_async_copy(
                w_ref.at[p, :, columns],
                held.at[p, :, pl.ds(r * part, part)],
                sem.at[p, r],
            )

        @pl.when(which == 0)
        def _():
            for p in range(3):
                for r in range(splits):
                    copy(p, r).start()
            values = tok_ref[...].astype(F32)
            low = (values * inverse_rms(values) * gain_ref[...]).astype(BF16)
            normed_ref[...] = low
            for z in range(splits):
                for g in range(groups):
                    parts_ref[z, g] = low[
                        g * shard : (g + 1) * shard, z * part : (z + 1) * part
                    ]

        for r in range(splits):
            copy(which, r).wait()
            result = dot_nn(normed_ref[...], held[which, :, r * part : (r + 1) * part])
            first = 0
            for g in range(groups):
                low = result[g * shard : (g + 1) * shard].astype(BF16)
                if listed[g]:
                    outs[first + r][0] = low
                else:
                    outs[first][owner(r), 0] = low
                first += counts[g]

    specs, shapes = [], []
    for g in range(groups):
        specs += out_specs_of(listed[g], splits, (1, shard, part), lambda p, s: (p, 0, 0))
        shapes += out_shapes_of(listed[g], splits, (3, shard, part), BF16)
    result = kernel_call(
        body,
        "project_first",
        (3,),
        [whole_block((rows, width)), whole_block((1, width)), ANYWHERE],
        specs + [whole_block((splits, groups, shard, part)), whole_block((rows, width))],
        shapes
        + [shape_of((splits, groups, shard, part), BF16), shape_of((rows, width), BF16)],
        scratch=[
            pltpu.VMEM((3, width, width), BF16),
            pltpu.SemaphoreType.DMA((3, splits)),
        ],
        prefetch=1,
        flops=6 * rows * width * width,
        moved=6 * width * width,
    )(place, tokens, gain, w_qkv)
    outs, first = [], 0
    for g in range(groups):
        outs.append(out_pieces_of(listed[g], result[first : first + counts[g]]))
        first += counts[g]
    return outs, result[total], result[total + 1]


def pick_sets(gathered, picks, groups, sets, sections, normed=None):
    count, _, part = gathered.shape
    width = count * part
    shard = normed.shape[0] // groups if normed is not None else 0
    number = len(sections)

    def body(pick_ref, in_ref, *rest):
        normed_ref = rest[0] if shard else None
        outs = rest[1:] if shard else rest
        outs, sem = outs[:-1], outs[-1]
        copies = []
        for g in range(groups):
            for i, (first, own) in enumerate(sections):
                for e in range(count):
                    copies.append(
                        pltpu.make_async_copy(
                            in_ref.at[e, pl.ds(pl.multiple_of(first + pick_ref[g] * own, own), own)],
                            outs[i].at[g, :, pl.ds(e * part, part)],
                            sem.at[(g * number + i) * count + e],
                        )
                    )
        for copy in copies:
            copy.start()
        for copy in copies:
            copy.wait()
        if shard:
            for g in range(groups):
                outs[number][g] = dot_nt(
                    outs[0][g], normed_ref[g * shard : (g + 1) * shard]
                ).astype(BF16)

    shapes = [(groups, own, width) for _, own in sections]
    if shard:
        shapes.append((groups, sections[0][1], shard))
    return kernel_call(
        body,
        "pick_sets",
        (1,),
        [ANYWHERE] + ([whole_block(normed.shape)] if shard else []),
        [whole_block(shape) for shape in shapes],
        [shape_of(shape, BF16) for shape in shapes],
        scratch=[pltpu.SemaphoreType.DMA((groups * number * count,))],
        prefetch=1,
        moved=4 * groups * width * sum(own for _, own in sections),
    )(picks, gathered, *([normed] if shard else []))


def route(ids, gates, choice, experts):
    top, tokens = ids.shape

    def body(ids_ref, gates_ref, choice_ref, out_ref):
        expert = lax.broadcasted_iota(jnp.int32, (experts, tokens), 0)
        weights = jnp.zeros((experts, tokens), F32)
        named = jnp.zeros((experts, tokens), F32)
        for k in range(top):
            hit = expert == ids_ref[k : k + 1]
            weights = jnp.where(hit, gates_ref[k : k + 1], weights)
            named = jnp.where(hit, 1.0, named)
        earlier = lax.broadcasted_iota(jnp.int32, (tokens, tokens), 0) < lax.broadcasted_iota(
            jnp.int32, (tokens, tokens), 1
        )
        ranks = dot_nn(named.astype(BF16), jnp.where(earlier, 1.0, 0.0).astype(BF16))
        slots = jnp.where(named > 0.0, ranks, -1.0)
        front = weights.astype(BF16)
        out_ref[:experts] = slots.astype(BF16)
        out_ref[experts : 2 * experts] = front
        out_ref[2 * experts : 3 * experts] = (weights - front.astype(F32)).astype(BF16)
        out_ref[3 * experts :] = jnp.broadcast_to(choice_ref[...], (16, tokens)).astype(BF16)

    shape = (3 * experts + 16, tokens)
    return kernel_call(
        body,
        "route",
        (1,),
        [whole_block(ids.shape), whole_block(gates.shape), whole_block(choice.shape)],
        whole_block(shape),
        shape_of(shape, BF16),
        moved=12 * experts * tokens,
    )(ids, gates, choice)


def rotate(values, cosine, sine):
    return values * cosine + pltpu.roll(values, HEAD // 2, 1) * sine


def rotate_back(values, cosine, sine):
    return values * cosine - pltpu.roll(values, HEAD // 2, 1) * sine


def softmax_rows(queries, keys, live):
    scores = jnp.where(live, dot_nt(queries, keys) * SCORE_SCALE, MASKED)
    exponent = jnp.exp(scores - jnp.max(scores, axis=-1, keepdims=True))
    return exponent * (1.0 / jnp.sum(exponent, axis=-1, keepdims=True))


def attend(length, raw, mids, ups, query_gain, key_gain, positions, cosine, sine):
    listed = is_list(raw)
    splits, (_, shard, part) = piece_shape(raw)
    rank = ups.shape[1]
    total = splits * shard
    heads = part // HEAD

    def body(len_ref, up_ref, qg_ref, kg_ref, pos_ref, cos_ref, sin_ref, *rest):
        raw_refs, mid_ref = rest[:splits], rest[splits]
        att_refs = out_refs_of(listed, rest[splits + 1 : -5])
        q_ref, k_ref, v_ref, rq_ref, rk_ref = rest[-5:]

        def full(which):
            base = jnp.concatenate([ref[which] for ref in raw_refs], axis=0).astype(F32)
            mid = jnp.concatenate(
                [mid_ref[r, which * rank : (which + 1) * rank] for r in range(splits)], axis=1
            )
            return base + ADAPTER_SCALE * dot_tn(mid, up_ref[which])

        raw_q, raw_k, raw_v = full(0), full(1), full(2)
        rq_ref[0] = raw_q
        rk_ref[0] = raw_k
        cosine, sine = cos_ref[...], sin_ref[...]
        queries = rotate(raw_q * inverse_rms(raw_q) * qg_ref[...], cosine, sine).astype(BF16)
        keys = rotate(raw_k * inverse_rms(raw_k) * kg_ref[...], cosine, sine).astype(BF16)
        values = raw_v.astype(BF16)
        q_ref[0] = queries
        k_ref[0] = keys
        v_ref[0] = values
        weights = softmax_rows(queries, keys, pos_ref[...] < len_ref[0]).astype(BF16)
        result = dot_nn(weights, values).astype(BF16)
        for r in range(splits):
            att_refs[r][...] = result[r * shard : (r + 1) * shard]

    head_block = pl.BlockSpec((1, total, HEAD), lambda h, s: (h, 0, 0))
    result = kernel_call(
        body,
        "attend",
        (heads,),
        [
            pl.BlockSpec((3, rank, HEAD), lambda h, s: (0, 0, h)),
            whole_block((1, HEAD)),
            whole_block((1, HEAD)),
            whole_block((1, total)),
            whole_block((total, HEAD)),
            whole_block((total, HEAD)),
        ]
        + piece_specs(raw, (3, shard, HEAD), lambda h, s: (0, 0, h))
        + [whole_block(mids.shape)],
        out_specs_of(listed, splits, (shard, HEAD), lambda h, s: (0, h)) + [head_block] * 5,
        out_shapes_of(listed, splits, (shard, part), BF16)
        + [shape_of((heads, total, HEAD), BF16)] * 3
        + [shape_of((heads, total, HEAD), F32)] * 2,
        prefetch=1,
        flops=4 * heads * total * total * HEAD,
        moved=heads * total * HEAD * 24 + 4 * heads * total * total,
    )(length, ups, query_gain, key_gain, positions, cosine, sine, *piece_arrays(raw, splits), mids)
    return out_pieces_of(listed, result[:-5]), result[-5:]


def attend_back(length, grads, group, saved, mids, rank, query_gain, key_gain, positions, cosine, sine):
    listed = False
    splits, _, shard, part = grads.shape
    total = splits * shard
    heads = part // HEAD

    def body(len_ref, qg_ref, kg_ref, pos_ref, cos_ref, sin_ref, *rest):
        grad_refs, mid_ref = rest[:splits], rest[splits]
        q_ref, k_ref, v_ref, rq_ref, rk_ref = rest[splits + 1 : splits + 6]
        out_refs = out_refs_of(listed, rest[splits + 6 : -1])
        gup_ref = rest[-1]
        queries, keys, values = q_ref[0], k_ref[0], v_ref[0]
        grad = jnp.concatenate([ref[...] for ref in grad_refs], axis=0)
        weights = softmax_rows(queries, keys, pos_ref[...] < len_ref[0])
        grad_probs = dot_nt(grad, values)
        inner = jnp.sum(weights * grad_probs, axis=-1, keepdims=True)
        grad_scores = (weights * (grad_probs - inner)).astype(BF16)
        grad_q = dot_nn(grad_scores, keys) * SCORE_SCALE
        grad_k = dot_tn(grad_scores, queries) * SCORE_SCALE
        grad_v = dot_tn(weights.astype(BF16), grad)
        cosine, sine = cos_ref[...], sin_ref[...]
        grad_q = norm_back(rq_ref[0], qg_ref[...], rotate_back(grad_q, cosine, sine))
        grad_k = norm_back(rk_ref[0], kg_ref[...], rotate_back(grad_k, cosine, sine))

        for which, value in enumerate((grad_q, grad_k, grad_v)):
            low = value.astype(BF16)
            for r in range(splits):
                out_refs[r][which] = low[r * shard : (r + 1) * shard]
            mid = jnp.concatenate(
                [mid_ref[r, which * rank : (which + 1) * rank] for r in range(splits)], axis=1
            )
            gup_ref[which * rank : (which + 1) * rank] = (
                ADAPTER_SCALE * dot_nn(mid, low)
            ).astype(BF16)

    head_block = pl.BlockSpec((1, total, HEAD), lambda h, s: (h, 0, 0))
    result = kernel_call(
        body,
        "attend_back",
        (heads,),
        [
            whole_block((1, HEAD)),
            whole_block((1, HEAD)),
            whole_block((1, total)),
            whole_block((total, HEAD)),
            whole_block((total, HEAD)),
        ]
        + [
            pl.BlockSpec((None, None, shard, HEAD), lambda h, s, r=r: (r, group, 0, h))
            for r in range(splits)
        ]
        + [whole_block(mids.shape)]
        + [head_block] * 5,
        out_specs_of(listed, splits, (3, shard, HEAD), lambda h, s: (0, 0, h))
        + [pl.BlockSpec((3 * rank, HEAD), lambda h, s: (0, h))],
        out_shapes_of(listed, splits, (3, shard, part), BF16)
        + [shape_of((3 * rank, part), BF16)],
        prefetch=1,
        flops=10 * heads * total * total * HEAD,
        moved=heads * total * HEAD * 24 + 8 * heads * total * total,
    )(length, query_gain, key_gain, positions, cosine, sine, *[grads] * splits, mids, *saved)
    return out_pieces_of(listed, result[:-1]), result[-1]


def project_out(attended, w_out, down, up, tokens, gain):
    splits, groups, shard, part = attended.shape
    width = splits * part
    rank = down.shape[1]
    rows = groups * shard

    def body(att_ref, w_ref, down_ref, up_ref, tok_ref, gain_ref, *rest):
        mixed_ref, mid_ref = rest[:2]
        moe_refs = rest[2 : 2 + groups]
        att, held, sem = rest[2 + groups :]
        copies = [
            pltpu.make_async_copy(
                w_ref.at[pl.ds(i * part, part)], held.at[pl.ds(i * part, part)], sem.at[i]
            )
            for i in range(splits)
        ]
        for copy in copies:
            copy.start()
        adapter = []
        for g in range(groups):
            at = slice(g * shard, (g + 1) * shard)
            for z in range(splits):
                att[at, z * part : (z + 1) * part] = att_ref[z, g]
            mid = dot_nt(down_ref[g], att[at]).astype(BF16)
            mid_ref[g] = mid
            adapter.append(
                tok_ref[g].astype(F32) + ADAPTER_SCALE * dot_tn(mid, up_ref[g])
            )
        total = jnp.concatenate(adapter, axis=0)
        for i, copy in enumerate(copies):
            copy.wait()
            total += dot_nn(att[:, i * part : (i + 1) * part], held[i * part : (i + 1) * part])
        low = (total * inverse_rms(total) * gain_ref[...]).astype(BF16)
        for g in range(groups):
            mixed_ref[g] = total[g * shard : (g + 1) * shard]
            moe_refs[g][...] = low[g * shard : (g + 1) * shard]

    result = kernel_call(
        body,
        "project_out",
        (1,),
        [
            whole_block(attended.shape),
            ANYWHERE,
            whole_block(down.shape),
            whole_block(up.shape),
            whole_block(tokens.shape),
            whole_block((1, width)),
        ],
        [
            whole_block((groups, shard, width)),
            whole_block((groups, rank, shard)),
        ]
        + [whole_block((shard, width))] * groups,
        [shape_of((groups, shard, width), F32), shape_of((groups, rank, shard), BF16)]
        + [shape_of((shard, width), BF16)] * groups,
        scratch=[
            pltpu.VMEM((rows, width), BF16),
            pltpu.VMEM((width, width), BF16),
            pltpu.SemaphoreType.DMA((splits,)),
        ],
        flops=2 * rows * width * width,
        moved=2 * width * width,
    )(attended, w_out, down, up, tokens, gain)
    return result[0], result[1], result[2:]


def one_hot(slot_row, capacity):
    tokens = slot_row.shape[1]
    index = lax.broadcasted_iota(jnp.int32, (capacity, tokens), 0).astype(F32)
    return index == slot_row


def pick_rows(sources, meta_ref, ring, sem, picked, capacity, weigh, begin=0):
    count = meta_ref.shape[0]
    experts = picked.shape[0]
    slots = ring.shape[0]

    def copies(m):
        found = sources(m)
        size = ring.shape[1] // len(found)
        return [
            pltpu.make_async_copy(
                ref, ring.at[m % slots, pl.ds(i * size, size)], sem.at[m, i]
            )
            for i, ref in enumerate(found)
        ]

    for m in range(slots):
        for copy in copies(m):
            copy.start()
    for m in range(count):
        named = jnp.concatenate(
            [one_hot(meta_ref[m, 0, e : e + 1], capacity) for e in range(begin, begin + experts)], axis=0
        )
        for copy in copies(m):
            copy.wait()
        result = dot_nn(named.astype(BF16), ring[m % slots])
        if weigh:
            weights = jnp.concatenate(
                [
                    jnp.broadcast_to(meta_ref[m, 1, e : e + 1], (capacity, named.shape[1]))
                    for e in range(begin, begin + experts)
                ],
                axis=0,
            )
            result = result * jnp.sum(jnp.where(named, weights, 0.0), axis=1, keepdims=True)
        low = result.astype(BF16)
        for e in range(experts):
            picked[e, m * capacity : (m + 1) * capacity] = low[e * capacity : (e + 1) * capacity]
        if m + slots < count:
            for copy in copies(m + slots):
                copy.start()


def expert_grad_hidden(place, gathered, meta, expert_down, capacity, begin, end):
    _, hidden, width = expert_down.shape
    experts = end - begin
    count = meta.shape[0]
    tokens = meta.shape[-1]
    rows = count * capacity

    def body(place_ref, meta_ref, w_ref, rows_ref, *rest):
        out_ref, ring, picked, sem = rest[-4:]
        expert = pl.program_id(0)

        @pl.when(expert == 0)
        def _():
            pick_rows(
                lambda m: [rows_ref.at[place_ref[1] ^ m]],
                meta_ref, ring, sem, picked, capacity, True, begin,
            )

        out_ref[0] = dot_nt(picked[expert], w_ref[0]).astype(BF16)

    return kernel_call(
        body,
        "expert_grad_hidden",
        (experts,),
        [
            whole_block(meta.shape),
            pl.BlockSpec((1, hidden, width), lambda e, s: (e + begin, 0, 0)),
            ANYWHERE,
        ],
        pl.BlockSpec((1, rows, hidden), lambda e, s: (e, 0, 0)),
        shape_of((experts, rows, hidden), BF16),
        scratch=[
            pltpu.VMEM((4, tokens, width), BF16),
            pltpu.VMEM((experts, rows, width), BF16),
            pltpu.SemaphoreType.DMA((count, 1)),
        ],
        prefetch=1,
        flops=2 * experts * rows * (hidden + tokens) * width,
        moved=2 * experts * hidden * width + 2 * count * tokens * width,
    )(place, meta, expert_down, gathered)


def combine_rows(meta_ref, picked, m, capacity):
    experts, _, width = picked.shape
    named = jnp.concatenate(
        [one_hot(meta_ref[m, 0, e : e + 1], capacity) for e in range(experts)], axis=0
    )
    named = jnp.where(named, 1.0, 0.0).T.astype(BF16)
    held = jnp.concatenate(
        [picked[e, m * capacity : (m + 1) * capacity] for e in range(experts)], axis=0
    )
    return dot_nn(named, held)


def send_combined(meta_ref, picked, ring, sem, capacity, targets):
    count = meta_ref.shape[0]
    tokens = ring.shape[1]
    slots = ring.shape[0]
    waiting = {}
    for i, m in enumerate(reversed(range(count))):
        for copy in waiting.pop(i - slots, []):
            copy.wait()
        ring[i % slots] = combine_rows(meta_ref, picked, m, capacity).astype(BF16)
        found = targets(m)
        size = tokens // len(found)
        waiting[i] = [
            pltpu.make_async_copy(
                ring.at[i % slots, pl.ds(b * size, size)], ref, sem.at[i % slots, b]
            )
            for b, ref in enumerate(found)
        ]
        for copy in waiting[i]:
            copy.start()
    for copies in waiting.values():
        for copy in copies:
            copy.wait()


def expert_middle(
    place, gathered, meta, expert_gate, expert_up, grad_hidden, capacity, groups, paired
):
    experts, width, hidden = expert_gate.shape
    count = meta.shape[0]
    tokens = meta.shape[-1]
    rows = count * capacity
    chunk = 256 if rows % 256 == 0 else rows
    numbers = [len(found) for found in gathered]
    arrays = [array for found in gathered for array in found]
    even = [m for m in range(count) if m % 2 == 0]

    def body(place_ref, meta_ref, gate_ref, up_ref, gh_ref, *rest):
        refs, (h_ref, *outs) = rest[: len(arrays)], rest[len(arrays) : -5]
        ring, picked, made, sem, out_sem = rest[-5:]
        expert = pl.program_id(0)

        @pl.when(expert == 0)
        def _():
            pick_rows(
                lambda m: refs[sum(numbers[:m]) : sum(numbers[: m + 1])],
                meta_ref, ring, sem, picked, capacity, False,
            )

        for c in range(rows // chunk):
            at = slice(c * chunk, (c + 1) * chunk)
            x = picked[expert, at]
            gate = dot_nn(x, gate_ref[0])
            up = dot_nn(x, up_ref[0])
            sigma = sigmoid(gate)
            value = gate * sigma
            grad = gh_ref[0, at].astype(F32)
            h_ref[0, at] = (value * up).astype(BF16)
            grad_gate = (grad * up * (sigma + value * (1.0 - sigma))).astype(BF16)
            grad_up = (grad * value).astype(BF16)
            made[expert, at] = (
                dot_nt(grad_gate, gate_ref[0]) + dot_nt(grad_up, up_ref[0])
            ).astype(BF16)

        @pl.when(expert == experts - 1)
        def _():
            def targets(m):
                if not paired:
                    return [outs[0].at[place_ref[1] ^ m]]
                if m % 2:
                    return [outs[-1].at[m // 2]]
                return outs[m // 2 * groups : (m // 2 + 1) * groups]

            send_combined(meta_ref, made, ring, out_sem, capacity, targets)

    if paired:
        shapes = [shape_of((tokens // groups, width), BF16)] * (len(even) * groups)
        shapes.append(shape_of((count // 2, tokens, width), BF16))
    else:
        shapes = [shape_of((count, tokens, width), BF16)]
    result = kernel_call(
        body,
        "expert_middle",
        (experts,),
        [
            whole_block(meta.shape),
            pl.BlockSpec((1, width, hidden), lambda e, s: (e, 0, 0)),
            pl.BlockSpec((1, width, hidden), lambda e, s: (e, 0, 0)),
            pl.BlockSpec((1, rows, hidden), lambda e, s: (e, 0, 0)),
        ]
        + [ANYWHERE] * len(arrays),
        [pl.BlockSpec((1, rows, hidden), lambda e, s: (e, 0, 0))] + [ANYWHERE] * len(shapes),
        [shape_of((experts, rows, hidden), BF16)] + shapes,
        scratch=[
            pltpu.VMEM((2, tokens, width), BF16),
            pltpu.VMEM((experts, rows, width), BF16),
            pltpu.VMEM((experts, rows, width), BF16),
            pltpu.SemaphoreType.DMA((count, max(numbers))),
            pltpu.SemaphoreType.DMA((2, groups)),
        ],
        prefetch=1,
        flops=2 * experts * rows * (4 * hidden + tokens) * width,
        moved=4 * experts * hidden * width + 4 * experts * rows * width,
    )(place, meta, expert_gate, expert_up, grad_hidden, *arrays)
    if not paired:
        return result[0], result[1], None
    near = {m: result[1 + i * groups : 1 + (i + 1) * groups] for i, m in enumerate(even)}
    return result[0], near, result[-1]


def expert_produce(place, hidden_rows, meta, expert_down, capacity, first, last, before=None):
    experts, hidden, width = expert_down.shape
    count = meta.shape[0]
    tokens = meta.shape[-1]
    rows = count * capacity
    held = before.shape[0] if before is not None else 0

    def body(place_ref, meta_ref, h_ref, w_ref, *rest):
        expert = pl.program_id(0) + first
        result = dot_nn(h_ref[0], w_ref[0])
        if held:
            before_ref, out_ref, ring, made, sem, before_sem = rest
            copy = pltpu.make_async_copy(before_ref, made.at[pl.ds(0, held)], before_sem)

            @pl.when(expert == first)
            def _():
                copy.start()

        else:
            (out_ref,) = rest
        for m in range(count):
            named = one_hot(meta_ref[m, 0, pl.ds(expert, 1)], capacity)
            weight = jnp.sum(
                jnp.where(named, meta_ref[m, 1, pl.ds(expert, 1)], 0.0), axis=1, keepdims=True
            )
            at = slice(m * capacity, (m + 1) * capacity)
            value = (weight * result[at]).astype(BF16)
            if held:
                made[expert, at] = value
            else:
                out_ref[0, at] = value

        if held:

            @pl.when(expert == last - 1)
            def _():
                copy.wait()
                send_combined(
                    meta_ref, made, ring, sem, capacity, lambda m: [out_ref.at[place_ref[1] ^ m]]
                )

    out_spec, shape = ANYWHERE, shape_of((count, tokens, width), BF16)
    if not held:
        out_spec = pl.BlockSpec((1, rows, width), lambda e, s: (e, 0, 0))
        shape = shape_of((last - first, rows, width), BF16)
    return kernel_call(
        body,
        "expert_produce",
        (last - first,),
        [
            whole_block(meta.shape),
            pl.BlockSpec((1, rows, hidden), lambda e, s: (e + first, 0, 0)),
            pl.BlockSpec((1, hidden, width), lambda e, s: (e + first, 0, 0)),
        ]
        + ([ANYWHERE] if held else []),
        out_spec,
        shape,
        scratch=[
            pltpu.VMEM((2, tokens, width), BF16),
            pltpu.VMEM((experts, rows, width), BF16),
            pltpu.SemaphoreType.DMA((2, 1)),
            pltpu.SemaphoreType.DMA,
        ]
        if held
        else [],
        prefetch=1,
        flops=2 * (last - first) * rows * hidden * width,
        moved=2 * experts * hidden * width + 2 * experts * rows * width,
    )(place, meta, hidden_rows, expert_down, *([before] if held else []))


def project_out_back(pieces, mixed, upstream, gain, w_out, down, up, attended, mids):
    splits, groups, shard, part = attended.shape
    width = splits * part
    rank = down.shape[1]
    rows = groups * shard
    number = len(pieces[0])

    def body(up_stream_ref, gain_ref, w_ref, down_ref, up_ref, mixed_ref, att_ref, mid_ref, *rest):
        refs, rest = rest[: groups * number], rest[groups * number :]
        gm_ref, gdown_ref, gup_ref, out_ref, low, held, sem = rest
        copies = [
            pltpu.make_async_copy(w_ref.at[pl.ds(z * part, part)], held.at[z], sem.at[z])
            for z in range(splits)
        ]
        for copy in copies:
            copy.start()
        smalls = []
        for g in range(groups):
            total = refs[g * number][...].astype(F32)
            for ref in refs[g * number + 1 : (g + 1) * number]:
                total += ref[...].astype(F32)
            grad = up_stream_ref[g].astype(F32) + norm_back(mixed_ref[g], gain_ref[...], total)
            gm_ref[g] = grad
            grad = grad.astype(BF16)
            low[g * shard : (g + 1) * shard] = grad
            small = (ADAPTER_SCALE * dot_nt(up_ref[g], grad)).astype(BF16)
            smalls.append(small)
            gup_ref[g] = (ADAPTER_SCALE * dot_nn(mid_ref[g], grad)).astype(BF16)
        for z in range(splits):
            columns = slice(z * part, (z + 1) * part)
            copies[z].wait()
            result = dot_nt(low[...], held[z])
            for g in range(groups):
                out_ref[z, g] = (
                    result[g * shard : (g + 1) * shard] + dot_tn(smalls[g], down_ref[g, :, columns])
                ).astype(BF16)
                gdown_ref[g, :, columns] = dot_nn(smalls[g], att_ref[z, g]).astype(BF16)

    return kernel_call(
        body,
        "project_out_back",
        (1,),
        [
            whole_block(upstream.shape),
            whole_block((1, width)),
            ANYWHERE,
            whole_block(down.shape),
            whole_block(up.shape),
            whole_block(mixed.shape),
            whole_block(attended.shape),
            whole_block(mids.shape),
        ]
        + [whole_block((shard, width))] * (groups * number),
        [
            whole_block((groups, shard, width)),
            whole_block((groups, rank, width)),
            whole_block((groups, rank, width)),
            whole_block(attended.shape),
        ],
        [
            shape_of((groups, shard, width), F32),
            shape_of((groups, rank, width), BF16),
            shape_of((groups, rank, width), BF16),
            shape_of(attended.shape, BF16),
        ],
        scratch=[
            pltpu.VMEM((rows, width), BF16),
            pltpu.VMEM((splits, part, width), BF16),
            pltpu.SemaphoreType.DMA((splits,)),
        ],
        flops=2 * rows * width * width,
        moved=2 * width * width,
    )(
        upstream, gain, w_out, down, up, mixed, attended, mids,
        *[array for found in pieces for array in found],
    )


def adapter_grads(place, group, grads, normed, ups, devices):
    listed = is_list(grads)
    splits, (_, shard, part) = piece_shape(grads)
    width = splits * part
    own = ups.shape[1]
    rank = own // 3
    slice_width = width // devices

    def body(place_ref, normed_ref, up_ref, *rest):
        refs, (small_ref, down_ref, low) = rest[:splits], rest[splits:]
        for which in range(3):
            for r in range(splits):
                owner = lax.rem(place_ref[0] + r, splits) if listed else r
                low[:, pl.ds(pl.multiple_of(owner * part, part), part)] = refs[r][which]
            at = slice(which * rank, (which + 1) * rank)
            small = (ADAPTER_SCALE * dot_nt(up_ref[at], low[...])).astype(BF16)
            small_ref[at] = small
            result = dot_nn(small, normed_ref[...]).astype(BF16)
            for e in range(devices):
                down_ref[e, at] = result[:, e * slice_width : (e + 1) * slice_width]

    return kernel_call(
        body,
        "adapter_grads",
        (1,),
        [
            pl.BlockSpec((shard, width), lambda i, s: (group, 0)),
            group_block(ups.shape, group),
        ]
        + piece_specs(grads, (3, shard, part), lambda i, s: (0, 0, 0)),
        [whole_block((own, shard)), whole_block((devices, own, slice_width))],
        [shape_of((own, shard), BF16), shape_of((devices, own, slice_width), BF16)],
        scratch=[pltpu.VMEM((shard, width), BF16)],
        prefetch=1,
        flops=12 * shard * rank * width,
        moved=6 * shard * width,
    )(place, normed, ups, *piece_arrays(grads, splits))


def project_first_back(place, grads, smalls, downs, w_qkv, tokens, gain, grad_mixed):
    groups = len(grads)
    listed = [is_list(pieces) for pieces in grads]
    splits, (_, shard, part) = piece_shape(grads[0])
    width = splits * part
    rows = groups * shard

    rank = downs.shape[1] // 3

    def body(place_ref, down_ref, w_ref, tok_ref, gain_ref, mixed_ref, *rest):
        small_refs, refs = rest[:groups], rest[groups : groups + groups * splits]
        out_ref, low, total, held, sem = rest[groups + groups * splits :]
        which = pl.program_id(0)

        def copy(p):
            return pltpu.make_async_copy(w_ref.at[p], held.at[p], sem.at[p])

        @pl.when(which == 0)
        def _():
            for p in range(3):
                copy(p).start()

        for g in range(groups):
            for r in range(splits):
                owner = lax.rem(place_ref[0] + r, splits) if listed[g] else r
                low[
                    g * shard : (g + 1) * shard, pl.ds(pl.multiple_of(owner * part, part), part)
                ] = refs[g * splits + r][0]
        at = pl.ds(pl.multiple_of(which * rank, rank), rank)
        small = jnp.concatenate(
            [dot_tn(small_refs[g][at], down_ref[g, at]) for g in range(groups)], axis=0
        )
        copy(which).wait()
        result = dot_nt(low[...], held[which]) + small

        @pl.when(which == 0)
        def _():
            total[...] = result

        @pl.when(which == 1)
        def _():
            total[...] += result

        @pl.when(which == 2)
        def _():
            back = norm_back(tok_ref[...].astype(F32), gain_ref[...], total[...] + result)
            for g in range(groups):
                out_ref[g] = mixed_ref[g] + back[g * shard : (g + 1) * shard]

    return kernel_call(
        body,
        "project_first_back",
        (3,),
        [
            whole_block(downs.shape),
            ANYWHERE,
            whole_block((rows, width)),
            whole_block((1, width)),
            whole_block(grad_mixed.shape),
        ]
        + [whole_block((3 * rank, shard))] * groups
        + [
            spec
            for pieces in grads
            for spec in piece_specs(pieces, (1, shard, part), lambda p, s: (p, 0, 0))
        ],
        whole_block((groups, shard, width)),
        shape_of((groups, shard, width), F32),
        scratch=[
            pltpu.VMEM((rows, width), BF16),
            pltpu.VMEM((rows, width), F32),
            pltpu.VMEM((3, width, width), BF16),
            pltpu.SemaphoreType.DMA((3,)),
        ],
        prefetch=1,
        flops=6 * rows * width * width,
        moved=6 * width * width,
    )(
        place, downs, w_qkv, tokens, gain, grad_mixed, *smalls,
        *[piece for pieces in grads for piece in piece_arrays(pieces, splits)],
    )


def local(
    tokens,
    cotangent,
    lengths,
    adapter_choice,
    expert_ids,
    gate_weights,
    attn_gain,
    moe_gain,
    query_gain,
    key_gain,
    w_qkv,
    w_out,
    expert_gate,
    expert_up,
    expert_down,
    adapt_down,
    first_down,
    second_down,
    adapt_up,
    first_up,
    second_up,
):
    groups, shard, width = tokens.shape
    splits = lax.axis_size("seq")
    devices = lax.axis_size("exp")
    here = lax.axis_index("seq")
    total = shard * splits
    part = width // splits
    rows = groups * shard
    sets, projections, slice_width, rank = adapt_down.shape
    local_experts = expert_gate.shape[0]
    experts = local_experts * devices
    top = expert_ids.shape[-1]
    capacity = 3 * rows * top // (2 * experts)
    listed = [False] * groups

    position = lax.axis_index("exp")
    place = jnp.stack([here, position]).astype(jnp.int32)
    flat_tokens = tokens.reshape(rows, width)
    gain_row = attn_gain.reshape(1, width)
    moe_row = moe_gain.reshape(1, width)
    query_row = query_gain.reshape(1, HEAD)
    key_row = key_gain.reshape(1, HEAD)

    own_positions = here * shard + jnp.arange(shard, dtype=jnp.int32)
    own_live = own_positions[None, :] < lengths[:, None]
    upstream = jnp.where(own_live[:, :, None], cotangent, jnp.zeros((), BF16))
    ids = expert_ids.reshape(rows, top).T
    gates = gate_weights.reshape(rows, top).T
    choice = adapter_choice.astype(F32).reshape(1, groups * sets)
    choice = jnp.pad(choice, ((0, 0), (0, rows - groups * sets)))
    routed = route(ids, gates, choice, experts)
    down_rows = jnp.swapaxes(adapt_down.astype(BF16), 2, 3)
    adapter_rows = jnp.concatenate(
        [
            down_rows[:, :3].reshape(-1, slice_width),
            down_rows[:, 3].reshape(-1, slice_width),
            adapt_up[:, :3].astype(BF16).reshape(-1, slice_width),
            adapt_up[:, 3].astype(BF16).reshape(-1, slice_width),
            routed.reshape(-1, slice_width),
        ]
    )
    all_adapters = lax.all_gather(adapter_rows, "exp")

    base, _, normed = project_first(
        place, after(flat_tokens, adapter_rows), gain_row, w_qkv, groups, splits, listed
    )
    raw = [forward_seq(base[0])]
    cot_rows = lax.all_gather(after(upstream, normed).reshape(rows, width), "exp")

    own = 3 * rank
    chosen = jnp.sum(adapter_choice * jnp.arange(sets, dtype=jnp.int32)[None, :], axis=1)
    sections = [
        (0, own), (sets * own, rank), (sets * (own + rank), own), (sets * (2 * own + rank), rank),
    ]
    downs, out_downs, ups, out_ups, mids = pick_sets(
        all_adapters, chosen, groups, sets, sections, normed
    )
    all_mids = by_distance(jnp.stack(forward_seq([mids] * splits)))
    raw[0], all_mids = lax.optimization_barrier((raw[0], all_mids))
    for g in range(1, groups):
        raw.append(forward_seq(after(base[g], raw[g - 1])))
    gathered = after(all_adapters, raw[0])[:, 2 * sets * projections * rank :]
    gathered = gathered.reshape(devices, 3 * experts + 16, rows)
    choices = gathered[:, 3 * experts, : groups * sets].reshape(devices, groups, sets)
    meta = gathered[:, : 3 * experts].reshape(devices, 3, experts, rows)
    meta = lax.dynamic_slice_in_dim(meta, position * local_experts, local_experts, axis=2)
    meta = meta.astype(F32)
    meta = by_relative(jnp.stack([meta[:, 0], meta[:, 1] + meta[:, 2]], axis=1))
    own_ups = lax.dynamic_slice_in_dim(ups, here * part, part, axis=2)
    own_ups = own_ups.reshape(groups, 3, rank, part)

    blocks = jnp.arange(splits, dtype=jnp.int32)
    frequency = ROPE_BASE ** (-(2.0 / HEAD) * jnp.arange(HEAD // 2, dtype=F32))
    tables = []
    for g in range(groups):
        positions = blocks[:, None] * shard + jnp.arange(shard, dtype=jnp.int32)[None, :]
        angles = after(positions, raw[0]).reshape(total, 1).astype(F32) * frequency[None, :]
        cosine, sine = jnp.cos(angles), jnp.sin(angles)
        tables.append(
            (
                positions.reshape(1, total),
                jnp.concatenate([cosine, cosine], axis=1),
                jnp.concatenate([-sine, sine], axis=1),
            )
        )

    saved, heads_rows = [], []
    for g in range(groups):
        if g:
            raw[g] = after(raw[g], heads_rows)
        att, kept = attend(
            lengths[g : g + 1],
            raw[g],
            all_mids[:, g],
            own_ups[g],
            query_row,
            key_row,
            *tables[g],
        )
        saved.append(kept)
        heads_rows.append(att)
    heads_rows = jnp.stack(heads_rows, axis=1)
    attended = lax.all_to_all(heads_rows, "seq", 0, 0)
    grad_hidden = expert_grad_hidden(
        place, cot_rows, after(meta, heads_rows), expert_down, capacity, 0, local_experts
    )
    attended, grad_hidden = lax.optimization_barrier((attended, grad_hidden))
    mixed, mid_out, moe_rows = project_out(
        attended, w_out, out_downs, out_ups, tokens, moe_row
    )
    gathered = gather_rows(moe_rows)
    half = local_experts // 2

    paired = devices == 8 and groups == 2
    hidden, parts, others = expert_middle(
        place,
        gathered,
        meta,
        expert_gate,
        expert_up,
        grad_hidden,
        capacity,
        groups,
        paired,
    )
    if paired:
        beside = swap(others, 1).reshape(devices // 2, groups, shard, width)
        far_sums = [add_low(parts[6][g], beside[3][g]) for g in range(groups)]
        near_sums = [add_low(parts[WAYS[g][0]][g], beside[WAYS[g][0] // 2][g]) for g in range(groups)]
        far_sums, near_sums = lax.optimization_barrier((far_sums, near_sums))
        far = [swap(far_sums[g], WAYS[g][0]) for g in range(groups)]
        near = [swap(near_sums[g], WAYS[g][0]) for g in range(groups)]
        produced = expert_produce(
            place, after(hidden, far_sums), meta, expert_down, capacity, 0, half
        )
        far, produced = lax.optimization_barrier((far, produced))
        joined_sums = [
            add_low(parts[WAYS[g][1]][g], beside[WAYS[g][1] // 2][g], far[g]) for g in range(groups)
        ]
        joined = [swap(joined_sums[g], WAYS[g][1]) for g in range(groups)]
        grad_pieces = [
            [parts[0][g], beside[0][g], near[g], joined[g]] for g in range(groups)
        ]
    else:
        summed = lax.psum_scatter(parts, "exp").reshape(groups, shard, width)
        grad_pieces = [[summed[g]] for g in range(groups)]
        produced = expert_produce(place, hidden, meta, expert_down, capacity, 0, half)
    grad_mixed, grad_out_downs, grad_out_ups, grad_att = project_out_back(
        grad_pieces, mixed, upstream, moe_row, w_out, out_downs, out_ups, attended, mid_out
    )
    out_parts = expert_produce(
        place, hidden, after(meta, grad_mixed), expert_down, capacity, half, local_experts, produced
    )
    grad_att = lax.all_to_all(grad_att, "seq", 0, 0)
    grad_raw, gups = [], []
    for g in range(groups):
        if g:
            grad_att = after(grad_att, gups)
        back, gup = attend_back(
            lengths[g : g + 1],
            grad_att,
            g,
            saved[g],
            all_mids[:, g],
            rank,
            query_row,
            key_row,
            *tables[g],
        )
        gups.append(gup)
        if not g:
            out_sum = lax.psum_scatter(after(out_parts, gup), "exp")
        grad_raw.append(forward_seq(after(back, grad_raw) if g else back))
    out_sum = out_sum.reshape(groups, shard, width)

    gups = jnp.stack(after(gups, grad_raw[0]))
    wide_ups = lax.dynamic_update_slice_in_dim(
        jnp.zeros((groups, own, width), BF16), gups, here * part, axis=2
    )
    early = jnp.concatenate([grad_out_downs, wide_ups, grad_out_ups], axis=1)
    early = jnp.moveaxis(early.reshape(groups, -1, devices, slice_width), 2, 0)
    output = (mixed + after(out_sum, gups).astype(F32)).astype(BF16)

    smalls, late = [], []
    for g in range(groups):
        small, down = adapter_grads(place, g, grad_raw[g], normed, ups, devices)
        smalls.append(small)
        late.append(down)
    late = jnp.concatenate([jnp.stack(late, axis=1), early], axis=2)
    late = lax.all_to_all(late, "exp", 0, 0)
    grad_input = project_first_back(
        place, grad_raw, smalls, downs, w_qkv, after(flat_tokens, output), gain_row, grad_mixed
    )
    late = after(late, grad_input)
    pieces = jnp.einsum("dgk,dgrw->krw", choices, late, preferred_element_type=F32)
    pieces = pieces.astype(BF16)
    pieces = pieces.reshape(splits, -1, slice_width)
    order = (here + jnp.arange(splits)) % splits
    pieces = list(jnp.take(pieces, order, axis=0))
    summed = add_low(*forward_seq(pieces))
    in_sets = by_distance(jnp.stack(forward_seq([summed] * splits)))
    in_sets = in_sets.reshape(sets, 2, projections, rank, slice_width).astype(F32)
    shard_down = jnp.swapaxes(in_sets[:, 0], 2, 3)
    shard_up = in_sets[:, 1]
    new_first_down, new_second_down, new_down = adam_update(
        adapt_down, shard_down, first_down, second_down, RATE_DOWN
    )
    new_first_up, new_second_up, new_up = adam_update(
        adapt_up, shard_up, first_up, second_up, RATE_UP
    )
    return (
        output,
        grad_input,
        new_first_down,
        new_second_down,
        new_down,
        new_first_up,
        new_second_up,
        new_up,
    )


def solution(mesh):
    in_specs = (
        P("exp", "seq", None),
        P("exp", "seq", None),
        P("exp"),
        P("exp", None),
        P("exp", "seq", None, None, None),
        P("exp", "seq", None, None, None),
        P(),
        P(),
        P(),
        P(),
        P(),
        P(),
        P("exp", None, None),
        P("exp", None, None),
        P("exp", None, None),
        P(None, None, "exp", None),
        P(None, None, "exp", None),
        P(None, None, "exp", None),
        P(None, None, None, "exp"),
        P(None, None, None, "exp"),
        P(None, None, None, "exp"),
    )
    out_specs = (
        P("exp", "seq", None),
        P("exp", "seq", None),
        P(None, None, "exp", None),
        P(None, None, "exp", None),
        P(None, None, "exp", None),
        P(None, None, None, "exp"),
        P(None, None, None, "exp"),
        P(None, None, None, "exp"),
    )
    return jax.shard_map(local, mesh=mesh, in_specs=in_specs, out_specs=out_specs, check_vma=False)
```

```python
import functools

import jax
import jax.numpy as jnp
from jax import lax
from jax.experimental import pallas as pl
from jax.experimental.pallas import tpu as pltpu
from jax.sharding import PartitionSpec as P

HEAD = 128
STEP = 5

NORM_EPS = 1e-05
ROPE_BASE = 50000.0
ADAPTER_SCALE = 0.5
BETA_FIRST = 0.5
BETA_SECOND = 0.5
RATE_DOWN = 0.02
RATE_UP = 0.2
WEIGHT_DECAY = 0.01
ADAM_EPS = 1e-08
MASKED = -1e30
SCORE_SCALE = HEAD ** (-0.5)

F32 = jnp.float32
BF16 = jnp.bfloat16
VMEM_LIMIT = 62 * 1024 * 1024
COST_SHARE = 0.01


def dot_nn(a, b):
    return lax.dot_general(a, b, (((1,), (0,)), ((), ())), preferred_element_type=F32)


def dot_nt(a, b):
    return lax.dot_general(a, b, (((1,), (1,)), ((), ())), preferred_element_type=F32)


def dot_tn(a, b):
    return lax.dot_general(a, b, (((0,), (0,)), ((), ())), preferred_element_type=F32)


def inverse_rms(values):
    return lax.rsqrt(jnp.mean(values * values, axis=-1, keepdims=True) + NORM_EPS)


def norm_back(values, gain, upstream):
    inverse = inverse_rms(values)
    scaled = upstream * gain
    return inverse * scaled - values * (inverse * inverse * inverse) * jnp.mean(
        values * scaled, axis=-1, keepdims=True
    )


def sigmoid(values):
    return 0.5 + 0.5 * jnp.tanh(0.5 * values)


def adam_update(weight, gradient, first, second, step_rate):
    new_first = BETA_FIRST * first + (1.0 - BETA_FIRST) * gradient
    new_second = BETA_SECOND * second + (1.0 - BETA_SECOND) * gradient * gradient
    first_hat = new_first / (1.0 - BETA_FIRST**STEP)
    second_hat = new_second / (1.0 - BETA_SECOND**STEP)
    new_weight = weight - step_rate * (
        first_hat / (jnp.sqrt(second_hat) + ADAM_EPS) + WEIGHT_DECAY * weight
    )
    return (new_first, new_second, new_weight)


def shape_of(shape, dtype):
    return jax.ShapeDtypeStruct(shape, dtype)


def whole_block(shape):
    rank = len(shape)
    return pl.BlockSpec(tuple(shape), lambda *_: (0,) * rank)


def kernel_call(
    body, name, grid, in_specs, out_specs, out_shape, scratch=(), prefetch=0, flops=0, moved=0,
    aliases=None,
):
    return pl.pallas_call(
        body,
        grid_spec=pltpu.PrefetchScalarGridSpec(
            num_scalar_prefetch=prefetch,
            grid=grid,
            in_specs=in_specs,
            out_specs=out_specs,
            scratch_shapes=list(scratch),
        ),
        out_shape=out_shape,
        input_output_aliases=aliases or {},
        name=name,
        cost_estimate=pl.CostEstimate(
            flops=int(flops * COST_SHARE), bytes_accessed=int(moved * COST_SHARE), transcendentals=0
        ),
        compiler_params=pltpu.CompilerParams(vmem_limit_bytes=VMEM_LIMIT),
    )


def swap(values, mask):
    count = lax.axis_size("exp")
    return lax.ppermute(values, "exp", [(i, i ^ mask) for i in range(count)])


def shift(values, distance):
    count = lax.axis_size("seq")
    return lax.ppermute(values, "seq", [(i, (i + distance) % count) for i in range(count)])


def shift_order():
    count = lax.axis_size("seq")
    return sorted(range(1, count), key=lambda r: -min(r, count - r))


def forward_seq(pieces):
    if not isinstance(pieces, (list, tuple)):
        return lax.all_to_all(pieces, "seq", 0, 0)
    came = {r: shift(pieces[r], r) for r in shift_order()}
    return [pieces[0]] + [came[r] for r in range(1, len(pieces))]


def backward_seq(pieces):
    if not isinstance(pieces, (list, tuple)):
        return lax.all_to_all(pieces, "seq", 0, 0)
    came = {r: shift(pieces[r], -r) for r in shift_order()}
    return [pieces[0]] + [came[r] for r in range(1, len(pieces))]


def tell_all(values, axis):
    count = lax.axis_size(axis)
    return lax.all_to_all(jnp.broadcast_to(values[None], (count,) + values.shape), axis, 0, 0)


def by_distance(stacked):
    count = lax.axis_size("seq")
    order = (lax.axis_index("seq") - jnp.arange(count)) % count
    return jnp.take(stacked, order, axis=0)


def by_relative(stacked):
    count = lax.axis_size("exp")
    return jnp.take(stacked, lax.axis_index("exp") ^ jnp.arange(count), axis=0)


STEP_HEADS = 1

WAYS = ((2, 4), (4, 2))


def gather_near(rows):
    near = {2: [None] * len(rows), 4: [None] * len(rows)}
    for g, (first, _) in enumerate(WAYS):
        near[first][g] = swap(rows[g], first)
    for g, (_, second) in enumerate(WAYS):
        near[second][g] = swap(rows[g], second)
    return near


def far_of(near):
    return [swap(near[first][g], second) for g, (first, second) in enumerate(WAYS)]


def gather_far(rows, near, far=None):
    far = far or far_of(near)
    found = []
    for blocks in (rows, near[2], near[4], far):
        found += [list(blocks), [swap(block, 1) for block in blocks]]
    return found


def gather_whole(rows):
    everything = by_relative(lax.all_gather(jnp.concatenate(rows), "exp"))
    return [[block] for block in everything]


def near_sums_of(parts, others):
    groups = len(parts[0])
    beside = swap(others, 1).reshape((4, groups) + parts[0][0].shape)
    far = [add_low(parts[6][g], beside[3][g]) for g in range(groups)]
    near = [add_low(parts[WAYS[g][0]][g], beside[WAYS[g][0] // 2][g]) for g in range(groups)]
    return lax.optimization_barrier((far, near)) + (beside,)


def send_near(far, near):
    far = [swap(far[g], WAYS[g][0]) for g in range(len(far))]
    return far, [swap(near[g], WAYS[g][0]) for g in range(len(near))]


def joined_sums_of(parts, beside, far):
    return [
        add_low(parts[WAYS[g][1]][g], beside[WAYS[g][1] // 2][g], far[g]) for g in range(len(far))
    ]


def send_joined(joined):
    return [swap(joined[g], WAYS[g][1]) for g in range(len(joined))]


def add_low(*values):
    return functools.reduce(jnp.add, [value.astype(F32) for value in values]).astype(BF16)


def after(values, *first):
    return lax.optimization_barrier((values, first))[0]


ANYWHERE = pl.BlockSpec(memory_space=pl.ANY)


def group_block(shape, group):
    rank = len(shape) - 1
    return pl.BlockSpec((None,) + tuple(shape[1:]), lambda *_: (group,) + (0,) * rank)


def is_list(pieces):
    return isinstance(pieces, (list, tuple))


def piece_shape(pieces):
    if is_list(pieces):
        return len(pieces), pieces[0].shape
    return pieces.shape[0], pieces.shape[1:]


def piece_arrays(pieces, splits):
    return list(pieces) if is_list(pieces) else [pieces] * splits


def piece_specs(pieces, block, index):
    if is_list(pieces):
        return [pl.BlockSpec(block, index)] * len(pieces)
    return [
        pl.BlockSpec((None,) + tuple(block), lambda *at, r=r: (r,) + tuple(index(*at)))
        for r in range(pieces.shape[0])
    ]


def out_specs_of(listed, splits, block, index):
    if listed:
        return [pl.BlockSpec(block, index)] * splits
    return [pl.BlockSpec((splits,) + tuple(block), lambda *at: (0,) + tuple(index(*at)))]


def out_shapes_of(listed, splits, shape, dtype):
    if listed:
        return [shape_of(shape, dtype)] * splits
    return [shape_of((splits,) + tuple(shape), dtype)]


def out_refs_of(listed, refs):
    return list(refs) if listed else [refs[0].at[r] for r in range(refs[0].shape[0])]


def out_pieces_of(listed, results):
    return list(results) if listed else results[0]


def project_first(place, tokens, gain, w_qkv, groups, splits, listed):
    rows, width = tokens.shape
    part = width // splits
    shard = rows // groups
    counts = [splits if listed[g] else 1 for g in range(groups)]
    total = sum(counts)

    def body(place_ref, tok_ref, gain_ref, w_ref, *rest):
        outs = rest[:total]
        parts_ref, normed_ref, held, sem = rest[total:]
        which = pl.program_id(0)

        def owner(r):
            return lax.rem(place_ref[0] + r, splits)

        def copy(p, r):
            columns = pl.ds(pl.multiple_of(owner(r) * part, part), part)
            return pltpu.make_async_copy(
                w_ref.at[p, :, columns],
                held.at[p, :, pl.ds(r * part, part)],
                sem.at[p, r],
            )

        @pl.when(which == 0)
        def _():
            for p in range(3):
                for r in range(splits):
                    copy(p, r).start()
            values = tok_ref[...].astype(F32)
            low = (values * inverse_rms(values) * gain_ref[...]).astype(BF16)
            normed_ref[...] = low
            for z in range(splits):
                for g in range(groups):
                    parts_ref[z, g] = low[
                        g * shard : (g + 1) * shard, z * part : (z + 1) * part
                    ]

        for r in range(splits):
            copy(which, r).wait()
            result = dot_nn(normed_ref[...], held[which, :, r * part : (r + 1) * part])
            first = 0
            for g in range(groups):
                low = result[g * shard : (g + 1) * shard].astype(BF16)
                if listed[g]:
                    outs[first + r][0] = low
                else:
                    outs[first][owner(r), 0] = low
                first += counts[g]

    specs, shapes = [], []
    for g in range(groups):
        specs += out_specs_of(listed[g], splits, (1, shard, part), lambda p, s: (p, 0, 0))
        shapes += out_shapes_of(listed[g], splits, (3, shard, part), BF16)
    result = kernel_call(
        body,
        "project_first",
        (3,),
        [whole_block((rows, width)), whole_block((1, width)), ANYWHERE],
        specs + [whole_block((splits, groups, shard, part)), whole_block((rows, width))],
        shapes
        + [shape_of((splits, groups, shard, part), BF16), shape_of((rows, width), BF16)],
        scratch=[
            pltpu.VMEM((3, width, width), BF16),
            pltpu.SemaphoreType.DMA((3, splits)),
        ],
        prefetch=1,
        flops=6 * rows * width * width,
        moved=6 * width * width,
    )(place, tokens, gain, w_qkv)
    outs, first = [], 0
    for g in range(groups):
        outs.append(out_pieces_of(listed[g], result[first : first + counts[g]]))
        first += counts[g]
    return outs, result[total], result[total + 1]


def pick_sets(gathered, picks, groups, sections, normed):
    count = len(gathered)
    part = gathered[0].shape[1]
    width = count * part
    shard = normed.shape[0] // groups
    number = len(sections)

    def body(pick_ref, normed_ref, *rest):
        refs, outs, sem = rest[:count], rest[count:-1], rest[-1]
        copies = []
        for g in range(groups):
            for i, (first, own) in enumerate(sections):
                for m in range(count):
                    columns = pl.ds(pl.multiple_of((pick_ref[groups] ^ m) * part, part), part)
                    copies.append(
                        pltpu.make_async_copy(
                            refs[m].at[pl.ds(pl.multiple_of(first + pick_ref[g] * own, own), own)],
                            outs[i].at[g, :, columns],
                            sem.at[(g * number + i) * count + m],
                        )
                    )
        for copy in copies:
            copy.start()
        for copy in copies:
            copy.wait()
        for g in range(groups):
            outs[number][g] = dot_nt(
                outs[0][g], normed_ref[g * shard : (g + 1) * shard]
            ).astype(BF16)

    shapes = [(groups, own, width) for _, own in sections]
    shapes.append((groups, sections[0][1], shard))
    return kernel_call(
        body,
        "pick_sets",
        (1,),
        [whole_block(normed.shape)] + [ANYWHERE] * count,
        [whole_block(shape) for shape in shapes],
        [shape_of(shape, BF16) for shape in shapes],
        scratch=[pltpu.SemaphoreType.DMA((groups * number * count,))],
        prefetch=1,
        moved=4 * groups * width * sum(own for _, own in sections),
    )(picks, normed, *gathered)


def route(ids, gates, choice, experts):
    top, tokens = ids.shape

    def body(ids_ref, gates_ref, choice_ref, out_ref):
        expert = lax.broadcasted_iota(jnp.int32, (experts, tokens), 0)
        weights = jnp.zeros((experts, tokens), F32)
        named = jnp.zeros((experts, tokens), F32)
        for k in range(top):
            hit = expert == ids_ref[k : k + 1]
            weights = jnp.where(hit, gates_ref[k : k + 1], weights)
            named = jnp.where(hit, 1.0, named)
        earlier = lax.broadcasted_iota(jnp.int32, (tokens, tokens), 0) < lax.broadcasted_iota(
            jnp.int32, (tokens, tokens), 1
        )
        ranks = dot_nn(named.astype(BF16), jnp.where(earlier, 1.0, 0.0).astype(BF16))
        slots = jnp.where(named > 0.0, ranks, -1.0)
        front = weights.astype(BF16)
        out_ref[:experts] = slots.astype(BF16)
        out_ref[experts : 2 * experts] = front
        out_ref[2 * experts : 3 * experts] = (weights - front.astype(F32)).astype(BF16)
        out_ref[3 * experts :] = jnp.broadcast_to(choice_ref[...], (16, tokens)).astype(BF16)

    shape = (3 * experts + 16, tokens)
    return kernel_call(
        body,
        "route",
        (1,),
        [whole_block(ids.shape), whole_block(gates.shape), whole_block(choice.shape)],
        whole_block(shape),
        shape_of(shape, BF16),
        moved=12 * experts * tokens,
    )(ids, gates, choice)


def rotate(values, cosine, sine):
    return values * cosine + pltpu.roll(values, HEAD // 2, 1) * sine


def rotate_back(values, cosine, sine):
    return values * cosine - pltpu.roll(values, HEAD // 2, 1) * sine


def softmax_rows(queries, keys, live):
    scores = jnp.where(live, dot_nt(queries, keys) * SCORE_SCALE, MASKED)
    exponent = jnp.exp(scores - jnp.max(scores, axis=-1, keepdims=True))
    return exponent * (1.0 / jnp.sum(exponent, axis=-1, keepdims=True))


def attend(length, raw, mids, ups, query_gain, key_gain, positions, cosine, sine):
    listed = is_list(raw)
    splits, (_, shard, part) = piece_shape(raw)
    rank = ups.shape[1]
    total = splits * shard
    heads = part // HEAD
    step_heads = min(heads, STEP_HEADS)

    def body(len_ref, up_ref, qg_ref, kg_ref, pos_ref, cos_ref, sin_ref, *rest):
        raw_refs, mid_ref = rest[:splits], rest[splits]
        att_refs = out_refs_of(listed, rest[splits + 1 : -5])
        q_ref, k_ref, v_ref, rq_ref, rk_ref = rest[-5:]

        mids = [
            jnp.concatenate(
                [mid_ref[r, which * rank : (which + 1) * rank] for r in range(splits)], axis=1
            )
            for which in range(3)
        ]
        cosine, sine = cos_ref[...], sin_ref[...]
        for h in range(step_heads):
            at = slice(h * HEAD, (h + 1) * HEAD)

            def full(which):
                base = jnp.concatenate([ref[which, :, at] for ref in raw_refs], axis=0)
                added = dot_tn(mids[which], up_ref[which, :, at])
                return base.astype(F32) + ADAPTER_SCALE * added

            raw_q, raw_k, raw_v = full(0), full(1), full(2)
            rq_ref[h] = raw_q
            rk_ref[h] = raw_k
            queries = rotate(raw_q * inverse_rms(raw_q) * qg_ref[...], cosine, sine).astype(BF16)
            keys = rotate(raw_k * inverse_rms(raw_k) * kg_ref[...], cosine, sine).astype(BF16)
            values = raw_v.astype(BF16)
            q_ref[h] = queries
            k_ref[h] = keys
            v_ref[h] = values
            weights = softmax_rows(queries, keys, pos_ref[...] < len_ref[0]).astype(BF16)
            result = dot_nn(weights, values).astype(BF16)
            for r in range(splits):
                att_refs[r][:, at] = result[r * shard : (r + 1) * shard]

    wide = step_heads * HEAD
    head_block = pl.BlockSpec((step_heads, total, HEAD), lambda h, s: (h, 0, 0))
    result = kernel_call(
        body,
        "attend",
        (heads // step_heads,),
        [
            pl.BlockSpec((3, rank, wide), lambda h, s: (0, 0, h)),
            whole_block((1, HEAD)),
            whole_block((1, HEAD)),
            whole_block((1, total)),
            whole_block((total, HEAD)),
            whole_block((total, HEAD)),
        ]
        + piece_specs(raw, (3, shard, wide), lambda h, s: (0, 0, h))
        + [whole_block(mids.shape)],
        out_specs_of(listed, splits, (shard, wide), lambda h, s: (0, h)) + [head_block] * 5,
        out_shapes_of(listed, splits, (shard, part), BF16)
        + [shape_of((heads, total, HEAD), BF16)] * 3
        + [shape_of((heads, total, HEAD), F32)] * 2,
        prefetch=1,
        flops=4 * heads * total * total * HEAD,
        moved=heads * total * HEAD * 24 + 4 * heads * total * total,
    )(length, ups, query_gain, key_gain, positions, cosine, sine, *piece_arrays(raw, splits), mids)
    return out_pieces_of(listed, result[:-5]), result[-5:]


def attend_back(length, grads, group, saved, mids, rank, query_gain, key_gain, positions, cosine, sine):
    listed = False
    splits, _, shard, part = grads.shape
    total = splits * shard
    heads = part // HEAD
    step_heads = min(heads, STEP_HEADS)

    def body(len_ref, qg_ref, kg_ref, pos_ref, cos_ref, sin_ref, *rest):
        grad_refs, mid_ref = rest[:splits], rest[splits]
        q_ref, k_ref, v_ref, rq_ref, rk_ref = rest[splits + 1 : splits + 6]
        out_refs = out_refs_of(listed, rest[splits + 6 : -1])
        gup_ref = rest[-1]
        cosine, sine = cos_ref[...], sin_ref[...]
        mids = [
            jnp.concatenate(
                [mid_ref[r, which * rank : (which + 1) * rank] for r in range(splits)], axis=1
            )
            for which in range(3)
        ]
        for h in range(step_heads):
            at = slice(h * HEAD, (h + 1) * HEAD)
            queries, keys, values = q_ref[h], k_ref[h], v_ref[h]
            grad = jnp.concatenate([ref[:, at] for ref in grad_refs], axis=0)
            weights = softmax_rows(queries, keys, pos_ref[...] < len_ref[0])
            grad_probs = dot_nt(grad, values)
            inner = jnp.sum(weights * grad_probs, axis=-1, keepdims=True)
            grad_scores = (weights * (grad_probs - inner)).astype(BF16)
            grad_q = dot_nn(grad_scores, keys) * SCORE_SCALE
            grad_k = dot_tn(grad_scores, queries) * SCORE_SCALE
            grad_v = dot_tn(weights.astype(BF16), grad)
            grad_q = norm_back(rq_ref[h], qg_ref[...], rotate_back(grad_q, cosine, sine))
            grad_k = norm_back(rk_ref[h], kg_ref[...], rotate_back(grad_k, cosine, sine))
            for which, value in enumerate((grad_q, grad_k, grad_v)):
                low = value.astype(BF16)
                for r in range(splits):
                    out_refs[r][which, :, at] = low[r * shard : (r + 1) * shard]
                gup_ref[which * rank : (which + 1) * rank, at] = (
                    ADAPTER_SCALE * dot_nn(mids[which], low)
                ).astype(BF16)

    wide = step_heads * HEAD
    head_block = pl.BlockSpec((step_heads, total, HEAD), lambda h, s: (h, 0, 0))
    result = kernel_call(
        body,
        "attend_back",
        (heads // step_heads,),
        [
            whole_block((1, HEAD)),
            whole_block((1, HEAD)),
            whole_block((1, total)),
            whole_block((total, HEAD)),
            whole_block((total, HEAD)),
        ]
        + [
            pl.BlockSpec((None, None, shard, wide), lambda h, s, r=r: (r, group, 0, h))
            for r in range(splits)
        ]
        + [whole_block(mids.shape)]
        + [head_block] * 5,
        out_specs_of(listed, splits, (3, shard, wide), lambda h, s: (0, 0, h))
        + [pl.BlockSpec((3 * rank, wide), lambda h, s: (0, h))],
        out_shapes_of(listed, splits, (3, shard, part), BF16)
        + [shape_of((3 * rank, part), BF16)],
        prefetch=1,
        flops=10 * heads * total * total * HEAD,
        moved=heads * total * HEAD * 24 + 8 * heads * total * total,
    )(length, query_gain, key_gain, positions, cosine, sine, *[grads] * splits, mids, *saved)
    return out_pieces_of(listed, result[:-1]), result[-1]


def project_out(attended, w_out, down, up, tokens, gain):
    splits, groups, shard, part = attended.shape
    width = splits * part
    rank = down.shape[1]
    rows = groups * shard

    def body(att_ref, w_ref, down_ref, up_ref, tok_ref, gain_ref, *rest):
        mixed_ref, mid_ref = rest[:2]
        moe_refs = rest[2 : 2 + groups]
        att, held, sem = rest[2 + groups :]
        copies = [
            pltpu.make_async_copy(
                w_ref.at[pl.ds(i * part, part)], held.at[pl.ds(i * part, part)], sem.at[i]
            )
            for i in range(splits)
        ]
        for copy in copies:
            copy.start()
        adapter = []
        for g in range(groups):
            at = slice(g * shard, (g + 1) * shard)
            for z in range(splits):
                att[at, z * part : (z + 1) * part] = att_ref[z, g]
            mid = dot_nt(down_ref[g], att[at]).astype(BF16)
            mid_ref[g] = mid
            adapter.append(
                tok_ref[g].astype(F32) + ADAPTER_SCALE * dot_tn(mid, up_ref[g])
            )
        total = jnp.concatenate(adapter, axis=0)
        for i, copy in enumerate(copies):
            copy.wait()
            total += dot_nn(att[:, i * part : (i + 1) * part], held[i * part : (i + 1) * part])
        low = (total * inverse_rms(total) * gain_ref[...]).astype(BF16)
        for g in range(groups):
            mixed_ref[g] = total[g * shard : (g + 1) * shard]
            moe_refs[g][...] = low[g * shard : (g + 1) * shard]

    result = kernel_call(
        body,
        "project_out",
        (1,),
        [
            whole_block(attended.shape),
            ANYWHERE,
            whole_block(down.shape),
            whole_block(up.shape),
            whole_block(tokens.shape),
            whole_block((1, width)),
        ],
        [
            whole_block((groups, shard, width)),
            whole_block((groups, rank, shard)),
        ]
        + [whole_block((shard, width))] * groups,
        [shape_of((groups, shard, width), F32), shape_of((groups, rank, shard), BF16)]
        + [shape_of((shard, width), BF16)] * groups,
        scratch=[
            pltpu.VMEM((rows, width), BF16),
            pltpu.VMEM((width, width), BF16),
            pltpu.SemaphoreType.DMA((splits,)),
        ],
        flops=2 * rows * width * width,
        moved=2 * width * width,
    )(attended, w_out, down, up, tokens, gain)
    return result[0], result[1], result[2:]


def one_hot(slot_row, capacity):
    tokens = slot_row.shape[1]
    index = lax.broadcasted_iota(jnp.int32, (capacity, tokens), 0).astype(F32)
    return index == slot_row


def pick_rows(sources, meta_ref, ring, sem, picked, capacity, weigh, begin=0):
    count = meta_ref.shape[0]
    experts = picked.shape[0]
    slots = ring.shape[0]

    def copies(m):
        found = sources(m)
        size = ring.shape[1] // len(found)
        return [
            pltpu.make_async_copy(
                ref, ring.at[m % slots, pl.ds(i * size, size)], sem.at[m, i]
            )
            for i, ref in enumerate(found)
        ]

    for m in range(slots):
        for copy in copies(m):
            copy.start()
    for m in range(count):
        named = jnp.concatenate(
            [one_hot(meta_ref[m, 0, e : e + 1], capacity) for e in range(begin, begin + experts)], axis=0
        )
        for copy in copies(m):
            copy.wait()
        result = dot_nn(named.astype(BF16), ring[m % slots])
        if weigh:
            weights = jnp.concatenate(
                [
                    jnp.broadcast_to(meta_ref[m, 1, e : e + 1], (capacity, named.shape[1]))
                    for e in range(begin, begin + experts)
                ],
                axis=0,
            )
            result = result * jnp.sum(jnp.where(named, weights, 0.0), axis=1, keepdims=True)
        low = result.astype(BF16)
        for e in range(experts):
            picked[e, m * capacity : (m + 1) * capacity] = low[e * capacity : (e + 1) * capacity]
        if m + slots < count:
            for copy in copies(m + slots):
                copy.start()


def expert_grad_hidden(gathered, meta, expert_down, capacity):
    experts, hidden, width = expert_down.shape
    numbers = [len(found) for found in gathered]
    arrays = [array for found in gathered for array in found]
    count = meta.shape[0]
    tokens = meta.shape[-1]
    rows = count * capacity

    def body(meta_ref, w_ref, *rest):
        refs, (out_ref, ring, picked, sem) = rest[: len(arrays)], rest[len(arrays) :]
        expert = pl.program_id(0)

        @pl.when(expert == 0)
        def _():
            pick_rows(
                lambda m: refs[sum(numbers[:m]) : sum(numbers[: m + 1])],
                meta_ref, ring, sem, picked, capacity, True,
            )

        out_ref[0] = dot_nt(picked[expert], w_ref[0]).astype(BF16)

    return kernel_call(
        body,
        "expert_grad_hidden",
        (experts,),
        [
            whole_block(meta.shape),
            pl.BlockSpec((1, hidden, width), lambda e: (e, 0, 0)),
        ]
        + [ANYWHERE] * len(arrays),
        pl.BlockSpec((1, rows, hidden), lambda e: (e, 0, 0)),
        shape_of((experts, rows, hidden), BF16),
        scratch=[
            pltpu.VMEM((4, tokens, width), BF16),
            pltpu.VMEM((experts, rows, width), BF16),
            pltpu.SemaphoreType.DMA((count, max(numbers))),
        ],
        flops=2 * experts * rows * (hidden + tokens) * width,
        moved=2 * experts * hidden * width + 2 * count * tokens * width,
    )(meta, expert_down, *arrays)


def combine_rows(meta_ref, picked, m, capacity):
    experts, _, width = picked.shape
    named = jnp.concatenate(
        [one_hot(meta_ref[m, 0, e : e + 1], capacity) for e in range(experts)], axis=0
    )
    named = jnp.where(named, 1.0, 0.0).T.astype(BF16)
    held = jnp.concatenate(
        [picked[e, m * capacity : (m + 1) * capacity] for e in range(experts)], axis=0
    )
    return dot_nn(named, held)


def send_combined(meta_ref, picked, ring, sem, capacity, targets):
    count = meta_ref.shape[0]
    tokens = ring.shape[1]
    slots = ring.shape[0]
    waiting = {}
    for i, m in enumerate(reversed(range(count))):
        for copy in waiting.pop(i - slots, []):
            copy.wait()
        ring[i % slots] = combine_rows(meta_ref, picked, m, capacity).astype(BF16)
        found = targets(m)
        size = tokens // len(found)
        waiting[i] = [
            pltpu.make_async_copy(
                ring.at[i % slots, pl.ds(b * size, size)], ref, sem.at[i % slots, b]
            )
            for b, ref in enumerate(found)
        ]
        for copy in waiting[i]:
            copy.start()
    for copies in waiting.values():
        for copy in copies:
            copy.wait()


def sum_shapes(count, tokens, width, groups, paired):
    if not paired:
        return [shape_of((count, tokens, width), BF16)]
    one = shape_of((tokens // groups, width), BF16)
    return [one] * (count // 2 * groups) + [shape_of((count // 2, tokens, width), BF16)]


def sum_targets(outs, place_ref, m, groups, paired):
    if not paired:
        return [outs[0].at[place_ref[1] ^ m]]
    if m % 2:
        return [outs[-1].at[m // 2]]
    return outs[m // 2 * groups : (m // 2 + 1) * groups]


def sums_of(result, count, groups, paired):
    if not paired:
        return result[0], None
    return {m: result[m // 2 * groups : (m // 2 + 1) * groups] for m in range(0, count, 2)}, result[-1]


def expert_middle(
    place, gathered, meta, expert_gate, expert_up, grad_hidden, capacity, groups, paired
):
    experts, width, hidden = expert_gate.shape
    count = meta.shape[0]
    tokens = meta.shape[-1]
    rows = count * capacity
    chunk = 256 if rows % 256 == 0 else rows
    numbers = [len(found) for found in gathered]
    arrays = [array for found in gathered for array in found]

    def body(place_ref, meta_ref, gate_ref, up_ref, gh_ref, *rest):
        refs, (h_ref, *outs) = rest[: len(arrays)], rest[len(arrays) : -5]
        ring, picked, made, sem, out_sem = rest[-5:]
        expert = pl.program_id(0)

        @pl.when(expert == 0)
        def _():
            pick_rows(
                lambda m: refs[sum(numbers[:m]) : sum(numbers[: m + 1])],
                meta_ref, ring, sem, picked, capacity, False,
            )

        for c in range(rows // chunk):
            at = slice(c * chunk, (c + 1) * chunk)
            x = picked[expert, at]
            gate = dot_nn(x, gate_ref[0])
            up = dot_nn(x, up_ref[0])
            sigma = sigmoid(gate)
            value = gate * sigma
            grad = gh_ref[0, at].astype(F32)
            h_ref[0, at] = (value * up).astype(BF16)
            grad_gate = (grad * up * (sigma + value * (1.0 - sigma))).astype(BF16)
            grad_up = (grad * value).astype(BF16)
            made[expert, at] = (
                dot_nt(grad_gate, gate_ref[0]) + dot_nt(grad_up, up_ref[0])
            ).astype(BF16)

        @pl.when(expert == experts - 1)
        def _():
            send_combined(
                meta_ref, made, ring, out_sem, capacity,
                lambda m: sum_targets(outs, place_ref, m, groups, paired),
            )

    shapes = sum_shapes(count, tokens, width, groups, paired)
    result = kernel_call(
        body,
        "expert_middle",
        (experts,),
        [
            whole_block(meta.shape),
            pl.BlockSpec((1, width, hidden), lambda e, s: (e, 0, 0)),
            pl.BlockSpec((1, width, hidden), lambda e, s: (e, 0, 0)),
            pl.BlockSpec((1, rows, hidden), lambda e, s: (e, 0, 0)),
        ]
        + [ANYWHERE] * len(arrays),
        [pl.BlockSpec((1, rows, hidden), lambda e, s: (e, 0, 0))] + [ANYWHERE] * len(shapes),
        [shape_of((experts, rows, hidden), BF16)] + shapes,
        scratch=[
            pltpu.VMEM((2, tokens, width), BF16),
            pltpu.VMEM((experts, rows, width), BF16),
            pltpu.VMEM((experts, rows, width), BF16),
            pltpu.SemaphoreType.DMA((count, max(numbers))),
            pltpu.SemaphoreType.DMA((2, groups)),
        ],
        prefetch=1,
        flops=2 * experts * rows * (4 * hidden + tokens) * width,
        moved=4 * experts * hidden * width + 4 * experts * rows * width,
    )(place, meta, expert_gate, expert_up, grad_hidden, *arrays)
    return (result[0],) + sums_of(result[1:], count, groups, paired)


def expert_produce(
    place, hidden_rows, meta, expert_down, capacity, first, last, groups, paired, before=None
):
    experts, hidden, width = expert_down.shape
    count = meta.shape[0]
    tokens = meta.shape[-1]
    rows = count * capacity
    held = before.shape[0] if before is not None else 0

    def body(place_ref, meta_ref, h_ref, w_ref, *rest):
        expert = pl.program_id(0) + first
        result = dot_nn(h_ref[0], w_ref[0])
        if held:
            before_ref, outs, (ring, made, sem, before_sem) = rest[0], rest[1:-4], rest[-4:]
            copy = pltpu.make_async_copy(before_ref, made.at[pl.ds(0, held)], before_sem)

            @pl.when(expert == first)
            def _():
                copy.start()

        else:
            (out_ref,) = rest
        for m in range(count):
            named = one_hot(meta_ref[m, 0, pl.ds(expert, 1)], capacity)
            weight = jnp.sum(
                jnp.where(named, meta_ref[m, 1, pl.ds(expert, 1)], 0.0), axis=1, keepdims=True
            )
            at = slice(m * capacity, (m + 1) * capacity)
            value = (weight * result[at]).astype(BF16)
            if held:
                made[expert, at] = value
            else:
                out_ref[0, at] = value

        if held:

            @pl.when(expert == last - 1)
            def _():
                copy.wait()
                send_combined(
                    meta_ref, made, ring, sem, capacity,
                    lambda m: sum_targets(outs, place_ref, m, groups, paired),
                )

    if held:
        shapes = sum_shapes(count, tokens, width, groups, paired)
        out_specs = [ANYWHERE] * len(shapes)
    else:
        shapes = [shape_of((last - first, rows, width), BF16)]
        out_specs = [pl.BlockSpec((1, rows, width), lambda e, s: (e, 0, 0))]
    result = kernel_call(
        body,
        "expert_produce",
        (last - first,),
        [
            whole_block(meta.shape),
            pl.BlockSpec((1, rows, hidden), lambda e, s: (e + first, 0, 0)),
            pl.BlockSpec((1, hidden, width), lambda e, s: (e + first, 0, 0)),
        ]
        + ([ANYWHERE] if held else []),
        out_specs,
        shapes,
        scratch=[
            pltpu.VMEM((2, tokens, width), BF16),
            pltpu.VMEM((experts, rows, width), BF16),
            pltpu.SemaphoreType.DMA((2, groups)),
            pltpu.SemaphoreType.DMA,
        ]
        if held
        else [],
        prefetch=1,
        flops=2 * (last - first) * rows * hidden * width,
        moved=2 * experts * hidden * width + 2 * experts * rows * width,
    )(place, meta, hidden_rows, expert_down, *([before] if held else []))
    return sums_of(result, count, groups, paired) if held else result[0]


def project_out_back(pieces, mixed, upstream, gain, w_out, down, up, attended, mids):
    splits, groups, shard, part = attended.shape
    width = splits * part
    rank = down.shape[1]
    rows = groups * shard
    number = len(pieces[0])

    def body(up_stream_ref, gain_ref, w_ref, down_ref, up_ref, mixed_ref, att_ref, mid_ref, *rest):
        refs, rest = rest[: groups * number], rest[groups * number :]
        gm_ref, gdown_ref, gup_ref, out_ref, low, held, sem = rest
        copies = [
            pltpu.make_async_copy(w_ref.at[pl.ds(z * part, part)], held.at[z], sem.at[z])
            for z in range(splits)
        ]
        for copy in copies:
            copy.start()
        smalls = []
        for g in range(groups):
            total = refs[g * number][...].astype(F32)
            for ref in refs[g * number + 1 : (g + 1) * number]:
                total += ref[...].astype(F32)
            grad = up_stream_ref[g].astype(F32) + norm_back(mixed_ref[g], gain_ref[...], total)
            gm_ref[g] = grad
            grad = grad.astype(BF16)
            low[g * shard : (g + 1) * shard] = grad
            small = (ADAPTER_SCALE * dot_nt(up_ref[g], grad)).astype(BF16)
            smalls.append(small)
            gup_ref[g] = (ADAPTER_SCALE * dot_nn(mid_ref[g], grad)).astype(BF16)
        for z in range(splits):
            columns = slice(z * part, (z + 1) * part)
            copies[z].wait()
            result = dot_nt(low[...], held[z])
            for g in range(groups):
                out_ref[z, g] = (
                    result[g * shard : (g + 1) * shard] + dot_tn(smalls[g], down_ref[g, :, columns])
                ).astype(BF16)
                gdown_ref[g, :, columns] = dot_nn(smalls[g], att_ref[z, g]).astype(BF16)

    return kernel_call(
        body,
        "project_out_back",
        (1,),
        [
            whole_block(upstream.shape),
            whole_block((1, width)),
            ANYWHERE,
            whole_block(down.shape),
            whole_block(up.shape),
            whole_block(mixed.shape),
            whole_block(attended.shape),
            whole_block(mids.shape),
        ]
        + [whole_block((shard, width))] * (groups * number),
        [
            whole_block((groups, shard, width)),
            whole_block((groups, rank, width)),
            whole_block((groups, rank, width)),
            whole_block(attended.shape),
        ],
        [
            shape_of((groups, shard, width), F32),
            shape_of((groups, rank, width), BF16),
            shape_of((groups, rank, width), BF16),
            shape_of(attended.shape, BF16),
        ],
        scratch=[
            pltpu.VMEM((rows, width), BF16),
            pltpu.VMEM((splits, part, width), BF16),
            pltpu.SemaphoreType.DMA((splits,)),
        ],
        flops=2 * rows * width * width,
        moved=2 * width * width,
    )(
        upstream, gain, w_out, down, up, mixed, attended, mids,
        *[array for found in pieces for array in found],
    )


def adapter_grads(place, group, grads, normed, ups, into):
    listed = is_list(grads)
    splits, (_, shard, part) = piece_shape(grads)
    width = splits * part
    own = ups.shape[1]
    devices = into.shape[0]
    rank = own // 3
    slice_width = width // devices

    def body(place_ref, normed_ref, up_ref, *rest):
        refs, (_, small_ref, down_ref, low) = rest[:splits], rest[splits:]
        for which in range(3):
            for r in range(splits):
                owner = lax.rem(place_ref[0] + r, splits) if listed else r
                low[:, pl.ds(pl.multiple_of(owner * part, part), part)] = refs[r][which]
            at = slice(which * rank, (which + 1) * rank)
            small = (ADAPTER_SCALE * dot_nt(up_ref[at], low[...])).astype(BF16)
            small_ref[at] = small
            result = dot_nn(small, normed_ref[...]).astype(BF16)
            for e in range(devices):
                down_ref[e, at] = result[:, e * slice_width : (e + 1) * slice_width]

    return kernel_call(
        body,
        "adapter_grads",
        (1,),
        [
            pl.BlockSpec((shard, width), lambda i, s: (group, 0)),
            group_block(ups.shape, group),
        ]
        + piece_specs(grads, (3, shard, part), lambda i, s: (0, 0, 0))
        + [ANYWHERE],
        [
            whole_block((own, shard)),
            pl.BlockSpec((devices, None, own, slice_width), lambda i, s: (0, group, 0, 0)),
        ],
        [shape_of((own, shard), BF16), shape_of(into.shape, BF16)],
        scratch=[pltpu.VMEM((shard, width), BF16)],
        prefetch=1,
        aliases={3 + splits: 1},
        flops=12 * shard * rank * width,
        moved=6 * shard * width,
    )(place, normed, ups, *piece_arrays(grads, splits), into)


def project_first_back(group, grads, smalls, downs, w_qkv, tokens, gain, grad_mixed, into=None):
    splits, _, shard, part = grads.shape
    width = splits * part
    rank = downs.shape[1] // 3
    groups = tokens.shape[0]

    def body(down_ref, w_ref, tok_ref, gain_ref, mixed_ref, small_ref, grad_ref, *rest):
        out_ref, low, held, sem = rest[-4:]

        def copy(p, i):
            at = pl.ds(i * part, part)
            return pltpu.make_async_copy(w_ref.at[p, at], held.at[p, at], sem.at[p, i])

        for p in range(3):
            for i in range(splits):
                copy(p, i).start()
        totals = [None] * splits
        for p in range(3):
            for z in range(splits):
                low[:, z * part : (z + 1) * part] = grad_ref[z, p]
            at = slice(p * rank, (p + 1) * rank)
            small = dot_tn(small_ref[at], down_ref[at])
            for i in range(splits):
                copy(p, i).wait()
                columns = slice(i * part, (i + 1) * part)
                result = dot_nt(low[...], held[p, columns]) + small[:, columns]
                totals[i] = result if p == 0 else totals[i] + result
        total = jnp.concatenate(totals, axis=1)
        out_ref[...] = mixed_ref[...] + norm_back(tok_ref[...].astype(F32), gain_ref[...], total)

    return kernel_call(
        body,
        "project_first_back",
        (1,),
        [
            group_block(downs.shape, group),
            ANYWHERE,
            group_block(tokens.shape, group),
            whole_block((1, width)),
            group_block(grad_mixed.shape, group),
            whole_block((3 * rank, shard)),
            whole_block(grads.shape),
        ]
        + ([ANYWHERE] if into is not None else []),
        pl.BlockSpec((None, shard, width), lambda i: (group, 0, 0)),
        shape_of((groups, shard, width), F32),
        scratch=[
            pltpu.VMEM((shard, width), BF16),
            pltpu.VMEM((3, width, width), BF16),
            pltpu.SemaphoreType.DMA((3, splits)),
        ],
        aliases={7: 0} if into is not None else None,
        flops=6 * shard * width * width,
        moved=6 * width * width,
    )(
        downs, w_qkv, tokens, gain, grad_mixed, smalls, grads,
        *([into] if into is not None else []),
    )


def local(
    tokens,
    cotangent,
    lengths,
    adapter_choice,
    expert_ids,
    gate_weights,
    attn_gain,
    moe_gain,
    query_gain,
    key_gain,
    w_qkv,
    w_out,
    expert_gate,
    expert_up,
    expert_down,
    adapt_down,
    first_down,
    second_down,
    adapt_up,
    first_up,
    second_up,
):
    groups, shard, width = tokens.shape
    splits = lax.axis_size("seq")
    devices = lax.axis_size("exp")
    here = lax.axis_index("seq")
    total = shard * splits
    part = width // splits
    rows = groups * shard
    sets, projections, slice_width, rank = adapt_down.shape
    local_experts = expert_gate.shape[0]
    experts = local_experts * devices
    top = expert_ids.shape[-1]
    capacity = 3 * rows * top // (2 * experts)
    listed = [False] * groups

    position = lax.axis_index("exp")
    place = jnp.stack([here, position]).astype(jnp.int32)
    flat_tokens = tokens.reshape(rows, width)
    gain_row = attn_gain.reshape(1, width)
    moe_row = moe_gain.reshape(1, width)
    query_row = query_gain.reshape(1, HEAD)
    key_row = key_gain.reshape(1, HEAD)

    paired = devices == 8 and groups == 2
    own_positions = here * shard + jnp.arange(shard, dtype=jnp.int32)
    own_live = own_positions[None, :] < lengths[:, None]

    base, _, normed = project_first(
        place, flat_tokens, gain_row, w_qkv, groups, splits, listed
    )
    raw = [forward_seq(base[0])]

    adapt_down_low, adapt_up_low, ids, gates = after(
        (adapt_down, adapt_up, expert_ids, gate_weights), normed
    )
    ids = ids.reshape(rows, top).T
    gates = gates.reshape(rows, top).T
    choice = adapter_choice.astype(F32).reshape(1, groups * sets)
    choice = jnp.pad(choice, ((0, 0), (0, rows - groups * sets)))
    routed = route(ids, gates, choice, experts)
    down_rows = jnp.swapaxes(adapt_down_low.astype(BF16), 2, 3)
    up_rows = adapt_up_low.astype(BF16)
    own = 3 * rank
    blocks = [
        jnp.concatenate([found.reshape(-1, slice_width) for found in sources])
        for sources in (
            (down_rows[:, :3], down_rows[:, 3], routed),
            (up_rows[:, :3], up_rows[:, 3]),
        )
    ]
    if paired:
        all_blocks = gather_far(blocks, gather_near(blocks))
        all_downs, all_ups = ([found[g] for found in all_blocks] for g in range(2))
    else:
        cut = blocks[0].shape[0]
        all_downs = [found[0][:cut] for found in gather_whole(blocks)]
        all_ups = [found[0][cut:] for found in gather_whole(blocks)]
    chosen = jnp.sum(adapter_choice * jnp.arange(sets, dtype=jnp.int32)[None, :], axis=1)
    picks = jnp.concatenate([chosen, position.reshape(1)]).astype(jnp.int32)
    sections = [(0, own), (sets * own, rank)]
    downs, out_downs, mids = pick_sets(all_downs, picks, groups, sections, normed)
    ups, out_ups, _ = pick_sets(after(all_ups, mids), picks, groups, sections, normed)
    all_mids = by_distance(jnp.stack(forward_seq([mids] * splits)))

    live_rows = after(own_live, mids)
    upstream = jnp.where(live_rows[:, :, None], cotangent, jnp.zeros((), BF16))
    upstream = [upstream[g] for g in range(groups)]
    routes = jnp.stack([found[sets * (own + rank) :] for found in after(all_downs, mids)])
    routes = routes.reshape(devices, 3 * experts + 16, rows)
    choices = by_relative(routes[:, 3 * experts, : groups * sets])
    choices = choices.reshape(devices, groups, sets)
    meta = routes[:, : 3 * experts].reshape(devices, 3, experts, rows)
    meta = lax.dynamic_slice_in_dim(meta, position * local_experts, local_experts, axis=2)
    meta = meta.astype(F32)
    meta = jnp.stack([meta[:, 0], meta[:, 1] + meta[:, 2]], axis=1)
    blocks = jnp.arange(splits, dtype=jnp.int32)
    frequency = ROPE_BASE ** (-(2.0 / HEAD) * jnp.arange(HEAD // 2, dtype=F32))
    tables = []
    for g in range(groups):
        positions = blocks[:, None] * shard + jnp.arange(shard, dtype=jnp.int32)[None, :]
        angles = after(positions, normed).reshape(total, 1).astype(F32) * frequency[None, :]
        cosine, sine = jnp.cos(angles), jnp.sin(angles)
        tables.append(
            (
                positions.reshape(1, total),
                jnp.concatenate([cosine, cosine], axis=1),
                jnp.concatenate([-sine, sine], axis=1),
            )
        )

    raw[0], all_mids, meta, choices, tables = lax.optimization_barrier(
        (raw[0], all_mids, meta, choices, tables)
    )
    for g in range(1, groups):
        raw.append(forward_seq(after(base[g], raw[g - 1])))
    own_ups = lax.dynamic_slice_in_dim(ups, here * part, part, axis=2)
    own_ups = own_ups.reshape(groups, 3, rank, part)

    saved, heads_rows = [], []
    for g in range(groups):
        if g:
            raw[g] = after(raw[g], heads_rows)
        att, kept = attend(
            lengths[g : g + 1],
            raw[g],
            all_mids[:, g],
            own_ups[g],
            query_row,
            key_row,
            *tables[g],
        )
        saved.append(kept)
        heads_rows.append(att)
        if paired and g == 0:
            near = gather_near(upstream)
            far = far_of(after(near, att))
            cot_rows = gather_far(upstream, near, far)
    if not paired:
        cot_rows = gather_whole(upstream)
    heads_rows = jnp.stack(heads_rows, axis=1)
    if paired:
        heads_rows, cot_rows = lax.optimization_barrier((heads_rows, cot_rows))
    attended = lax.all_to_all(heads_rows, "seq", 0, 0)
    grad_hidden = expert_grad_hidden(
        cot_rows, after(meta, heads_rows), expert_down, capacity
    )
    attended, grad_hidden = lax.optimization_barrier((attended, grad_hidden))
    mixed, mid_out, moe_rows = project_out(
        attended, w_out, out_downs, out_ups, tokens, moe_row
    )
    gathered = gather_far(moe_rows, gather_near(moe_rows)) if paired else gather_whole(moe_rows)
    half = local_experts // 2

    hidden, parts, others = expert_middle(
        place,
        gathered,
        meta,
        expert_gate,
        expert_up,
        grad_hidden,
        capacity,
        groups,
        paired,
    )
    if paired:
        far, near, beside = near_sums_of(parts, others)
        produced = expert_produce(
            place, after(hidden, far), meta, expert_down, capacity, 0, half, groups, paired
        )
        far, near = send_near(far, near)
        far, produced = lax.optimization_barrier((far, produced))
        joined = send_joined(joined_sums_of(parts, beside, far))
        grad_pieces = [
            [parts[0][g], beside[0][g], near[g], joined[g]] for g in range(groups)
        ]
    else:
        summed = lax.psum_scatter(parts, "exp").reshape(groups, shard, width)
        grad_pieces = [[summed[g]] for g in range(groups)]
        produced = expert_produce(
            place, hidden, meta, expert_down, capacity, 0, half, groups, paired
        )
    grad_mixed, grad_out_downs, grad_out_ups, grad_att = project_out_back(
        grad_pieces, mixed, jnp.stack(upstream), moe_row, w_out, out_downs, out_ups, attended, mid_out
    )
    out_parts, out_others = expert_produce(
        place, hidden, after(meta, grad_mixed), expert_down, capacity, half, local_experts,
        groups, paired, produced,
    )
    grad_att = lax.all_to_all(grad_att, "seq", 0, 0)
    grad_raw, gups = [], []
    for g in range(groups):
        if g:
            grad_att = after(grad_att, gups)
        back, gup = attend_back(
            lengths[g : g + 1],
            grad_att,
            g,
            saved[g],
            all_mids[:, g],
            rank,
            query_row,
            key_row,
            *tables[g],
        )
        gups.append(gup)
        if paired and not g:
            out_far, out_near, out_beside = near_sums_of(out_parts, after(out_others, gup))
        if paired and g:
            out_far, out_near = send_near(out_far, out_near)
            back, out_far, out_near = lax.optimization_barrier((back, out_far, out_near))
        grad_raw.append(forward_seq(after(back, grad_raw) if g else back))
    if paired:
        joined_sums = joined_sums_of(out_parts, out_beside, out_far)
        out_joined = send_joined(joined_sums)
        normed = after(normed, joined_sums)
    gups = jnp.stack(after(gups, grad_raw[0]))
    wide_ups = lax.dynamic_update_slice_in_dim(
        jnp.zeros((groups, own, width), BF16), gups, here * part, axis=2
    )
    early = jnp.concatenate([grad_out_downs, wide_ups, grad_out_ups], axis=1)
    early = jnp.moveaxis(early.reshape(groups, -1, devices, slice_width), 2, 0)

    late = jnp.pad(early, ((0, 0), (0, 0), (own, 0), (0, 0)))
    grad_input = None
    for g in range(groups):
        small, late = adapter_grads(place, g, grad_raw[g], normed, ups, late)
        if g == groups - 1:
            late = lax.all_to_all(late, "exp", 0, 0)
        grad_input = project_first_back(
            g, grad_raw[g], small, downs, w_qkv, tokens, gain_row, grad_mixed, grad_input
        )
        if g < groups - 1:
            late, grad_input = lax.optimization_barrier((late, grad_input))
            if paired:
                outputs = [
                    mixed[g]
                    + functools.reduce(
                        jnp.add,
                        [
                            value.astype(F32)
                            for value in (out_parts[0][g], out_beside[0][g], out_near[g], out_joined[g])
                        ],
                    )
                    for g in range(groups)
                ]
                output = jnp.stack(outputs).astype(BF16)
            else:
                out_sum = lax.psum_scatter(out_parts, "exp").reshape(groups, shard, width)
                output = (mixed + out_sum.astype(F32)).astype(BF16)
            late, output = lax.optimization_barrier((late, output))
    late, grad_input = lax.optimization_barrier((late, grad_input))
    pieces = jnp.einsum("dgk,dgrw->krw", choices, late, preferred_element_type=F32)
    pieces = pieces.astype(BF16)
    pieces = pieces.reshape(splits, -1, slice_width)
    order = (here + jnp.arange(splits)) % splits
    pieces = list(jnp.take(pieces, order, axis=0))
    summed = add_low(*forward_seq(pieces))
    in_sets = by_distance(jnp.stack(forward_seq([summed] * splits)))
    in_sets = in_sets.reshape(sets, 2, projections, rank, slice_width).astype(F32)
    shard_down = jnp.swapaxes(in_sets[:, 0], 2, 3)
    shard_up = in_sets[:, 1]
    new_first_down, new_second_down, new_down = adam_update(
        adapt_down, shard_down, first_down, second_down, RATE_DOWN
    )
    new_first_up, new_second_up, new_up = adam_update(
        adapt_up, shard_up, first_up, second_up, RATE_UP
    )
    return (
        output,
        grad_input,
        new_first_down,
        new_second_down,
        new_down,
        new_first_up,
        new_second_up,
        new_up,
    )


def solution(mesh):
    in_specs = (
        P("exp", "seq", None),
        P("exp", "seq", None),
        P("exp"),
        P("exp", None),
        P("exp", "seq", None, None, None),
        P("exp", "seq", None, None, None),
        P(),
        P(),
        P(),
        P(),
        P(),
        P(),
        P("exp", None, None),
        P("exp", None, None),
        P("exp", None, None),
        P(None, None, "exp", None),
        P(None, None, "exp", None),
        P(None, None, "exp", None),
        P(None, None, None, "exp"),
        P(None, None, None, "exp"),
        P(None, None, None, "exp"),
    )
    out_specs = (
        P("exp", "seq", None),
        P("exp", "seq", None),
        P(None, None, "exp", None),
        P(None, None, "exp", None),
        P(None, None, "exp", None),
        P(None, None, None, "exp"),
        P(None, None, None, "exp"),
        P(None, None, None, "exp"),
    )
    return jax.shard_map(local, mesh=mesh, in_specs=in_specs, out_specs=out_specs, check_vma=False)
```

```python
import functools

import jax
import jax.numpy as jnp
from jax import lax
from jax.experimental import pallas as pl
from jax.experimental.pallas import tpu as pltpu
from jax.sharding import PartitionSpec as P

HEAD = 128
STEP = 5

NORM_EPS = 1e-05
ROPE_BASE = 50000.0
ADAPTER_SCALE = 0.5
BETA_FIRST = 0.5
BETA_SECOND = 0.5
RATE_DOWN = 0.02
RATE_UP = 0.2
WEIGHT_DECAY = 0.01
ADAM_EPS = 1e-08
MASKED = -1e30
SCORE_SCALE = HEAD ** (-0.5)

F32 = jnp.float32
BF16 = jnp.bfloat16
VMEM_LIMIT = 62 * 1024 * 1024
COST_SHARE = 0.01


def dot_nn(a, b):
    return lax.dot_general(a, b, (((1,), (0,)), ((), ())), preferred_element_type=F32)


def dot_nt(a, b):
    return lax.dot_general(a, b, (((1,), (1,)), ((), ())), preferred_element_type=F32)


def dot_tn(a, b):
    return lax.dot_general(a, b, (((0,), (0,)), ((), ())), preferred_element_type=F32)


def inverse_rms(values):
    return lax.rsqrt(jnp.mean(values * values, axis=-1, keepdims=True) + NORM_EPS)


def norm_back(values, gain, upstream):
    inverse = inverse_rms(values)
    scaled = upstream * gain
    return inverse * scaled - values * (inverse * inverse * inverse) * jnp.mean(
        values * scaled, axis=-1, keepdims=True
    )


def sigmoid(values):
    return 0.5 + 0.5 * jnp.tanh(0.5 * values)


def adam_update(weight, gradient, first, second, step_rate):
    new_first = BETA_FIRST * first + (1.0 - BETA_FIRST) * gradient
    new_second = BETA_SECOND * second + (1.0 - BETA_SECOND) * gradient * gradient
    first_hat = new_first / (1.0 - BETA_FIRST**STEP)
    second_hat = new_second / (1.0 - BETA_SECOND**STEP)
    new_weight = weight - step_rate * (
        first_hat / (jnp.sqrt(second_hat) + ADAM_EPS) + WEIGHT_DECAY * weight
    )
    return (new_first, new_second, new_weight)


def shape_of(shape, dtype):
    return jax.ShapeDtypeStruct(shape, dtype)


def whole_block(shape):
    rank = len(shape)
    return pl.BlockSpec(tuple(shape), lambda *_: (0,) * rank)


def kernel_call(
    body, name, grid, in_specs, out_specs, out_shape, scratch=(), prefetch=0, flops=0, moved=0,
    aliases=None,
):
    return pl.pallas_call(
        body,
        grid_spec=pltpu.PrefetchScalarGridSpec(
            num_scalar_prefetch=prefetch,
            grid=grid,
            in_specs=in_specs,
            out_specs=out_specs,
            scratch_shapes=list(scratch),
        ),
        out_shape=out_shape,
        input_output_aliases=aliases or {},
        name=name,
        cost_estimate=pl.CostEstimate(
            flops=int(flops * COST_SHARE), bytes_accessed=int(moved * COST_SHARE), transcendentals=0
        ),
        compiler_params=pltpu.CompilerParams(vmem_limit_bytes=VMEM_LIMIT),
    )


def swap(values, mask):
    count = lax.axis_size("exp")
    return lax.ppermute(values, "exp", [(i, i ^ mask) for i in range(count)])


def shift(values, distance):
    count = lax.axis_size("seq")
    return lax.ppermute(values, "seq", [(i, (i + distance) % count) for i in range(count)])


def shift_order():
    count = lax.axis_size("seq")
    return sorted(range(1, count), key=lambda r: -min(r, count - r))


def forward_seq(pieces):
    if not isinstance(pieces, (list, tuple)):
        return lax.all_to_all(pieces, "seq", 0, 0)
    came = {r: shift(pieces[r], r) for r in shift_order()}
    return [pieces[0]] + [came[r] for r in range(1, len(pieces))]


def backward_seq(pieces):
    if not isinstance(pieces, (list, tuple)):
        return lax.all_to_all(pieces, "seq", 0, 0)
    came = {r: shift(pieces[r], -r) for r in shift_order()}
    return [pieces[0]] + [came[r] for r in range(1, len(pieces))]


def tell_all(values, axis):
    count = lax.axis_size(axis)
    return lax.all_to_all(jnp.broadcast_to(values[None], (count,) + values.shape), axis, 0, 0)


def by_distance(stacked):
    count = lax.axis_size("seq")
    order = (lax.axis_index("seq") - jnp.arange(count)) % count
    return jnp.take(stacked, order, axis=0)


def by_relative(stacked):
    count = lax.axis_size("exp")
    return jnp.take(stacked, lax.axis_index("exp") ^ jnp.arange(count), axis=0)


STEP_HEADS = 1

WAYS = ((2, 4), (4, 2))


def gather_near(rows):
    near = {2: [None] * len(rows), 4: [None] * len(rows)}
    for g, (first, _) in enumerate(WAYS):
        near[first][g] = swap(rows[g], first)
    for g, (_, second) in enumerate(WAYS):
        near[second][g] = swap(rows[g], second)
    return near


def far_of(near):
    return [swap(near[first][g], second) for g, (first, second) in enumerate(WAYS)]


def gather_far(rows, near, far=None):
    far = far or far_of(near)
    found = []
    for blocks in (rows, near[2], near[4], far):
        found += [list(blocks), [swap(block, 1) for block in blocks]]
    return found


def gather_whole(rows):
    everything = by_relative(lax.all_gather(jnp.concatenate(rows), "exp"))
    return [[block] for block in everything]


def near_sums_of(parts, others):
    groups = len(parts[0])
    last = swap(others[1], 1).reshape((groups,) + parts[0][0].shape)
    beside = swap(others[0], 1).reshape((3, groups) + parts[0][0].shape)
    far = [add_low(parts[6][g], last[g]) for g in range(groups)]
    beside = after(beside, far)
    near = [add_low(parts[WAYS[g][0]][g], beside[WAYS[g][0] // 2][g]) for g in range(groups)]
    return far, near, beside


def send_near(far, near):
    far = [swap(far[g], WAYS[g][0]) for g in range(len(far))]
    return far, [swap(near[g], WAYS[g][0]) for g in range(len(near))]


def joined_sums_of(parts, beside, far):
    return [
        add_low(parts[WAYS[g][1]][g], beside[WAYS[g][1] // 2][g], far[g]) for g in range(len(far))
    ]


def send_joined(joined):
    return [swap(joined[g], WAYS[g][1]) for g in range(len(joined))]


def add_low(*values):
    return functools.reduce(jnp.add, [value.astype(F32) for value in values]).astype(BF16)


def after(values, *first):
    return lax.optimization_barrier((values, first))[0]


ANYWHERE = pl.BlockSpec(memory_space=pl.ANY)


def group_block(shape, group):
    rank = len(shape) - 1
    return pl.BlockSpec((None,) + tuple(shape[1:]), lambda *_: (group,) + (0,) * rank)


def is_list(pieces):
    return isinstance(pieces, (list, tuple))


def piece_shape(pieces):
    if is_list(pieces):
        return len(pieces), pieces[0].shape
    return pieces.shape[0], pieces.shape[1:]


def piece_arrays(pieces, splits):
    return list(pieces) if is_list(pieces) else [pieces] * splits


def piece_specs(pieces, block, index):
    if is_list(pieces):
        return [pl.BlockSpec(block, index)] * len(pieces)
    return [
        pl.BlockSpec((None,) + tuple(block), lambda *at, r=r: (r,) + tuple(index(*at)))
        for r in range(pieces.shape[0])
    ]


def out_specs_of(listed, splits, block, index):
    if listed:
        return [pl.BlockSpec(block, index)] * splits
    return [pl.BlockSpec((splits,) + tuple(block), lambda *at: (0,) + tuple(index(*at)))]


def out_shapes_of(listed, splits, shape, dtype):
    if listed:
        return [shape_of(shape, dtype)] * splits
    return [shape_of((splits,) + tuple(shape), dtype)]


def out_refs_of(listed, refs):
    return list(refs) if listed else [refs[0].at[r] for r in range(refs[0].shape[0])]


def out_pieces_of(listed, results):
    return list(results) if listed else results[0]


def project_first(place, tokens, gain, w_qkv, groups, splits, listed):
    rows, width = tokens.shape
    part = width // splits
    shard = rows // groups
    counts = [splits if listed[g] else 1 for g in range(groups)]
    total = sum(counts)

    def body(place_ref, tok_ref, gain_ref, w_ref, *rest):
        outs = rest[:total]
        parts_ref, normed_ref, held, sem = rest[total:]
        which = pl.program_id(0)

        def owner(r):
            return lax.rem(place_ref[0] + r, splits)

        def copy(p, r):
            columns = pl.ds(pl.multiple_of(owner(r) * part, part), part)
            return pltpu.make_async_copy(
                w_ref.at[p, :, columns],
                held.at[p, :, pl.ds(r * part, part)],
                sem.at[p, r],
            )

        @pl.when(which == 0)
        def _():
            for p in range(3):
                for r in range(splits):
                    copy(p, r).start()
            values = tok_ref[...].astype(F32)
            low = (values * inverse_rms(values) * gain_ref[...]).astype(BF16)
            normed_ref[...] = low
            for z in range(splits):
                for g in range(groups):
                    parts_ref[z, g] = low[
                        g * shard : (g + 1) * shard, z * part : (z + 1) * part
                    ]

        for r in range(splits):
            copy(which, r).wait()
            result = dot_nn(normed_ref[...], held[which, :, r * part : (r + 1) * part])
            first = 0
            for g in range(groups):
                low = result[g * shard : (g + 1) * shard].astype(BF16)
                if listed[g]:
                    outs[first + r][0] = low
                else:
                    outs[first][owner(r), 0] = low
                first += counts[g]

    specs, shapes = [], []
    for g in range(groups):
        specs += out_specs_of(listed[g], splits, (1, shard, part), lambda p, s: (p, 0, 0))
        shapes += out_shapes_of(listed[g], splits, (3, shard, part), BF16)
    result = kernel_call(
        body,
        "project_first",
        (3,),
        [whole_block((rows, width)), whole_block((1, width)), ANYWHERE],
        specs + [whole_block((splits, groups, shard, part)), whole_block((rows, width))],
        shapes
        + [shape_of((splits, groups, shard, part), BF16), shape_of((rows, width), BF16)],
        scratch=[
            pltpu.VMEM((3, width, width), BF16),
            pltpu.SemaphoreType.DMA((3, splits)),
        ],
        prefetch=1,
        flops=6 * rows * width * width,
        moved=6 * width * width,
    )(place, tokens, gain, w_qkv)
    outs, first = [], 0
    for g in range(groups):
        outs.append(out_pieces_of(listed[g], result[first : first + counts[g]]))
        first += counts[g]
    return outs, result[total], result[total + 1]


def pick_sets(gathered, picks, groups, sections, normed):
    count = len(gathered)
    part = gathered[0].shape[1]
    width = count * part
    shard = normed.shape[0] // groups
    number = len(sections)

    def body(pick_ref, normed_ref, *rest):
        refs, outs, sem = rest[:count], rest[count:-1], rest[-1]
        copies = []
        for g in range(groups):
            for i, (first, own) in enumerate(sections):
                for m in range(count):
                    columns = pl.ds(pl.multiple_of((pick_ref[groups] ^ m) * part, part), part)
                    copies.append(
                        pltpu.make_async_copy(
                            refs[m].at[pl.ds(pl.multiple_of(first + pick_ref[g] * own, own), own)],
                            outs[i].at[g, :, columns],
                            sem.at[(g * number + i) * count + m],
                        )
                    )
        for copy in copies:
            copy.start()
        for copy in copies:
            copy.wait()
        for g in range(groups):
            outs[number][g] = dot_nt(
                outs[0][g], normed_ref[g * shard : (g + 1) * shard]
            ).astype(BF16)

    shapes = [(groups, own, width) for _, own in sections]
    shapes.append((groups, sections[0][1], shard))
    return kernel_call(
        body,
        "pick_sets",
        (1,),
        [whole_block(normed.shape)] + [ANYWHERE] * count,
        [whole_block(shape) for shape in shapes],
        [shape_of(shape, BF16) for shape in shapes],
        scratch=[pltpu.SemaphoreType.DMA((groups * number * count,))],
        prefetch=1,
        moved=4 * groups * width * sum(own for _, own in sections),
    )(picks, normed, *gathered)


def route(ids, gates, choice, experts):
    top, tokens = ids.shape

    def body(ids_ref, gates_ref, choice_ref, out_ref):
        expert = lax.broadcasted_iota(jnp.int32, (experts, tokens), 0)
        weights = jnp.zeros((experts, tokens), F32)
        named = jnp.zeros((experts, tokens), F32)
        for k in range(top):
            hit = expert == ids_ref[k : k + 1]
            weights = jnp.where(hit, gates_ref[k : k + 1], weights)
            named = jnp.where(hit, 1.0, named)
        earlier = lax.broadcasted_iota(jnp.int32, (tokens, tokens), 0) < lax.broadcasted_iota(
            jnp.int32, (tokens, tokens), 1
        )
        ranks = dot_nn(named.astype(BF16), jnp.where(earlier, 1.0, 0.0).astype(BF16))
        slots = jnp.where(named > 0.0, ranks, -1.0)
        front = weights.astype(BF16)
        out_ref[:experts] = slots.astype(BF16)
        out_ref[experts : 2 * experts] = front
        out_ref[2 * experts : 3 * experts] = (weights - front.astype(F32)).astype(BF16)
        out_ref[3 * experts :] = jnp.broadcast_to(choice_ref[...], (16, tokens)).astype(BF16)

    shape = (3 * experts + 16, tokens)
    return kernel_call(
        body,
        "route",
        (1,),
        [whole_block(ids.shape), whole_block(gates.shape), whole_block(choice.shape)],
        whole_block(shape),
        shape_of(shape, BF16),
        moved=12 * experts * tokens,
    )(ids, gates, choice)


def rotate(values, cosine, sine):
    return values * cosine + pltpu.roll(values, HEAD // 2, 1) * sine


def rotate_back(values, cosine, sine):
    return values * cosine - pltpu.roll(values, HEAD // 2, 1) * sine


def softmax_rows(queries, keys, live):
    scores = jnp.where(live, dot_nt(queries, keys) * SCORE_SCALE, MASKED)
    exponent = jnp.exp(scores - jnp.max(scores, axis=-1, keepdims=True))
    return exponent * (1.0 / jnp.sum(exponent, axis=-1, keepdims=True))


def attend(length, raw, mids, ups, query_gain, key_gain, positions, cosine, sine):
    listed = is_list(raw)
    splits, (_, shard, part) = piece_shape(raw)
    rank = ups.shape[1]
    total = splits * shard
    heads = part // HEAD
    step_heads = min(heads, STEP_HEADS)

    def body(len_ref, up_ref, qg_ref, kg_ref, pos_ref, cos_ref, sin_ref, *rest):
        raw_refs, mid_ref = rest[:splits], rest[splits]
        att_refs = out_refs_of(listed, rest[splits + 1 : -5])
        q_ref, k_ref, v_ref, rq_ref, rk_ref = rest[-5:]

        mids = [
            jnp.concatenate(
                [mid_ref[r, which * rank : (which + 1) * rank] for r in range(splits)], axis=1
            )
            for which in range(3)
        ]
        cosine, sine = cos_ref[...], sin_ref[...]
        for h in range(step_heads):
            at = slice(h * HEAD, (h + 1) * HEAD)

            def full(which):
                base = jnp.concatenate([ref[which, :, at] for ref in raw_refs], axis=0)
                added = dot_tn(mids[which], up_ref[which, :, at])
                return base.astype(F32) + ADAPTER_SCALE * added

            raw_q, raw_k, raw_v = full(0), full(1), full(2)
            rq_ref[h] = raw_q
            rk_ref[h] = raw_k
            queries = rotate(raw_q * inverse_rms(raw_q) * qg_ref[...], cosine, sine).astype(BF16)
            keys = rotate(raw_k * inverse_rms(raw_k) * kg_ref[...], cosine, sine).astype(BF16)
            values = raw_v.astype(BF16)
            q_ref[h] = queries
            k_ref[h] = keys
            v_ref[h] = values
            weights = softmax_rows(queries, keys, pos_ref[...] < len_ref[0]).astype(BF16)
            result = dot_nn(weights, values).astype(BF16)
            for r in range(splits):
                att_refs[r][:, at] = result[r * shard : (r + 1) * shard]

    wide = step_heads * HEAD
    head_block = pl.BlockSpec((step_heads, total, HEAD), lambda h, s: (h, 0, 0))
    result = kernel_call(
        body,
        "attend",
        (heads // step_heads,),
        [
            pl.BlockSpec((3, rank, wide), lambda h, s: (0, 0, h)),
            whole_block((1, HEAD)),
            whole_block((1, HEAD)),
            whole_block((1, total)),
            whole_block((total, HEAD)),
            whole_block((total, HEAD)),
        ]
        + piece_specs(raw, (3, shard, wide), lambda h, s: (0, 0, h))
        + [whole_block(mids.shape)],
        out_specs_of(listed, splits, (shard, wide), lambda h, s: (0, h)) + [head_block] * 5,
        out_shapes_of(listed, splits, (shard, part), BF16)
        + [shape_of((heads, total, HEAD), BF16)] * 3
        + [shape_of((heads, total, HEAD), F32)] * 2,
        prefetch=1,
        flops=4 * heads * total * total * HEAD,
        moved=heads * total * HEAD * 24 + 4 * heads * total * total,
    )(length, ups, query_gain, key_gain, positions, cosine, sine, *piece_arrays(raw, splits), mids)
    return out_pieces_of(listed, result[:-5]), result[-5:]


def attend_back(length, grads, group, saved, mids, rank, query_gain, key_gain, positions, cosine, sine):
    listed = False
    splits, _, shard, part = grads.shape
    total = splits * shard
    heads = part // HEAD
    step_heads = min(heads, STEP_HEADS)

    def body(len_ref, qg_ref, kg_ref, pos_ref, cos_ref, sin_ref, *rest):
        grad_refs, mid_ref = rest[:splits], rest[splits]
        q_ref, k_ref, v_ref, rq_ref, rk_ref = rest[splits + 1 : splits + 6]
        out_refs = out_refs_of(listed, rest[splits + 6 : -1])
        gup_ref = rest[-1]
        cosine, sine = cos_ref[...], sin_ref[...]
        mids = [
            jnp.concatenate(
                [mid_ref[r, which * rank : (which + 1) * rank] for r in range(splits)], axis=1
            )
            for which in range(3)
        ]
        for h in range(step_heads):
            at = slice(h * HEAD, (h + 1) * HEAD)
            queries, keys, values = q_ref[h], k_ref[h], v_ref[h]
            grad = jnp.concatenate([ref[:, at] for ref in grad_refs], axis=0)
            weights = softmax_rows(queries, keys, pos_ref[...] < len_ref[0])
            grad_probs = dot_nt(grad, values)
            inner = jnp.sum(weights * grad_probs, axis=-1, keepdims=True)
            grad_scores = (weights * (grad_probs - inner)).astype(BF16)
            grad_q = dot_nn(grad_scores, keys) * SCORE_SCALE
            grad_k = dot_tn(grad_scores, queries) * SCORE_SCALE
            grad_v = dot_tn(weights.astype(BF16), grad)
            grad_q = norm_back(rq_ref[h], qg_ref[...], rotate_back(grad_q, cosine, sine))
            grad_k = norm_back(rk_ref[h], kg_ref[...], rotate_back(grad_k, cosine, sine))
            for which, value in enumerate((grad_q, grad_k, grad_v)):
                low = value.astype(BF16)
                for r in range(splits):
                    out_refs[r][which, :, at] = low[r * shard : (r + 1) * shard]
                gup_ref[which * rank : (which + 1) * rank, at] = (
                    ADAPTER_SCALE * dot_nn(mids[which], low)
                ).astype(BF16)

    wide = step_heads * HEAD
    head_block = pl.BlockSpec((step_heads, total, HEAD), lambda h, s: (h, 0, 0))
    result = kernel_call(
        body,
        "attend_back",
        (heads // step_heads,),
        [
            whole_block((1, HEAD)),
            whole_block((1, HEAD)),
            whole_block((1, total)),
            whole_block((total, HEAD)),
            whole_block((total, HEAD)),
        ]
        + [
            pl.BlockSpec((None, None, shard, wide), lambda h, s, r=r: (r, group, 0, h))
            for r in range(splits)
        ]
        + [whole_block(mids.shape)]
        + [head_block] * 5,
        out_specs_of(listed, splits, (3, shard, wide), lambda h, s: (0, 0, h))
        + [pl.BlockSpec((3 * rank, wide), lambda h, s: (0, h))],
        out_shapes_of(listed, splits, (3, shard, part), BF16)
        + [shape_of((3 * rank, part), BF16)],
        prefetch=1,
        flops=10 * heads * total * total * HEAD,
        moved=heads * total * HEAD * 24 + 8 * heads * total * total,
    )(length, query_gain, key_gain, positions, cosine, sine, *[grads] * splits, mids, *saved)
    return out_pieces_of(listed, result[:-1]), result[-1]


def project_out(attended, w_out, down, up, tokens, gain):
    splits, groups, shard, part = attended.shape
    width = splits * part
    rank = down.shape[1]
    rows = groups * shard

    def body(att_ref, w_ref, down_ref, up_ref, tok_ref, gain_ref, *rest):
        mixed_ref, mid_ref = rest[:2]
        moe_refs = rest[2 : 2 + groups]
        att, held, sem = rest[2 + groups :]
        copies = [
            pltpu.make_async_copy(
                w_ref.at[pl.ds(i * part, part)], held.at[pl.ds(i * part, part)], sem.at[i]
            )
            for i in range(splits)
        ]
        for copy in copies:
            copy.start()
        adapter = []
        for g in range(groups):
            at = slice(g * shard, (g + 1) * shard)
            for z in range(splits):
                att[at, z * part : (z + 1) * part] = att_ref[z, g]
            mid = dot_nt(down_ref[g], att[at]).astype(BF16)
            mid_ref[g] = mid
            adapter.append(
                tok_ref[g].astype(F32) + ADAPTER_SCALE * dot_tn(mid, up_ref[g])
            )
        total = jnp.concatenate(adapter, axis=0)
        for i, copy in enumerate(copies):
            copy.wait()
            total += dot_nn(att[:, i * part : (i + 1) * part], held[i * part : (i + 1) * part])
        low = (total * inverse_rms(total) * gain_ref[...]).astype(BF16)
        for g in range(groups):
            mixed_ref[g] = total[g * shard : (g + 1) * shard]
            moe_refs[g][...] = low[g * shard : (g + 1) * shard]

    result = kernel_call(
        body,
        "project_out",
        (1,),
        [
            whole_block(attended.shape),
            ANYWHERE,
            whole_block(down.shape),
            whole_block(up.shape),
            whole_block(tokens.shape),
            whole_block((1, width)),
        ],
        [
            whole_block((groups, shard, width)),
            whole_block((groups, rank, shard)),
        ]
        + [whole_block((shard, width))] * groups,
        [shape_of((groups, shard, width), F32), shape_of((groups, rank, shard), BF16)]
        + [shape_of((shard, width), BF16)] * groups,
        scratch=[
            pltpu.VMEM((rows, width), BF16),
            pltpu.VMEM((width, width), BF16),
            pltpu.SemaphoreType.DMA((splits,)),
        ],
        flops=2 * rows * width * width,
        moved=2 * width * width,
    )(attended, w_out, down, up, tokens, gain)
    return result[0], result[1], result[2:]


def one_hot(slot_row, capacity):
    tokens = slot_row.shape[1]
    index = lax.broadcasted_iota(jnp.int32, (capacity, tokens), 0).astype(F32)
    return index == slot_row


def pick_rows(sources, meta_ref, ring, sem, picked, capacity, weigh, begin=0):
    count = meta_ref.shape[0]
    experts = picked.shape[0]
    slots = ring.shape[0]

    def copies(m):
        found = sources(m)
        size = ring.shape[1] // len(found)
        return [
            pltpu.make_async_copy(
                ref, ring.at[m % slots, pl.ds(i * size, size)], sem.at[m, i]
            )
            for i, ref in enumerate(found)
        ]

    for m in range(slots):
        for copy in copies(m):
            copy.start()
    for m in range(count):
        named = jnp.concatenate(
            [one_hot(meta_ref[m, 0, e : e + 1], capacity) for e in range(begin, begin + experts)], axis=0
        )
        for copy in copies(m):
            copy.wait()
        result = dot_nn(named.astype(BF16), ring[m % slots])
        if weigh:
            weights = jnp.concatenate(
                [
                    jnp.broadcast_to(meta_ref[m, 1, e : e + 1], (capacity, named.shape[1]))
                    for e in range(begin, begin + experts)
                ],
                axis=0,
            )
            result = result * jnp.sum(jnp.where(named, weights, 0.0), axis=1, keepdims=True)
        low = result.astype(BF16)
        for e in range(experts):
            picked[e, m * capacity : (m + 1) * capacity] = low[e * capacity : (e + 1) * capacity]
        if m + slots < count:
            for copy in copies(m + slots):
                copy.start()


def expert_grad_hidden(gathered, meta, expert_down, capacity):
    experts, hidden, width = expert_down.shape
    numbers = [len(found) for found in gathered]
    arrays = [array for found in gathered for array in found]
    count = meta.shape[0]
    tokens = meta.shape[-1]
    rows = count * capacity

    def body(meta_ref, w_ref, *rest):
        refs, (out_ref, ring, picked, sem) = rest[: len(arrays)], rest[len(arrays) :]
        expert = pl.program_id(0)

        @pl.when(expert == 0)
        def _():
            pick_rows(
                lambda m: refs[sum(numbers[:m]) : sum(numbers[: m + 1])],
                meta_ref, ring, sem, picked, capacity, True,
            )

        out_ref[0] = dot_nt(picked[expert], w_ref[0]).astype(BF16)

    return kernel_call(
        body,
        "expert_grad_hidden",
        (experts,),
        [
            whole_block(meta.shape),
            pl.BlockSpec((1, hidden, width), lambda e: (e, 0, 0)),
        ]
        + [ANYWHERE] * len(arrays),
        pl.BlockSpec((1, rows, hidden), lambda e: (e, 0, 0)),
        shape_of((experts, rows, hidden), BF16),
        scratch=[
            pltpu.VMEM((4, tokens, width), BF16),
            pltpu.VMEM((experts, rows, width), BF16),
            pltpu.SemaphoreType.DMA((count, max(numbers))),
        ],
        flops=2 * experts * rows * (hidden + tokens) * width,
        moved=2 * experts * hidden * width + 2 * count * tokens * width,
    )(meta, expert_down, *arrays)


def combine_rows(meta_ref, picked, m, capacity):
    experts, _, width = picked.shape
    named = jnp.concatenate(
        [one_hot(meta_ref[m, 0, e : e + 1], capacity) for e in range(experts)], axis=0
    )
    named = jnp.where(named, 1.0, 0.0).T.astype(BF16)
    held = jnp.concatenate(
        [picked[e, m * capacity : (m + 1) * capacity] for e in range(experts)], axis=0
    )
    return dot_nn(named, held)


def send_combined(meta_ref, picked, ring, sem, capacity, targets):
    count = meta_ref.shape[0]
    tokens = ring.shape[1]
    slots = ring.shape[0]
    waiting = {}
    for i, m in enumerate(reversed(range(count))):
        for copy in waiting.pop(i - slots, []):
            copy.wait()
        ring[i % slots] = combine_rows(meta_ref, picked, m, capacity).astype(BF16)
        found = targets(m)
        size = tokens // len(found)
        waiting[i] = [
            pltpu.make_async_copy(
                ring.at[i % slots, pl.ds(b * size, size)], ref, sem.at[i % slots, b]
            )
            for b, ref in enumerate(found)
        ]
        for copy in waiting[i]:
            copy.start()
    for copies in waiting.values():
        for copy in copies:
            copy.wait()


def sum_shapes(count, tokens, width, groups, paired):
    if not paired:
        return [shape_of((count, tokens, width), BF16)]
    one = shape_of((tokens // groups, width), BF16)
    return [one] * (count // 2 * groups) + [
        shape_of((count // 2 - 1, tokens, width), BF16),
        shape_of((1, tokens, width), BF16),
    ]


def sum_targets(outs, place_ref, m, groups, paired):
    if not paired:
        return [outs[0].at[place_ref[1] ^ m]]
    if m == 2 * (outs[-2].shape[0] + 1) - 1:
        return [outs[-1].at[0]]
    if m % 2:
        return [outs[-2].at[m // 2]]
    return outs[m // 2 * groups : (m // 2 + 1) * groups]


def sums_of(result, count, groups, paired):
    if not paired:
        return result[0], None
    even = {m: result[m // 2 * groups : (m // 2 + 1) * groups] for m in range(0, count, 2)}
    return even, result[-2:]


def expert_middle(
    place, gathered, meta, expert_gate, expert_up, grad_hidden, capacity, groups, paired
):
    experts, width, hidden = expert_gate.shape
    count = meta.shape[0]
    tokens = meta.shape[-1]
    rows = count * capacity
    chunk = 256 if rows % 256 == 0 else rows
    numbers = [len(found) for found in gathered]
    arrays = [array for found in gathered for array in found]

    def body(place_ref, meta_ref, gate_ref, up_ref, gh_ref, *rest):
        refs, (h_ref, *outs) = rest[: len(arrays)], rest[len(arrays) : -5]
        ring, picked, made, sem, out_sem = rest[-5:]
        expert = pl.program_id(0)

        @pl.when(expert == 0)
        def _():
            pick_rows(
                lambda m: refs[sum(numbers[:m]) : sum(numbers[: m + 1])],
                meta_ref, ring, sem, picked, capacity, False,
            )

        for c in range(rows // chunk):
            at = slice(c * chunk, (c + 1) * chunk)
            x = picked[expert, at]
            gate = dot_nn(x, gate_ref[0])
            up = dot_nn(x, up_ref[0])
            sigma = sigmoid(gate)
            value = gate * sigma
            grad = gh_ref[0, at].astype(F32)
            h_ref[0, at] = (value * up).astype(BF16)
            grad_gate = (grad * up * (sigma + value * (1.0 - sigma))).astype(BF16)
            grad_up = (grad * value).astype(BF16)
            made[expert, at] = (
                dot_nt(grad_gate, gate_ref[0]) + dot_nt(grad_up, up_ref[0])
            ).astype(BF16)

        @pl.when(expert == experts - 1)
        def _():
            send_combined(
                meta_ref, made, ring, out_sem, capacity,
                lambda m: sum_targets(outs, place_ref, m, groups, paired),
            )

    shapes = sum_shapes(count, tokens, width, groups, paired)
    result = kernel_call(
        body,
        "expert_middle",
        (experts,),
        [
            whole_block(meta.shape),
            pl.BlockSpec((1, width, hidden), lambda e, s: (e, 0, 0)),
            pl.BlockSpec((1, width, hidden), lambda e, s: (e, 0, 0)),
            pl.BlockSpec((1, rows, hidden), lambda e, s: (e, 0, 0)),
        ]
        + [ANYWHERE] * len(arrays),
        [pl.BlockSpec((1, rows, hidden), lambda e, s: (e, 0, 0))] + [ANYWHERE] * len(shapes),
        [shape_of((experts, rows, hidden), BF16)] + shapes,
        scratch=[
            pltpu.VMEM((2, tokens, width), BF16),
            pltpu.VMEM((experts, rows, width), BF16),
            pltpu.VMEM((experts, rows, width), BF16),
            pltpu.SemaphoreType.DMA((count, max(numbers))),
            pltpu.SemaphoreType.DMA((2, groups)),
        ],
        prefetch=1,
        flops=2 * experts * rows * (4 * hidden + tokens) * width,
        moved=4 * experts * hidden * width + 4 * experts * rows * width,
    )(place, meta, expert_gate, expert_up, grad_hidden, *arrays)
    return (result[0],) + sums_of(result[1:], count, groups, paired)


def expert_produce(
    place, hidden_rows, meta, expert_down, capacity, first, last, groups, paired, before=None
):
    experts, hidden, width = expert_down.shape
    count = meta.shape[0]
    tokens = meta.shape[-1]
    rows = count * capacity
    held = before.shape[0] if before is not None else 0

    def body(place_ref, meta_ref, h_ref, w_ref, *rest):
        expert = pl.program_id(0) + first
        result = dot_nn(h_ref[0], w_ref[0])
        if held:
            before_ref, outs, (ring, made, sem, before_sem) = rest[0], rest[1:-4], rest[-4:]
            copy = pltpu.make_async_copy(before_ref, made.at[pl.ds(0, held)], before_sem)

            @pl.when(expert == first)
            def _():
                copy.start()

        else:
            (out_ref,) = rest
        for m in range(count):
            named = one_hot(meta_ref[m, 0, pl.ds(expert, 1)], capacity)
            weight = jnp.sum(
                jnp.where(named, meta_ref[m, 1, pl.ds(expert, 1)], 0.0), axis=1, keepdims=True
            )
            at = slice(m * capacity, (m + 1) * capacity)
            value = (weight * result[at]).astype(BF16)
            if held:
                made[expert, at] = value
            else:
                out_ref[0, at] = value

        if held:

            @pl.when(expert == last - 1)
            def _():
                copy.wait()
                send_combined(
                    meta_ref, made, ring, sem, capacity,
                    lambda m: sum_targets(outs, place_ref, m, groups, paired),
                )

    if held:
        shapes = sum_shapes(count, tokens, width, groups, paired)
        out_specs = [ANYWHERE] * len(shapes)
    else:
        shapes = [shape_of((last - first, rows, width), BF16)]
        out_specs = [pl.BlockSpec((1, rows, width), lambda e, s: (e, 0, 0))]
    result = kernel_call(
        body,
        "expert_produce",
        (last - first,),
        [
            whole_block(meta.shape),
            pl.BlockSpec((1, rows, hidden), lambda e, s: (e + first, 0, 0)),
            pl.BlockSpec((1, hidden, width), lambda e, s: (e + first, 0, 0)),
        ]
        + ([ANYWHERE] if held else []),
        out_specs,
        shapes,
        scratch=[
            pltpu.VMEM((2, tokens, width), BF16),
            pltpu.VMEM((experts, rows, width), BF16),
            pltpu.SemaphoreType.DMA((2, groups)),
            pltpu.SemaphoreType.DMA,
        ]
        if held
        else [],
        prefetch=1,
        flops=2 * (last - first) * rows * hidden * width,
        moved=2 * experts * hidden * width + 2 * experts * rows * width,
    )(place, meta, hidden_rows, expert_down, *([before] if held else []))
    return sums_of(result, count, groups, paired) if held else result[0]


def project_out_back(pieces, mixed, upstream, gain, w_out, down, up, attended, mids):
    splits, groups, shard, part = attended.shape
    width = splits * part
    rank = down.shape[1]
    rows = groups * shard
    number = len(pieces[0])

    def body(up_stream_ref, gain_ref, w_ref, down_ref, up_ref, mixed_ref, att_ref, mid_ref, *rest):
        refs, rest = rest[: groups * number], rest[groups * number :]
        gm_ref, gdown_ref, gup_ref, out_ref, low, held, sem = rest
        copies = [
            pltpu.make_async_copy(w_ref.at[pl.ds(z * part, part)], held.at[z], sem.at[z])
            for z in range(splits)
        ]
        for copy in copies:
            copy.start()
        smalls = []
        for g in range(groups):
            total = refs[g * number][...].astype(F32)
            for ref in refs[g * number + 1 : (g + 1) * number]:
                total += ref[...].astype(F32)
            grad = up_stream_ref[g].astype(F32) + norm_back(mixed_ref[g], gain_ref[...], total)
            gm_ref[g] = grad
            grad = grad.astype(BF16)
            low[g * shard : (g + 1) * shard] = grad
            small = (ADAPTER_SCALE * dot_nt(up_ref[g], grad)).astype(BF16)
            smalls.append(small)
            gup_ref[g] = (ADAPTER_SCALE * dot_nn(mid_ref[g], grad)).astype(BF16)
        for z in range(splits):
            columns = slice(z * part, (z + 1) * part)
            copies[z].wait()
            result = dot_nt(low[...], held[z])
            for g in range(groups):
                out_ref[z, g] = (
                    result[g * shard : (g + 1) * shard] + dot_tn(smalls[g], down_ref[g, :, columns])
                ).astype(BF16)
                gdown_ref[g, :, columns] = dot_nn(smalls[g], att_ref[z, g]).astype(BF16)

    return kernel_call(
        body,
        "project_out_back",
        (1,),
        [
            whole_block(upstream.shape),
            whole_block((1, width)),
            ANYWHERE,
            whole_block(down.shape),
            whole_block(up.shape),
            whole_block(mixed.shape),
            whole_block(attended.shape),
            whole_block(mids.shape),
        ]
        + [whole_block((shard, width))] * (groups * number),
        [
            whole_block((groups, shard, width)),
            whole_block((groups, rank, width)),
            whole_block((groups, rank, width)),
            whole_block(attended.shape),
        ],
        [
            shape_of((groups, shard, width), F32),
            shape_of((groups, rank, width), BF16),
            shape_of((groups, rank, width), BF16),
            shape_of(attended.shape, BF16),
        ],
        scratch=[
            pltpu.VMEM((rows, width), BF16),
            pltpu.VMEM((splits, part, width), BF16),
            pltpu.SemaphoreType.DMA((splits,)),
        ],
        flops=2 * rows * width * width,
        moved=2 * width * width,
    )(
        upstream, gain, w_out, down, up, mixed, attended, mids,
        *[array for found in pieces for array in found],
    )


def adapter_grads(place, group, grads, normed, ups, into):
    listed = is_list(grads)
    splits, (_, shard, part) = piece_shape(grads)
    width = splits * part
    own = ups.shape[1]
    devices = into.shape[0]
    rank = own // 3
    slice_width = width // devices

    def body(place_ref, normed_ref, up_ref, *rest):
        refs, (_, small_ref, down_ref, low) = rest[:splits], rest[splits:]
        for which in range(3):
            for r in range(splits):
                owner = lax.rem(place_ref[0] + r, splits) if listed else r
                low[:, pl.ds(pl.multiple_of(owner * part, part), part)] = refs[r][which]
            at = slice(which * rank, (which + 1) * rank)
            small = (ADAPTER_SCALE * dot_nt(up_ref[at], low[...])).astype(BF16)
            small_ref[at] = small
            result = dot_nn(small, normed_ref[...]).astype(BF16)
            for e in range(devices):
                down_ref[e, at] = result[:, e * slice_width : (e + 1) * slice_width]

    return kernel_call(
        body,
        "adapter_grads",
        (1,),
        [
            pl.BlockSpec((shard, width), lambda i, s: (group, 0)),
            group_block(ups.shape, group),
        ]
        + piece_specs(grads, (3, shard, part), lambda i, s: (0, 0, 0))
        + [ANYWHERE],
        [
            whole_block((own, shard)),
            pl.BlockSpec((devices, None, own, slice_width), lambda i, s: (0, group, 0, 0)),
        ],
        [shape_of((own, shard), BF16), shape_of(into.shape, BF16)],
        scratch=[pltpu.VMEM((shard, width), BF16)],
        prefetch=1,
        aliases={3 + splits: 1},
        flops=12 * shard * rank * width,
        moved=6 * shard * width,
    )(place, normed, ups, *piece_arrays(grads, splits), into)


def project_first_back(group, grads, smalls, downs, w_qkv, tokens, gain, grad_mixed, into=None):
    splits, _, shard, part = grads.shape
    width = splits * part
    rank = downs.shape[1] // 3
    groups = tokens.shape[0]

    def body(down_ref, w_ref, tok_ref, gain_ref, mixed_ref, small_ref, grad_ref, *rest):
        out_ref, low, held, sem = rest[-4:]

        def copy(p, i):
            at = pl.ds(i * part, part)
            return pltpu.make_async_copy(w_ref.at[p, at], held.at[p, at], sem.at[p, i])

        for p in range(3):
            for i in range(splits):
                copy(p, i).start()
        totals = [None] * splits
        for p in range(3):
            for z in range(splits):
                low[:, z * part : (z + 1) * part] = grad_ref[z, p]
            at = slice(p * rank, (p + 1) * rank)
            small = dot_tn(small_ref[at], down_ref[at])
            for i in range(splits):
                copy(p, i).wait()
                columns = slice(i * part, (i + 1) * part)
                result = dot_nt(low[...], held[p, columns]) + small[:, columns]
                totals[i] = result if p == 0 else totals[i] + result
        total = jnp.concatenate(totals, axis=1)
        out_ref[...] = mixed_ref[...] + norm_back(tok_ref[...].astype(F32), gain_ref[...], total)

    return kernel_call(
        body,
        "project_first_back",
        (1,),
        [
            group_block(downs.shape, group),
            ANYWHERE,
            group_block(tokens.shape, group),
            whole_block((1, width)),
            group_block(grad_mixed.shape, group),
            whole_block((3 * rank, shard)),
            whole_block(grads.shape),
        ]
        + ([ANYWHERE] if into is not None else []),
        pl.BlockSpec((None, shard, width), lambda i: (group, 0, 0)),
        shape_of((groups, shard, width), F32),
        scratch=[
            pltpu.VMEM((shard, width), BF16),
            pltpu.VMEM((3, width, width), BF16),
            pltpu.SemaphoreType.DMA((3, splits)),
        ],
        aliases={7: 0} if into is not None else None,
        flops=6 * shard * width * width,
        moved=6 * width * width,
    )(
        downs, w_qkv, tokens, gain, grad_mixed, smalls, grads,
        *([into] if into is not None else []),
    )


def local(
    tokens,
    cotangent,
    lengths,
    adapter_choice,
    expert_ids,
    gate_weights,
    attn_gain,
    moe_gain,
    query_gain,
    key_gain,
    w_qkv,
    w_out,
    expert_gate,
    expert_up,
    expert_down,
    adapt_down,
    first_down,
    second_down,
    adapt_up,
    first_up,
    second_up,
):
    groups, shard, width = tokens.shape
    splits = lax.axis_size("seq")
    devices = lax.axis_size("exp")
    here = lax.axis_index("seq")
    total = shard * splits
    part = width // splits
    rows = groups * shard
    sets, projections, slice_width, rank = adapt_down.shape
    local_experts = expert_gate.shape[0]
    experts = local_experts * devices
    top = expert_ids.shape[-1]
    capacity = 3 * rows * top // (2 * experts)
    listed = [False] * groups

    position = lax.axis_index("exp")
    place = jnp.stack([here, position]).astype(jnp.int32)
    flat_tokens = tokens.reshape(rows, width)
    gain_row = attn_gain.reshape(1, width)
    moe_row = moe_gain.reshape(1, width)
    query_row = query_gain.reshape(1, HEAD)
    key_row = key_gain.reshape(1, HEAD)

    paired = devices == 8 and groups == 2
    own_positions = here * shard + jnp.arange(shard, dtype=jnp.int32)
    own_live = own_positions[None, :] < lengths[:, None]

    base, _, normed = project_first(
        place, flat_tokens, gain_row, w_qkv, groups, splits, listed
    )
    raw = [forward_seq(base[0])]

    adapt_down_low, adapt_up_low, ids, gates = after(
        (adapt_down, adapt_up, expert_ids, gate_weights), normed
    )
    ids = ids.reshape(rows, top).T
    gates = gates.reshape(rows, top).T
    choice = adapter_choice.astype(F32).reshape(1, groups * sets)
    choice = jnp.pad(choice, ((0, 0), (0, rows - groups * sets)))
    routed = route(ids, gates, choice, experts)
    down_rows = jnp.swapaxes(adapt_down_low.astype(BF16), 2, 3)
    up_rows = adapt_up_low.astype(BF16)
    own = 3 * rank
    blocks = [
        jnp.concatenate([found.reshape(-1, slice_width) for found in sources])
        for sources in (
            (down_rows[:, :3], down_rows[:, 3], routed),
            (up_rows[:, :3], up_rows[:, 3]),
        )
    ]
    if paired:
        all_blocks = gather_far(blocks, gather_near(blocks))
        all_downs, all_ups = ([found[g] for found in all_blocks] for g in range(2))
    else:
        cut = blocks[0].shape[0]
        all_downs = [found[0][:cut] for found in gather_whole(blocks)]
        all_ups = [found[0][cut:] for found in gather_whole(blocks)]
    chosen = jnp.sum(adapter_choice * jnp.arange(sets, dtype=jnp.int32)[None, :], axis=1)
    picks = jnp.concatenate([chosen, position.reshape(1)]).astype(jnp.int32)
    sections = [(0, own), (sets * own, rank)]
    downs, out_downs, mids = pick_sets(all_downs, picks, groups, sections, normed)
    ups, out_ups, _ = pick_sets(after(all_ups, mids), picks, groups, sections, normed)
    all_mids = by_distance(jnp.stack(forward_seq([mids] * splits)))

    live_rows = after(own_live, mids)
    upstream = jnp.where(live_rows[:, :, None], cotangent, jnp.zeros((), BF16))
    upstream = [upstream[g] for g in range(groups)]
    routes = jnp.stack([found[sets * (own + rank) :] for found in after(all_downs, mids)])
    routes = routes.reshape(devices, 3 * experts + 16, rows)
    choices = by_relative(routes[:, 3 * experts, : groups * sets])
    choices = choices.reshape(devices, groups, sets)
    meta = routes[:, : 3 * experts].reshape(devices, 3, experts, rows)
    meta = lax.dynamic_slice_in_dim(meta, position * local_experts, local_experts, axis=2)
    meta = meta.astype(F32)
    meta = jnp.stack([meta[:, 0], meta[:, 1] + meta[:, 2]], axis=1)
    blocks = jnp.arange(splits, dtype=jnp.int32)
    frequency = ROPE_BASE ** (-(2.0 / HEAD) * jnp.arange(HEAD // 2, dtype=F32))
    tables = []
    for g in range(groups):
        positions = blocks[:, None] * shard + jnp.arange(shard, dtype=jnp.int32)[None, :]
        angles = after(positions, normed).reshape(total, 1).astype(F32) * frequency[None, :]
        cosine, sine = jnp.cos(angles), jnp.sin(angles)
        tables.append(
            (
                positions.reshape(1, total),
                jnp.concatenate([cosine, cosine], axis=1),
                jnp.concatenate([-sine, sine], axis=1),
            )
        )

    raw[0], all_mids, meta, choices, tables = lax.optimization_barrier(
        (raw[0], all_mids, meta, choices, tables)
    )
    for g in range(1, groups):
        raw.append(forward_seq(after(base[g], raw[g - 1])))
    own_ups = lax.dynamic_slice_in_dim(ups, here * part, part, axis=2)
    own_ups = own_ups.reshape(groups, 3, rank, part)

    saved, heads_rows = [], []
    for g in range(groups):
        if g:
            raw[g] = after(raw[g], heads_rows)
        att, kept = attend(
            lengths[g : g + 1],
            raw[g],
            all_mids[:, g],
            own_ups[g],
            query_row,
            key_row,
            *tables[g],
        )
        saved.append(kept)
        heads_rows.append(att)
        if paired and g == 0:
            near = gather_near(upstream)
            far = far_of(after(near, att))
            cot_rows = gather_far(upstream, near, far)
    if not paired:
        cot_rows = gather_whole(upstream)
    heads_rows = jnp.stack(heads_rows, axis=1)
    if paired:
        heads_rows, cot_rows = lax.optimization_barrier((heads_rows, cot_rows))
    attended = lax.all_to_all(heads_rows, "seq", 0, 0)
    grad_hidden = expert_grad_hidden(
        cot_rows, after(meta, heads_rows), expert_down, capacity
    )
    attended, grad_hidden = lax.optimization_barrier((attended, grad_hidden))
    mixed, mid_out, moe_rows = project_out(
        attended, w_out, out_downs, out_ups, tokens, moe_row
    )
    gathered = gather_far(moe_rows, gather_near(moe_rows)) if paired else gather_whole(moe_rows)
    half = local_experts // 2

    hidden, parts, others = expert_middle(
        place,
        gathered,
        meta,
        expert_gate,
        expert_up,
        grad_hidden,
        capacity,
        groups,
        paired,
    )
    if paired:
        far, near, beside = near_sums_of(parts, others)
        produced = expert_produce(
            place, after(hidden, far, near), meta, expert_down, capacity, 0, half, groups, paired
        )
        far, near = send_near(far, near)
        far, produced = lax.optimization_barrier((far, produced))
        joined = send_joined(joined_sums_of(parts, beside, far))
        grad_pieces = [
            [parts[0][g], beside[0][g], near[g], joined[g]] for g in range(groups)
        ]
    else:
        summed = lax.psum_scatter(parts, "exp").reshape(groups, shard, width)
        grad_pieces = [[summed[g]] for g in range(groups)]
        produced = expert_produce(
            place, hidden, meta, expert_down, capacity, 0, half, groups, paired
        )
    grad_mixed, grad_out_downs, grad_out_ups, grad_att = project_out_back(
        grad_pieces, mixed, jnp.stack(upstream), moe_row, w_out, out_downs, out_ups, attended, mid_out
    )
    out_parts, out_others = expert_produce(
        place, hidden, after(meta, grad_mixed), expert_down, capacity, half, local_experts,
        groups, paired, produced,
    )
    grad_att = lax.all_to_all(grad_att, "seq", 0, 0)
    grad_raw, gups = [], []
    for g in range(groups):
        if g:
            grad_att = after(grad_att, gups)
        back, gup = attend_back(
            lengths[g : g + 1],
            grad_att,
            g,
            saved[g],
            all_mids[:, g],
            rank,
            query_row,
            key_row,
            *tables[g],
        )
        gups.append(gup)
        if paired and not g:
            out_far, out_near, out_beside = near_sums_of(out_parts, after(out_others, gup))
        if paired and g:
            out_far, out_near = send_near(out_far, out_near)
            back, out_far, out_near = lax.optimization_barrier((back, out_far, out_near))
        grad_raw.append(forward_seq(after(back, grad_raw) if g else back))
    if paired:
        joined_sums = joined_sums_of(out_parts, out_beside, out_far)
        out_joined = send_joined(joined_sums)
        normed = after(normed, joined_sums)
    gups = jnp.stack(after(gups, grad_raw[0]))
    wide_ups = lax.dynamic_update_slice_in_dim(
        jnp.zeros((groups, own, width), BF16), gups, here * part, axis=2
    )
    early = jnp.concatenate([grad_out_downs, wide_ups, grad_out_ups], axis=1)
    early = jnp.moveaxis(early.reshape(groups, -1, devices, slice_width), 2, 0)

    late = jnp.pad(early, ((0, 0), (0, 0), (own, 0), (0, 0)))
    grad_input = None
    for g in range(groups):
        small, late = adapter_grads(place, g, grad_raw[g], normed, ups, late)
        if g == groups - 1:
            late = lax.all_to_all(late, "exp", 0, 0)
        grad_input = project_first_back(
            g, grad_raw[g], small, downs, w_qkv, tokens, gain_row, grad_mixed, grad_input
        )
        if g < groups - 1:
            late, grad_input = lax.optimization_barrier((late, grad_input))
            if paired:
                outputs = [
                    mixed[g]
                    + functools.reduce(
                        jnp.add,
                        [
                            value.astype(F32)
                            for value in (out_parts[0][g], out_beside[0][g], out_near[g], out_joined[g])
                        ],
                    )
                    for g in range(groups)
                ]
                output = jnp.stack(outputs).astype(BF16)
            else:
                out_sum = lax.psum_scatter(out_parts, "exp").reshape(groups, shard, width)
                output = (mixed + out_sum.astype(F32)).astype(BF16)
            late, output = lax.optimization_barrier((late, output))
    late, grad_input = lax.optimization_barrier((late, grad_input))
    pieces = jnp.einsum("dgk,dgrw->krw", choices, late, preferred_element_type=F32)
    pieces = pieces.astype(BF16)
    pieces = pieces.reshape(splits, -1, slice_width)
    order = (here + jnp.arange(splits)) % splits
    pieces = list(jnp.take(pieces, order, axis=0))
    summed = add_low(*forward_seq(pieces))
    in_sets = by_distance(jnp.stack(forward_seq([summed] * splits)))
    in_sets = in_sets.reshape(sets, 2, projections, rank, slice_width).astype(F32)
    shard_down = jnp.swapaxes(in_sets[:, 0], 2, 3)
    shard_up = in_sets[:, 1]
    new_first_down, new_second_down, new_down = adam_update(
        adapt_down, shard_down, first_down, second_down, RATE_DOWN
    )
    new_first_up, new_second_up, new_up = adam_update(
        adapt_up, shard_up, first_up, second_up, RATE_UP
    )
    return (
        output,
        grad_input,
        new_first_down,
        new_second_down,
        new_down,
        new_first_up,
        new_second_up,
        new_up,
    )


def solution(mesh):
    in_specs = (
        P("exp", "seq", None),
        P("exp", "seq", None),
        P("exp"),
        P("exp", None),
        P("exp", "seq", None, None, None),
        P("exp", "seq", None, None, None),
        P(),
        P(),
        P(),
        P(),
        P(),
        P(),
        P("exp", None, None),
        P("exp", None, None),
        P("exp", None, None),
        P(None, None, "exp", None),
        P(None, None, "exp", None),
        P(None, None, "exp", None),
        P(None, None, None, "exp"),
        P(None, None, None, "exp"),
        P(None, None, None, "exp"),
    )
    out_specs = (
        P("exp", "seq", None),
        P("exp", "seq", None),
        P(None, None, "exp", None),
        P(None, None, "exp", None),
        P(None, None, "exp", None),
        P(None, None, None, "exp"),
        P(None, None, None, "exp"),
        P(None, None, None, "exp"),
    )
    return jax.shard_map(local, mesh=mesh, in_specs=in_specs, out_specs=out_specs, check_vma=False)
```

```python
import functools

import jax
import jax.numpy as jnp
from jax import lax
from jax.experimental import pallas as pl
from jax.experimental.pallas import tpu as pltpu
from jax.sharding import PartitionSpec as P

HEAD = 128
STEP = 5

NORM_EPS = 1e-05
ROPE_BASE = 50000.0
ADAPTER_SCALE = 0.5
BETA_FIRST = 0.5
BETA_SECOND = 0.5
RATE_DOWN = 0.02
RATE_UP = 0.2
WEIGHT_DECAY = 0.01
ADAM_EPS = 1e-08
MASKED = -1e30
SCORE_SCALE = HEAD ** (-0.5)

F32 = jnp.float32
BF16 = jnp.bfloat16
VMEM_LIMIT = 62 * 1024 * 1024
COST_SHARE = 0.01


def dot_nn(a, b):
    return lax.dot_general(a, b, (((1,), (0,)), ((), ())), preferred_element_type=F32)


def dot_nt(a, b):
    return lax.dot_general(a, b, (((1,), (1,)), ((), ())), preferred_element_type=F32)


def dot_tn(a, b):
    return lax.dot_general(a, b, (((0,), (0,)), ((), ())), preferred_element_type=F32)


def inverse_rms(values):
    return lax.rsqrt(jnp.mean(values * values, axis=-1, keepdims=True) + NORM_EPS)


def norm_back(values, gain, upstream):
    inverse = inverse_rms(values)
    scaled = upstream * gain
    return inverse * scaled - values * (inverse * inverse * inverse) * jnp.mean(
        values * scaled, axis=-1, keepdims=True
    )


def sigmoid(values):
    return 0.5 + 0.5 * jnp.tanh(0.5 * values)


def adam_update(weight, gradient, first, second, step_rate):
    new_first = BETA_FIRST * first + (1.0 - BETA_FIRST) * gradient
    new_second = BETA_SECOND * second + (1.0 - BETA_SECOND) * gradient * gradient
    first_hat = new_first / (1.0 - BETA_FIRST**STEP)
    second_hat = new_second / (1.0 - BETA_SECOND**STEP)
    new_weight = weight - step_rate * (
        first_hat / (jnp.sqrt(second_hat) + ADAM_EPS) + WEIGHT_DECAY * weight
    )
    return (new_first, new_second, new_weight)


def shape_of(shape, dtype):
    return jax.ShapeDtypeStruct(shape, dtype)


def whole_block(shape):
    rank = len(shape)
    return pl.BlockSpec(tuple(shape), lambda *_: (0,) * rank)


def kernel_call(
    body, name, grid, in_specs, out_specs, out_shape, scratch=(), prefetch=0, flops=0, moved=0,
    aliases=None,
):
    return pl.pallas_call(
        body,
        grid_spec=pltpu.PrefetchScalarGridSpec(
            num_scalar_prefetch=prefetch,
            grid=grid,
            in_specs=in_specs,
            out_specs=out_specs,
            scratch_shapes=list(scratch),
        ),
        out_shape=out_shape,
        input_output_aliases=aliases or {},
        name=name,
        cost_estimate=pl.CostEstimate(
            flops=int(flops * COST_SHARE), bytes_accessed=int(moved * COST_SHARE), transcendentals=0
        ),
        compiler_params=pltpu.CompilerParams(vmem_limit_bytes=VMEM_LIMIT),
    )


def swap(values, mask):
    count = lax.axis_size("exp")
    return lax.ppermute(values, "exp", [(i, i ^ mask) for i in range(count)])


def shift(values, distance):
    count = lax.axis_size("seq")
    return lax.ppermute(values, "seq", [(i, (i + distance) % count) for i in range(count)])


def shift_order():
    count = lax.axis_size("seq")
    return sorted(range(1, count), key=lambda r: -min(r, count - r))


def forward_seq(pieces):
    if not isinstance(pieces, (list, tuple)):
        return lax.all_to_all(pieces, "seq", 0, 0)
    came = {r: shift(pieces[r], r) for r in shift_order()}
    return [pieces[0]] + [came[r] for r in range(1, len(pieces))]


def backward_seq(pieces):
    if not isinstance(pieces, (list, tuple)):
        return lax.all_to_all(pieces, "seq", 0, 0)
    came = {r: shift(pieces[r], -r) for r in shift_order()}
    return [pieces[0]] + [came[r] for r in range(1, len(pieces))]


def tell_all(values, axis):
    count = lax.axis_size(axis)
    return lax.all_to_all(jnp.broadcast_to(values[None], (count,) + values.shape), axis, 0, 0)


def by_distance(stacked):
    count = lax.axis_size("seq")
    order = (lax.axis_index("seq") - jnp.arange(count)) % count
    return jnp.take(stacked, order, axis=0)


def by_relative(stacked):
    count = lax.axis_size("exp")
    return jnp.take(stacked, lax.axis_index("exp") ^ jnp.arange(count), axis=0)


STEP_HEADS = 1

WAYS = ((2, 4), (4, 2))


def gather_near(rows):
    near = {2: [None] * len(rows), 4: [None] * len(rows)}
    for g, (first, _) in enumerate(WAYS):
        near[first][g] = swap(rows[g], first)
    for g, (_, second) in enumerate(WAYS):
        near[second][g] = swap(rows[g], second)
    return near


def far_of(near):
    return [swap(near[first][g], second) for g, (first, second) in enumerate(WAYS)]


def gather_far(rows, near, far=None):
    far = far or far_of(near)
    found = []
    for blocks in (rows, near[2], near[4], far):
        found += [list(blocks), [swap(block, 1) for block in blocks]]
    return found


def gather_whole(rows):
    everything = by_relative(lax.all_gather(jnp.concatenate(rows), "exp"))
    return [[block] for block in everything]


def near_sums_of(parts, others):
    groups = len(parts[0])
    last = swap(others[1], 1).reshape((groups,) + parts[0][0].shape)
    beside = swap(others[0], 1).reshape((3, groups) + parts[0][0].shape)
    far = [add_low(parts[6][g], last[g]) for g in range(groups)]
    beside = after(beside, far)
    near = [add_low(parts[WAYS[g][0]][g], beside[WAYS[g][0] // 2][g]) for g in range(groups)]
    return far, near, beside


def send_near(far, near):
    far = [swap(far[g], WAYS[g][0]) for g in range(len(far))]
    return far, [swap(near[g], WAYS[g][0]) for g in range(len(near))]


def joined_sums_of(parts, beside, far):
    return [
        add_low(parts[WAYS[g][1]][g], beside[WAYS[g][1] // 2][g], far[g]) for g in range(len(far))
    ]


def send_joined(joined):
    return [swap(joined[g], WAYS[g][1]) for g in range(len(joined))]


def add_low(*values):
    return functools.reduce(jnp.add, [value.astype(F32) for value in values]).astype(BF16)


def after(values, *first):
    return lax.optimization_barrier((values, first))[0]


ANYWHERE = pl.BlockSpec(memory_space=pl.ANY)


def group_block(shape, group):
    rank = len(shape) - 1
    return pl.BlockSpec((None,) + tuple(shape[1:]), lambda *_: (group,) + (0,) * rank)


def is_list(pieces):
    return isinstance(pieces, (list, tuple))


def piece_shape(pieces):
    if is_list(pieces):
        return len(pieces), pieces[0].shape
    return pieces.shape[0], pieces.shape[1:]


def piece_arrays(pieces, splits):
    return list(pieces) if is_list(pieces) else [pieces] * splits


def piece_specs(pieces, block, index):
    if is_list(pieces):
        return [pl.BlockSpec(block, index)] * len(pieces)
    return [
        pl.BlockSpec((None,) + tuple(block), lambda *at, r=r: (r,) + tuple(index(*at)))
        for r in range(pieces.shape[0])
    ]


def out_specs_of(listed, splits, block, index):
    if listed:
        return [pl.BlockSpec(block, index)] * splits
    return [pl.BlockSpec((splits,) + tuple(block), lambda *at: (0,) + tuple(index(*at)))]


def out_shapes_of(listed, splits, shape, dtype):
    if listed:
        return [shape_of(shape, dtype)] * splits
    return [shape_of((splits,) + tuple(shape), dtype)]


def out_refs_of(listed, refs):
    return list(refs) if listed else [refs[0].at[r] for r in range(refs[0].shape[0])]


def out_pieces_of(listed, results):
    return list(results) if listed else results[0]


def project_first(place, tokens, gain, w_qkv, groups, splits, listed):
    rows, width = tokens.shape
    part = width // splits
    shard = rows // groups
    counts = [splits if listed[g] else 1 for g in range(groups)]
    total = sum(counts)

    def body(place_ref, tok_ref, gain_ref, w_ref, *rest):
        outs = rest[:total]
        parts_ref, normed_ref, held, sem = rest[total:]
        which = pl.program_id(0)

        def owner(r):
            return lax.rem(place_ref[0] + r, splits)

        def copy(p, r):
            columns = pl.ds(pl.multiple_of(owner(r) * part, part), part)
            return pltpu.make_async_copy(
                w_ref.at[p, :, columns],
                held.at[p, :, pl.ds(r * part, part)],
                sem.at[p, r],
            )

        @pl.when(which == 0)
        def _():
            for p in range(3):
                for r in range(splits):
                    copy(p, r).start()
            values = tok_ref[...].astype(F32)
            low = (values * inverse_rms(values) * gain_ref[...]).astype(BF16)
            normed_ref[...] = low
            for z in range(splits):
                for g in range(groups):
                    parts_ref[z, g] = low[
                        g * shard : (g + 1) * shard, z * part : (z + 1) * part
                    ]

        for r in range(splits):
            copy(which, r).wait()
            result = dot_nn(normed_ref[...], held[which, :, r * part : (r + 1) * part])
            first = 0
            for g in range(groups):
                low = result[g * shard : (g + 1) * shard].astype(BF16)
                if listed[g]:
                    outs[first + r][0] = low
                else:
                    outs[first][owner(r), 0] = low
                first += counts[g]

    specs, shapes = [], []
    for g in range(groups):
        specs += out_specs_of(listed[g], splits, (1, shard, part), lambda p, s: (p, 0, 0))
        shapes += out_shapes_of(listed[g], splits, (3, shard, part), BF16)
    result = kernel_call(
        body,
        "project_first",
        (3,),
        [whole_block((rows, width)), whole_block((1, width)), ANYWHERE],
        specs + [whole_block((splits, groups, shard, part)), whole_block((rows, width))],
        shapes
        + [shape_of((splits, groups, shard, part), BF16), shape_of((rows, width), BF16)],
        scratch=[
            pltpu.VMEM((3, width, width), BF16),
            pltpu.SemaphoreType.DMA((3, splits)),
        ],
        prefetch=1,
        flops=6 * rows * width * width,
        moved=6 * width * width,
    )(place, tokens, gain, w_qkv)
    outs, first = [], 0
    for g in range(groups):
        outs.append(out_pieces_of(listed[g], result[first : first + counts[g]]))
        first += counts[g]
    return outs, result[total], result[total + 1]


def pick_sets(gathered, picks, groups, sections, normed):
    count = len(gathered)
    part = gathered[0].shape[1]
    width = count * part
    shard = normed.shape[0] // groups
    number = len(sections)

    def body(pick_ref, normed_ref, *rest):
        refs, outs, sem = rest[:count], rest[count:-1], rest[-1]
        copies = []
        for g in range(groups):
            for i, (first, own) in enumerate(sections):
                for m in range(count):
                    columns = pl.ds(pl.multiple_of((pick_ref[groups] ^ m) * part, part), part)
                    copies.append(
                        pltpu.make_async_copy(
                            refs[m].at[pl.ds(pl.multiple_of(first + pick_ref[g] * own, own), own)],
                            outs[i].at[g, :, columns],
                            sem.at[(g * number + i) * count + m],
                        )
                    )
        for copy in copies:
            copy.start()
        for copy in copies:
            copy.wait()
        for g in range(groups):
            outs[number][g] = dot_nt(
                outs[0][g], normed_ref[g * shard : (g + 1) * shard]
            ).astype(BF16)

    shapes = [(groups, own, width) for _, own in sections]
    shapes.append((groups, sections[0][1], shard))
    return kernel_call(
        body,
        "pick_sets",
        (1,),
        [whole_block(normed.shape)] + [ANYWHERE] * count,
        [whole_block(shape) for shape in shapes],
        [shape_of(shape, BF16) for shape in shapes],
        scratch=[pltpu.SemaphoreType.DMA((groups * number * count,))],
        prefetch=1,
        moved=4 * groups * width * sum(own for _, own in sections),
    )(picks, normed, *gathered)


def route(ids, gates, choice, experts):
    top, tokens = ids.shape

    def body(ids_ref, gates_ref, choice_ref, out_ref):
        expert = lax.broadcasted_iota(jnp.int32, (experts, tokens), 0)
        weights = jnp.zeros((experts, tokens), F32)
        named = jnp.zeros((experts, tokens), F32)
        for k in range(top):
            hit = expert == ids_ref[k : k + 1]
            weights = jnp.where(hit, gates_ref[k : k + 1], weights)
            named = jnp.where(hit, 1.0, named)
        earlier = lax.broadcasted_iota(jnp.int32, (tokens, tokens), 0) < lax.broadcasted_iota(
            jnp.int32, (tokens, tokens), 1
        )
        ranks = dot_nn(named.astype(BF16), jnp.where(earlier, 1.0, 0.0).astype(BF16))
        slots = jnp.where(named > 0.0, ranks, -1.0)
        front = weights.astype(BF16)
        out_ref[:experts] = slots.astype(BF16)
        out_ref[experts : 2 * experts] = front
        out_ref[2 * experts : 3 * experts] = (weights - front.astype(F32)).astype(BF16)
        out_ref[3 * experts :] = jnp.broadcast_to(choice_ref[...], (16, tokens)).astype(BF16)

    shape = (3 * experts + 16, tokens)
    return kernel_call(
        body,
        "route",
        (1,),
        [whole_block(ids.shape), whole_block(gates.shape), whole_block(choice.shape)],
        whole_block(shape),
        shape_of(shape, BF16),
        moved=12 * experts * tokens,
    )(ids, gates, choice)


def rotate(values, cosine, sine):
    return values * cosine + pltpu.roll(values, HEAD // 2, 1) * sine


def rotate_back(values, cosine, sine):
    return values * cosine - pltpu.roll(values, HEAD // 2, 1) * sine


def softmax_rows(queries, keys, live):
    scores = jnp.where(live, dot_nt(queries, keys) * SCORE_SCALE, MASKED)
    exponent = jnp.exp(scores - jnp.max(scores, axis=-1, keepdims=True))
    return exponent * (1.0 / jnp.sum(exponent, axis=-1, keepdims=True))


def attend(length, raw, mids, ups, query_gain, key_gain, positions, cosine, sine):
    listed = is_list(raw)
    splits, (_, shard, part) = piece_shape(raw)
    rank = ups.shape[1]
    total = splits * shard
    heads = part // HEAD
    step_heads = min(heads, STEP_HEADS)

    def body(len_ref, up_ref, qg_ref, kg_ref, pos_ref, cos_ref, sin_ref, *rest):
        raw_refs, mid_ref = rest[:splits], rest[splits]
        att_refs = out_refs_of(listed, rest[splits + 1 : -5])
        q_ref, k_ref, v_ref, rq_ref, rk_ref = rest[-5:]

        mids = [
            jnp.concatenate(
                [mid_ref[r, which * rank : (which + 1) * rank] for r in range(splits)], axis=1
            )
            for which in range(3)
        ]
        cosine, sine = cos_ref[...], sin_ref[...]
        for h in range(step_heads):
            at = slice(h * HEAD, (h + 1) * HEAD)

            def full(which):
                base = jnp.concatenate([ref[which, :, at] for ref in raw_refs], axis=0)
                added = dot_tn(mids[which], up_ref[which, :, at])
                return base.astype(F32) + ADAPTER_SCALE * added

            raw_q, raw_k, raw_v = full(0), full(1), full(2)
            rq_ref[h] = raw_q
            rk_ref[h] = raw_k
            queries = rotate(raw_q * inverse_rms(raw_q) * qg_ref[...], cosine, sine).astype(BF16)
            keys = rotate(raw_k * inverse_rms(raw_k) * kg_ref[...], cosine, sine).astype(BF16)
            values = raw_v.astype(BF16)
            q_ref[h] = queries
            k_ref[h] = keys
            v_ref[h] = values
            weights = softmax_rows(queries, keys, pos_ref[...] < len_ref[0]).astype(BF16)
            result = dot_nn(weights, values).astype(BF16)
            for r in range(splits):
                att_refs[r][:, at] = result[r * shard : (r + 1) * shard]

    wide = step_heads * HEAD
    head_block = pl.BlockSpec((step_heads, total, HEAD), lambda h, s: (h, 0, 0))
    result = kernel_call(
        body,
        "attend",
        (heads // step_heads,),
        [
            pl.BlockSpec((3, rank, wide), lambda h, s: (0, 0, h)),
            whole_block((1, HEAD)),
            whole_block((1, HEAD)),
            whole_block((1, total)),
            whole_block((total, HEAD)),
            whole_block((total, HEAD)),
        ]
        + piece_specs(raw, (3, shard, wide), lambda h, s: (0, 0, h))
        + [whole_block(mids.shape)],
        out_specs_of(listed, splits, (shard, wide), lambda h, s: (0, h)) + [head_block] * 5,
        out_shapes_of(listed, splits, (shard, part), BF16)
        + [shape_of((heads, total, HEAD), BF16)] * 3
        + [shape_of((heads, total, HEAD), F32)] * 2,
        prefetch=1,
        flops=4 * heads * total * total * HEAD,
        moved=heads * total * HEAD * 24 + 4 * heads * total * total,
    )(length, ups, query_gain, key_gain, positions, cosine, sine, *piece_arrays(raw, splits), mids)
    return out_pieces_of(listed, result[:-5]), result[-5:]


def attend_back(length, grads, group, saved, mids, rank, query_gain, key_gain, positions, cosine, sine):
    listed = False
    splits, _, shard, part = grads.shape
    total = splits * shard
    heads = part // HEAD
    step_heads = min(heads, STEP_HEADS)

    def body(len_ref, qg_ref, kg_ref, pos_ref, cos_ref, sin_ref, *rest):
        grad_refs, mid_ref = rest[:splits], rest[splits]
        q_ref, k_ref, v_ref, rq_ref, rk_ref = rest[splits + 1 : splits + 6]
        out_refs = out_refs_of(listed, rest[splits + 6 : -1])
        gup_ref = rest[-1]
        cosine, sine = cos_ref[...], sin_ref[...]
        mids = [
            jnp.concatenate(
                [mid_ref[r, which * rank : (which + 1) * rank] for r in range(splits)], axis=1
            )
            for which in range(3)
        ]
        for h in range(step_heads):
            at = slice(h * HEAD, (h + 1) * HEAD)
            queries, keys, values = q_ref[h], k_ref[h], v_ref[h]
            grad = jnp.concatenate([ref[:, at] for ref in grad_refs], axis=0)
            weights = softmax_rows(queries, keys, pos_ref[...] < len_ref[0])
            grad_probs = dot_nt(grad, values)
            inner = jnp.sum(weights * grad_probs, axis=-1, keepdims=True)
            grad_scores = (weights * (grad_probs - inner)).astype(BF16)
            grad_q = dot_nn(grad_scores, keys) * SCORE_SCALE
            grad_k = dot_tn(grad_scores, queries) * SCORE_SCALE
            grad_v = dot_tn(weights.astype(BF16), grad)
            grad_q = norm_back(rq_ref[h], qg_ref[...], rotate_back(grad_q, cosine, sine))
            grad_k = norm_back(rk_ref[h], kg_ref[...], rotate_back(grad_k, cosine, sine))
            for which, value in enumerate((grad_q, grad_k, grad_v)):
                low = value.astype(BF16)
                for r in range(splits):
                    out_refs[r][which, :, at] = low[r * shard : (r + 1) * shard]
                gup_ref[which * rank : (which + 1) * rank, at] = (
                    ADAPTER_SCALE * dot_nn(mids[which], low)
                ).astype(BF16)

    wide = step_heads * HEAD
    head_block = pl.BlockSpec((step_heads, total, HEAD), lambda h, s: (h, 0, 0))
    result = kernel_call(
        body,
        "attend_back",
        (heads // step_heads,),
        [
            whole_block((1, HEAD)),
            whole_block((1, HEAD)),
            whole_block((1, total)),
            whole_block((total, HEAD)),
            whole_block((total, HEAD)),
        ]
        + [
            pl.BlockSpec((None, None, shard, wide), lambda h, s, r=r: (r, group, 0, h))
            for r in range(splits)
        ]
        + [whole_block(mids.shape)]
        + [head_block] * 5,
        out_specs_of(listed, splits, (3, shard, wide), lambda h, s: (0, 0, h))
        + [pl.BlockSpec((3 * rank, wide), lambda h, s: (0, h))],
        out_shapes_of(listed, splits, (3, shard, part), BF16)
        + [shape_of((3 * rank, part), BF16)],
        prefetch=1,
        flops=10 * heads * total * total * HEAD,
        moved=heads * total * HEAD * 24 + 8 * heads * total * total,
    )(length, query_gain, key_gain, positions, cosine, sine, *[grads] * splits, mids, *saved)
    return out_pieces_of(listed, result[:-1]), result[-1]


def project_out(attended, w_out, down, up, tokens, gain):
    splits, groups, shard, part = attended.shape
    width = splits * part
    rank = down.shape[1]
    rows = groups * shard

    def body(att_ref, w_ref, down_ref, up_ref, tok_ref, gain_ref, *rest):
        mixed_ref, mid_ref = rest[:2]
        moe_refs = rest[2 : 2 + groups]
        att, held, sem = rest[2 + groups :]
        copies = [
            pltpu.make_async_copy(
                w_ref.at[pl.ds(i * part, part)], held.at[pl.ds(i * part, part)], sem.at[i]
            )
            for i in range(splits)
        ]
        for copy in copies:
            copy.start()
        adapter = []
        for g in range(groups):
            at = slice(g * shard, (g + 1) * shard)
            for z in range(splits):
                att[at, z * part : (z + 1) * part] = att_ref[z, g]
            mid = dot_nt(down_ref[g], att[at]).astype(BF16)
            mid_ref[g] = mid
            adapter.append(
                tok_ref[g].astype(F32) + ADAPTER_SCALE * dot_tn(mid, up_ref[g])
            )
        total = jnp.concatenate(adapter, axis=0)
        for i, copy in enumerate(copies):
            copy.wait()
            total += dot_nn(att[:, i * part : (i + 1) * part], held[i * part : (i + 1) * part])
        low = (total * inverse_rms(total) * gain_ref[...]).astype(BF16)
        for g in range(groups):
            mixed_ref[g] = total[g * shard : (g + 1) * shard]
            moe_refs[g][...] = low[g * shard : (g + 1) * shard]

    result = kernel_call(
        body,
        "project_out",
        (1,),
        [
            whole_block(attended.shape),
            ANYWHERE,
            whole_block(down.shape),
            whole_block(up.shape),
            whole_block(tokens.shape),
            whole_block((1, width)),
        ],
        [
            whole_block((groups, shard, width)),
            whole_block((groups, rank, shard)),
        ]
        + [whole_block((shard, width))] * groups,
        [shape_of((groups, shard, width), F32), shape_of((groups, rank, shard), BF16)]
        + [shape_of((shard, width), BF16)] * groups,
        scratch=[
            pltpu.VMEM((rows, width), BF16),
            pltpu.VMEM((width, width), BF16),
            pltpu.SemaphoreType.DMA((splits,)),
        ],
        flops=2 * rows * width * width,
        moved=2 * width * width,
    )(attended, w_out, down, up, tokens, gain)
    return result[0], result[1], result[2:]


def one_hot(slot_row, capacity):
    tokens = slot_row.shape[1]
    index = lax.broadcasted_iota(jnp.int32, (capacity, tokens), 0).astype(F32)
    return index == slot_row


def pick_rows(sources, meta_ref, ring, sem, picked, capacity, weigh, begin=0):
    count = meta_ref.shape[0]
    experts = picked.shape[0]
    slots = ring.shape[0]

    def copies(m):
        found = sources(m)
        size = ring.shape[1] // len(found)
        return [
            pltpu.make_async_copy(
                ref, ring.at[m % slots, pl.ds(i * size, size)], sem.at[m, i]
            )
            for i, ref in enumerate(found)
        ]

    for m in range(slots):
        for copy in copies(m):
            copy.start()
    for m in range(count):
        named = jnp.concatenate(
            [one_hot(meta_ref[m, 0, e : e + 1], capacity) for e in range(begin, begin + experts)], axis=0
        )
        for copy in copies(m):
            copy.wait()
        result = dot_nn(named.astype(BF16), ring[m % slots])
        if weigh:
            weights = jnp.concatenate(
                [
                    jnp.broadcast_to(meta_ref[m, 1, e : e + 1], (capacity, named.shape[1]))
                    for e in range(begin, begin + experts)
                ],
                axis=0,
            )
            result = result * jnp.sum(jnp.where(named, weights, 0.0), axis=1, keepdims=True)
        low = result.astype(BF16)
        for e in range(experts):
            picked[e, m * capacity : (m + 1) * capacity] = low[e * capacity : (e + 1) * capacity]
        if m + slots < count:
            for copy in copies(m + slots):
                copy.start()


def expert_grad_hidden(gathered, meta, expert_down, capacity):
    experts, hidden, width = expert_down.shape
    numbers = [len(found) for found in gathered]
    arrays = [array for found in gathered for array in found]
    count = meta.shape[0]
    tokens = meta.shape[-1]
    rows = count * capacity

    def body(meta_ref, w_ref, *rest):
        refs, (out_ref, ring, picked, sem) = rest[: len(arrays)], rest[len(arrays) :]
        expert = pl.program_id(0)

        @pl.when(expert == 0)
        def _():
            pick_rows(
                lambda m: refs[sum(numbers[:m]) : sum(numbers[: m + 1])],
                meta_ref, ring, sem, picked, capacity, True,
            )

        out_ref[0] = dot_nt(picked[expert], w_ref[0]).astype(BF16)

    return kernel_call(
        body,
        "expert_grad_hidden",
        (experts,),
        [
            whole_block(meta.shape),
            pl.BlockSpec((1, hidden, width), lambda e: (e, 0, 0)),
        ]
        + [ANYWHERE] * len(arrays),
        pl.BlockSpec((1, rows, hidden), lambda e: (e, 0, 0)),
        shape_of((experts, rows, hidden), BF16),
        scratch=[
            pltpu.VMEM((4, tokens, width), BF16),
            pltpu.VMEM((experts, rows, width), BF16),
            pltpu.SemaphoreType.DMA((count, max(numbers))),
        ],
        flops=2 * experts * rows * (hidden + tokens) * width,
        moved=2 * experts * hidden * width + 2 * count * tokens * width,
    )(meta, expert_down, *arrays)


def combine_rows(meta_ref, picked, m, capacity):
    experts, _, width = picked.shape
    named = jnp.concatenate(
        [one_hot(meta_ref[m, 0, e : e + 1], capacity) for e in range(experts)], axis=0
    )
    named = jnp.where(named, 1.0, 0.0).T.astype(BF16)
    held = jnp.concatenate(
        [picked[e, m * capacity : (m + 1) * capacity] for e in range(experts)], axis=0
    )
    return dot_nn(named, held)


def send_combined(meta_ref, picked, ring, sem, capacity, targets):
    count = meta_ref.shape[0]
    tokens = ring.shape[1]
    slots = ring.shape[0]
    waiting = {}
    for i, m in enumerate(reversed(range(count))):
        for copy in waiting.pop(i - slots, []):
            copy.wait()
        ring[i % slots] = combine_rows(meta_ref, picked, m, capacity).astype(BF16)
        found = targets(m)
        size = tokens // len(found)
        waiting[i] = [
            pltpu.make_async_copy(
                ring.at[i % slots, pl.ds(b * size, size)], ref, sem.at[i % slots, b]
            )
            for b, ref in enumerate(found)
        ]
        for copy in waiting[i]:
            copy.start()
    for copies in waiting.values():
        for copy in copies:
            copy.wait()


def sum_shapes(count, tokens, width, groups, paired):
    if not paired:
        return [shape_of((count, tokens, width), BF16)]
    one = shape_of((tokens // groups, width), BF16)
    return [one] * (count // 2 * groups) + [
        shape_of((count // 2 - 1, tokens, width), BF16),
        shape_of((1, tokens, width), BF16),
    ]


def sum_targets(outs, place_ref, m, groups, paired):
    if not paired:
        return [outs[0].at[place_ref[1] ^ m]]
    if m == 2 * (outs[-2].shape[0] + 1) - 1:
        return [outs[-1].at[0]]
    if m % 2:
        return [outs[-2].at[m // 2]]
    return outs[m // 2 * groups : (m // 2 + 1) * groups]


def sums_of(result, count, groups, paired):
    if not paired:
        return result[0], None
    even = {m: result[m // 2 * groups : (m // 2 + 1) * groups] for m in range(0, count, 2)}
    return even, result[-2:]


def expert_middle(
    place, gathered, meta, expert_gate, expert_up, grad_hidden, capacity, groups, paired
):
    experts, width, hidden = expert_gate.shape
    count = meta.shape[0]
    tokens = meta.shape[-1]
    rows = count * capacity
    chunk = rows // 2 if rows % 32 == 0 else rows
    numbers = [len(found) for found in gathered]
    arrays = [array for found in gathered for array in found]

    def body(place_ref, meta_ref, gate_ref, up_ref, gh_ref, *rest):
        refs, (h_ref, *outs) = rest[: len(arrays)], rest[len(arrays) : -5]
        ring, picked, made, sem, out_sem = rest[-5:]
        expert = pl.program_id(0)

        @pl.when(expert == 0)
        def _():
            pick_rows(
                lambda m: refs[sum(numbers[:m]) : sum(numbers[: m + 1])],
                meta_ref, ring, sem, picked, capacity, False,
            )

        for c in range(rows // chunk):
            at = slice(c * chunk, (c + 1) * chunk)
            x = picked[expert, at]
            gate = dot_nn(x, gate_ref[0])
            up = dot_nn(x, up_ref[0])
            sigma = sigmoid(gate)
            value = gate * sigma
            grad = gh_ref[0, at].astype(F32)
            h_ref[0, at] = (value * up).astype(BF16)
            grad_gate = (grad * up * (sigma + value * (1.0 - sigma))).astype(BF16)
            grad_up = (grad * value).astype(BF16)
            made[expert, at] = (
                dot_nt(grad_gate, gate_ref[0]) + dot_nt(grad_up, up_ref[0])
            ).astype(BF16)

        @pl.when(expert == experts - 1)
        def _():
            send_combined(
                meta_ref, made, ring, out_sem, capacity,
                lambda m: sum_targets(outs, place_ref, m, groups, paired),
            )

    shapes = sum_shapes(count, tokens, width, groups, paired)
    result = kernel_call(
        body,
        "expert_middle",
        (experts,),
        [
            whole_block(meta.shape),
            pl.BlockSpec((1, width, hidden), lambda e, s: (e, 0, 0)),
            pl.BlockSpec((1, width, hidden), lambda e, s: (e, 0, 0)),
            pl.BlockSpec((1, rows, hidden), lambda e, s: (e, 0, 0)),
        ]
        + [ANYWHERE] * len(arrays),
        [pl.BlockSpec((1, rows, hidden), lambda e, s: (e, 0, 0))] + [ANYWHERE] * len(shapes),
        [shape_of((experts, rows, hidden), BF16)] + shapes,
        scratch=[
            pltpu.VMEM((2, tokens, width), BF16),
            pltpu.VMEM((experts, rows, width), BF16),
            pltpu.VMEM((experts, rows, width), BF16),
            pltpu.SemaphoreType.DMA((count, max(numbers))),
            pltpu.SemaphoreType.DMA((2, groups)),
        ],
        prefetch=1,
        flops=2 * experts * rows * (4 * hidden + tokens) * width,
        moved=4 * experts * hidden * width + 4 * experts * rows * width,
    )(place, meta, expert_gate, expert_up, grad_hidden, *arrays)
    return (result[0],) + sums_of(result[1:], count, groups, paired)


def expert_produce(
    place, hidden_rows, meta, expert_down, capacity, first, last, groups, paired, before=None
):
    experts, hidden, width = expert_down.shape
    count = meta.shape[0]
    tokens = meta.shape[-1]
    rows = count * capacity
    held = before.shape[0] if before is not None else 0

    def body(place_ref, meta_ref, h_ref, w_ref, *rest):
        expert = pl.program_id(0) + first
        result = dot_nn(h_ref[0], w_ref[0])
        if held:
            before_ref, outs, (ring, made, sem, before_sem) = rest[0], rest[1:-4], rest[-4:]
            copy = pltpu.make_async_copy(before_ref, made.at[pl.ds(0, held)], before_sem)

            @pl.when(expert == first)
            def _():
                copy.start()

        else:
            (out_ref,) = rest
        for m in range(count):
            named = one_hot(meta_ref[m, 0, pl.ds(expert, 1)], capacity)
            weight = jnp.sum(
                jnp.where(named, meta_ref[m, 1, pl.ds(expert, 1)], 0.0), axis=1, keepdims=True
            )
            at = slice(m * capacity, (m + 1) * capacity)
            value = (weight * result[at]).astype(BF16)
            if held:
                made[expert, at] = value
            else:
                out_ref[0, at] = value

        if held:

            @pl.when(expert == last - 1)
            def _():
                copy.wait()
                send_combined(
                    meta_ref, made, ring, sem, capacity,
                    lambda m: sum_targets(outs, place_ref, m, groups, paired),
                )

    if held:
        shapes = sum_shapes(count, tokens, width, groups, paired)
        out_specs = [ANYWHERE] * len(shapes)
    else:
        shapes = [shape_of((last - first, rows, width), BF16)]
        out_specs = [pl.BlockSpec((1, rows, width), lambda e, s: (e, 0, 0))]
    result = kernel_call(
        body,
        "expert_produce",
        (last - first,),
        [
            whole_block(meta.shape),
            pl.BlockSpec((1, rows, hidden), lambda e, s: (e + first, 0, 0)),
            pl.BlockSpec((1, hidden, width), lambda e, s: (e + first, 0, 0)),
        ]
        + ([ANYWHERE] if held else []),
        out_specs,
        shapes,
        scratch=[
            pltpu.VMEM((2, tokens, width), BF16),
            pltpu.VMEM((experts, rows, width), BF16),
            pltpu.SemaphoreType.DMA((2, groups)),
            pltpu.SemaphoreType.DMA,
        ]
        if held
        else [],
        prefetch=1,
        flops=2 * (last - first) * rows * hidden * width,
        moved=2 * experts * hidden * width + 2 * experts * rows * width,
    )(place, meta, hidden_rows, expert_down, *([before] if held else []))
    return sums_of(result, count, groups, paired) if held else result[0]


def project_out_back(pieces, mixed, upstream, gain, w_out, down, up, attended, mids):
    splits, groups, shard, part = attended.shape
    width = splits * part
    rank = down.shape[1]
    rows = groups * shard
    number = len(pieces[0])

    def body(up_stream_ref, gain_ref, w_ref, down_ref, up_ref, mixed_ref, att_ref, mid_ref, *rest):
        refs, rest = rest[: groups * number], rest[groups * number :]
        gm_ref, gdown_ref, gup_ref, out_ref, low, held, sem = rest
        copies = [
            pltpu.make_async_copy(w_ref.at[pl.ds(z * part, part)], held.at[z], sem.at[z])
            for z in range(splits)
        ]
        for copy in copies:
            copy.start()
        smalls = []
        for g in range(groups):
            total = refs[g * number][...].astype(F32)
            for ref in refs[g * number + 1 : (g + 1) * number]:
                total += ref[...].astype(F32)
            grad = up_stream_ref[g].astype(F32) + norm_back(mixed_ref[g], gain_ref[...], total)
            gm_ref[g] = grad
            grad = grad.astype(BF16)
            low[g * shard : (g + 1) * shard] = grad
            small = (ADAPTER_SCALE * dot_nt(up_ref[g], grad)).astype(BF16)
            smalls.append(small)
            gup_ref[g] = (ADAPTER_SCALE * dot_nn(mid_ref[g], grad)).astype(BF16)
        for z in range(splits):
            columns = slice(z * part, (z + 1) * part)
            copies[z].wait()
            result = dot_nt(low[...], held[z])
            for g in range(groups):
                out_ref[z, g] = (
                    result[g * shard : (g + 1) * shard] + dot_tn(smalls[g], down_ref[g, :, columns])
                ).astype(BF16)
                gdown_ref[g, :, columns] = dot_nn(smalls[g], att_ref[z, g]).astype(BF16)

    return kernel_call(
        body,
        "project_out_back",
        (1,),
        [
            whole_block(upstream.shape),
            whole_block((1, width)),
            ANYWHERE,
            whole_block(down.shape),
            whole_block(up.shape),
            whole_block(mixed.shape),
            whole_block(attended.shape),
            whole_block(mids.shape),
        ]
        + [whole_block((shard, width))] * (groups * number),
        [
            whole_block((groups, shard, width)),
            whole_block((groups, rank, width)),
            whole_block((groups, rank, width)),
            whole_block(attended.shape),
        ],
        [
            shape_of((groups, shard, width), F32),
            shape_of((groups, rank, width), BF16),
            shape_of((groups, rank, width), BF16),
            shape_of(attended.shape, BF16),
        ],
        scratch=[
            pltpu.VMEM((rows, width), BF16),
            pltpu.VMEM((splits, part, width), BF16),
            pltpu.SemaphoreType.DMA((splits,)),
        ],
        flops=2 * rows * width * width,
        moved=2 * width * width,
    )(
        upstream, gain, w_out, down, up, mixed, attended, mids,
        *[array for found in pieces for array in found],
    )


def adapter_grads(place, group, grads, normed, ups, into):
    listed = is_list(grads)
    splits, (_, shard, part) = piece_shape(grads)
    width = splits * part
    own = ups.shape[1]
    devices = into.shape[0]
    rank = own // 3
    slice_width = width // devices

    def body(place_ref, normed_ref, up_ref, *rest):
        refs, (_, small_ref, down_ref, low) = rest[:splits], rest[splits:]
        for which in range(3):
            for r in range(splits):
                owner = lax.rem(place_ref[0] + r, splits) if listed else r
                low[:, pl.ds(pl.multiple_of(owner * part, part), part)] = refs[r][which]
            at = slice(which * rank, (which + 1) * rank)
            small = (ADAPTER_SCALE * dot_nt(up_ref[at], low[...])).astype(BF16)
            small_ref[at] = small
            result = dot_nn(small, normed_ref[...]).astype(BF16)
            for e in range(devices):
                down_ref[e, at] = result[:, e * slice_width : (e + 1) * slice_width]

    return kernel_call(
        body,
        "adapter_grads",
        (1,),
        [
            pl.BlockSpec((shard, width), lambda i, s: (group, 0)),
            group_block(ups.shape, group),
        ]
        + piece_specs(grads, (3, shard, part), lambda i, s: (0, 0, 0))
        + [ANYWHERE],
        [
            whole_block((own, shard)),
            pl.BlockSpec((devices, None, own, slice_width), lambda i, s: (0, group, 0, 0)),
        ],
        [shape_of((own, shard), BF16), shape_of(into.shape, BF16)],
        scratch=[pltpu.VMEM((shard, width), BF16)],
        prefetch=1,
        aliases={3 + splits: 1},
        flops=12 * shard * rank * width,
        moved=6 * shard * width,
    )(place, normed, ups, *piece_arrays(grads, splits), into)


def project_first_back(group, grads, smalls, downs, w_qkv, tokens, gain, grad_mixed, into=None):
    splits, _, shard, part = grads.shape
    width = splits * part
    rank = downs.shape[1] // 3
    groups = tokens.shape[0]

    def body(down_ref, w_ref, tok_ref, gain_ref, mixed_ref, small_ref, grad_ref, *rest):
        out_ref, low, held, sem = rest[-4:]

        def copy(p, i):
            at = pl.ds(i * part, part)
            return pltpu.make_async_copy(w_ref.at[p, at], held.at[p, at], sem.at[p, i])

        for p in range(3):
            for i in range(splits):
                copy(p, i).start()
        totals = [None] * splits
        for p in range(3):
            for z in range(splits):
                low[:, z * part : (z + 1) * part] = grad_ref[z, p]
            at = slice(p * rank, (p + 1) * rank)
            small = dot_tn(small_ref[at], down_ref[at])
            for i in range(splits):
                copy(p, i).wait()
                columns = slice(i * part, (i + 1) * part)
                result = dot_nt(low[...], held[p, columns]) + small[:, columns]
                totals[i] = result if p == 0 else totals[i] + result
        total = jnp.concatenate(totals, axis=1)
        out_ref[...] = mixed_ref[...] + norm_back(tok_ref[...].astype(F32), gain_ref[...], total)

    return kernel_call(
        body,
        "project_first_back",
        (1,),
        [
            group_block(downs.shape, group),
            ANYWHERE,
            group_block(tokens.shape, group),
            whole_block((1, width)),
            group_block(grad_mixed.shape, group),
            whole_block((3 * rank, shard)),
            whole_block(grads.shape),
        ]
        + ([ANYWHERE] if into is not None else []),
        pl.BlockSpec((None, shard, width), lambda i: (group, 0, 0)),
        shape_of((groups, shard, width), F32),
        scratch=[
            pltpu.VMEM((shard, width), BF16),
            pltpu.VMEM((3, width, width), BF16),
            pltpu.SemaphoreType.DMA((3, splits)),
        ],
        aliases={7: 0} if into is not None else None,
        flops=6 * shard * width * width,
        moved=6 * width * width,
    )(
        downs, w_qkv, tokens, gain, grad_mixed, smalls, grads,
        *([into] if into is not None else []),
    )


def local(
    tokens,
    cotangent,
    lengths,
    adapter_choice,
    expert_ids,
    gate_weights,
    attn_gain,
    moe_gain,
    query_gain,
    key_gain,
    w_qkv,
    w_out,
    expert_gate,
    expert_up,
    expert_down,
    adapt_down,
    first_down,
    second_down,
    adapt_up,
    first_up,
    second_up,
):
    groups, shard, width = tokens.shape
    splits = lax.axis_size("seq")
    devices = lax.axis_size("exp")
    here = lax.axis_index("seq")
    total = shard * splits
    part = width // splits
    rows = groups * shard
    sets, projections, slice_width, rank = adapt_down.shape
    local_experts = expert_gate.shape[0]
    experts = local_experts * devices
    top = expert_ids.shape[-1]
    capacity = 3 * rows * top // (2 * experts)
    listed = [False] * groups

    position = lax.axis_index("exp")
    place = jnp.stack([here, position]).astype(jnp.int32)
    flat_tokens = tokens.reshape(rows, width)
    gain_row = attn_gain.reshape(1, width)
    moe_row = moe_gain.reshape(1, width)
    query_row = query_gain.reshape(1, HEAD)
    key_row = key_gain.reshape(1, HEAD)

    paired = devices == 8 and groups == 2
    own_positions = here * shard + jnp.arange(shard, dtype=jnp.int32)
    own_live = own_positions[None, :] < lengths[:, None]

    base, _, normed = project_first(
        place, flat_tokens, gain_row, w_qkv, groups, splits, listed
    )
    raw = [forward_seq(base[0])]

    adapt_down_low, adapt_up_low, ids, gates = after(
        (adapt_down, adapt_up, expert_ids, gate_weights), normed
    )
    ids = ids.reshape(rows, top).T
    gates = gates.reshape(rows, top).T
    choice = adapter_choice.astype(F32).reshape(1, groups * sets)
    choice = jnp.pad(choice, ((0, 0), (0, rows - groups * sets)))
    routed = route(ids, gates, choice, experts)
    down_rows = jnp.swapaxes(adapt_down_low.astype(BF16), 2, 3)
    up_rows = adapt_up_low.astype(BF16)
    own = 3 * rank
    blocks = [
        jnp.concatenate([found.reshape(-1, slice_width) for found in sources])
        for sources in (
            (down_rows[:, :3], down_rows[:, 3], routed),
            (up_rows[:, :3], up_rows[:, 3]),
        )
    ]
    if paired:
        all_blocks = gather_far(blocks, gather_near(blocks))
        all_downs, all_ups = ([found[g] for found in all_blocks] for g in range(2))
    else:
        cut = blocks[0].shape[0]
        all_downs = [found[0][:cut] for found in gather_whole(blocks)]
        all_ups = [found[0][cut:] for found in gather_whole(blocks)]
    chosen = jnp.sum(adapter_choice * jnp.arange(sets, dtype=jnp.int32)[None, :], axis=1)
    picks = jnp.concatenate([chosen, position.reshape(1)]).astype(jnp.int32)
    sections = [(0, own), (sets * own, rank)]
    downs, out_downs, mids = pick_sets(all_downs, picks, groups, sections, normed)
    ups, out_ups, _ = pick_sets(after(all_ups, mids), picks, groups, sections, normed)
    all_mids = by_distance(jnp.stack(forward_seq([mids] * splits)))

    live_rows = after(own_live, mids)
    upstream = jnp.where(live_rows[:, :, None], cotangent, jnp.zeros((), BF16))
    upstream = [upstream[g] for g in range(groups)]
    routes = jnp.stack([found[sets * (own + rank) :] for found in after(all_downs, mids)])
    routes = routes.reshape(devices, 3 * experts + 16, rows)
    choices = by_relative(routes[:, 3 * experts, : groups * sets])
    choices = choices.reshape(devices, groups, sets)
    meta = routes[:, : 3 * experts].reshape(devices, 3, experts, rows)
    meta = lax.dynamic_slice_in_dim(meta, position * local_experts, local_experts, axis=2)
    meta = meta.astype(F32)
    meta = jnp.stack([meta[:, 0], meta[:, 1] + meta[:, 2]], axis=1)
    blocks = jnp.arange(splits, dtype=jnp.int32)
    frequency = ROPE_BASE ** (-(2.0 / HEAD) * jnp.arange(HEAD // 2, dtype=F32))
    tables = []
    for g in range(groups):
        positions = blocks[:, None] * shard + jnp.arange(shard, dtype=jnp.int32)[None, :]
        angles = after(positions, normed).reshape(total, 1).astype(F32) * frequency[None, :]
        cosine, sine = jnp.cos(angles), jnp.sin(angles)
        tables.append(
            (
                positions.reshape(1, total),
                jnp.concatenate([cosine, cosine], axis=1),
                jnp.concatenate([-sine, sine], axis=1),
            )
        )

    raw[0], all_mids, meta, choices, tables = lax.optimization_barrier(
        (raw[0], all_mids, meta, choices, tables)
    )
    for g in range(1, groups):
        raw.append(forward_seq(after(base[g], raw[g - 1])))
    own_ups = lax.dynamic_slice_in_dim(ups, here * part, part, axis=2)
    own_ups = own_ups.reshape(groups, 3, rank, part)

    saved, heads_rows = [], []
    for g in range(groups):
        if g:
            raw[g] = after(raw[g], heads_rows)
        att, kept = attend(
            lengths[g : g + 1],
            raw[g],
            all_mids[:, g],
            own_ups[g],
            query_row,
            key_row,
            *tables[g],
        )
        saved.append(kept)
        heads_rows.append(att)
        if paired and g == 0:
            near = gather_near(upstream)
            far = far_of(after(near, att))
            cot_rows = gather_far(upstream, near, far)
    if not paired:
        cot_rows = gather_whole(upstream)
    heads_rows = jnp.stack(heads_rows, axis=1)
    if paired:
        heads_rows, cot_rows = lax.optimization_barrier((heads_rows, cot_rows))
    attended = lax.all_to_all(heads_rows, "seq", 0, 0)
    grad_hidden = expert_grad_hidden(
        cot_rows, after(meta, heads_rows), expert_down, capacity
    )
    attended, grad_hidden = lax.optimization_barrier((attended, grad_hidden))
    mixed, mid_out, moe_rows = project_out(
        attended, w_out, out_downs, out_ups, tokens, moe_row
    )
    gathered = gather_far(moe_rows, gather_near(moe_rows)) if paired else gather_whole(moe_rows)
    half = local_experts // 2

    hidden, parts, others = expert_middle(
        place,
        gathered,
        meta,
        expert_gate,
        expert_up,
        grad_hidden,
        capacity,
        groups,
        paired,
    )
    if paired:
        far, near, beside = near_sums_of(parts, others)
        produced = expert_produce(
            place, after(hidden, far, near), meta, expert_down, capacity, 0, half, groups, paired
        )
        far, near = send_near(far, near)
        far, produced = lax.optimization_barrier((far, produced))
        joined = send_joined(joined_sums_of(parts, beside, far))
        grad_pieces = [
            [parts[0][g], beside[0][g], near[g], joined[g]] for g in range(groups)
        ]
    else:
        summed = lax.psum_scatter(parts, "exp").reshape(groups, shard, width)
        grad_pieces = [[summed[g]] for g in range(groups)]
        produced = expert_produce(
            place, hidden, meta, expert_down, capacity, 0, half, groups, paired
        )
    grad_mixed, grad_out_downs, grad_out_ups, grad_att = project_out_back(
        grad_pieces, mixed, jnp.stack(upstream), moe_row, w_out, out_downs, out_ups, attended, mid_out
    )
    out_parts, out_others = expert_produce(
        place, hidden, after(meta, grad_mixed), expert_down, capacity, half, local_experts,
        groups, paired, produced,
    )
    grad_att = lax.all_to_all(grad_att, "seq", 0, 0)
    grad_raw, gups = [], []
    for g in range(groups):
        if g:
            grad_att = after(grad_att, gups)
        back, gup = attend_back(
            lengths[g : g + 1],
            grad_att,
            g,
            saved[g],
            all_mids[:, g],
            rank,
            query_row,
            key_row,
            *tables[g],
        )
        gups.append(gup)
        if paired and not g:
            out_far, out_near, out_beside = near_sums_of(out_parts, after(out_others, gup))
        if paired and g:
            out_far, out_near = send_near(out_far, out_near)
            back, out_far, out_near = lax.optimization_barrier((back, out_far, out_near))
        grad_raw.append(forward_seq(after(back, grad_raw) if g else back))
    if paired:
        joined_sums = joined_sums_of(out_parts, out_beside, out_far)
        out_joined = send_joined(joined_sums)
        normed = after(normed, joined_sums)
    gups = jnp.stack(after(gups, grad_raw[0]))
    wide_ups = lax.dynamic_update_slice_in_dim(
        jnp.zeros((groups, own, width), BF16), gups, here * part, axis=2
    )
    early = jnp.concatenate([grad_out_downs, wide_ups, grad_out_ups], axis=1)
    early = jnp.moveaxis(early.reshape(groups, -1, devices, slice_width), 2, 0)

    late = jnp.pad(early, ((0, 0), (0, 0), (own, 0), (0, 0)))
    grad_input = None
    for g in range(groups):
        small, late = adapter_grads(place, g, grad_raw[g], normed, ups, late)
        if g == groups - 1:
            late = lax.all_to_all(late, "exp", 0, 0)
        grad_input = project_first_back(
            g, grad_raw[g], small, downs, w_qkv, tokens, gain_row, grad_mixed, grad_input
        )
        if g < groups - 1:
            late, grad_input = lax.optimization_barrier((late, grad_input))
            if paired:
                outputs = [
                    mixed[g]
                    + functools.reduce(
                        jnp.add,
                        [
                            value.astype(F32)
                            for value in (out_parts[0][g], out_beside[0][g], out_near[g], out_joined[g])
                        ],
                    )
                    for g in range(groups)
                ]
                output = jnp.stack(outputs).astype(BF16)
            else:
                out_sum = lax.psum_scatter(out_parts, "exp").reshape(groups, shard, width)
                output = (mixed + out_sum.astype(F32)).astype(BF16)
            late, output = lax.optimization_barrier((late, output))
    late, grad_input = lax.optimization_barrier((late, grad_input))
    pieces = jnp.einsum("dgk,dgrw->krw", choices, late, preferred_element_type=F32)
    pieces = pieces.astype(BF16)
    pieces = pieces.reshape(splits, -1, slice_width)
    order = (here + jnp.arange(splits)) % splits
    pieces = list(jnp.take(pieces, order, axis=0))
    summed = add_low(*forward_seq(pieces))
    in_sets = by_distance(jnp.stack(forward_seq([summed] * splits)))
    in_sets = in_sets.reshape(sets, 2, projections, rank, slice_width).astype(F32)
    shard_down = jnp.swapaxes(in_sets[:, 0], 2, 3)
    shard_up = in_sets[:, 1]
    new_first_down, new_second_down, new_down = adam_update(
        adapt_down, shard_down, first_down, second_down, RATE_DOWN
    )
    new_first_up, new_second_up, new_up = adam_update(
        adapt_up, shard_up, first_up, second_up, RATE_UP
    )
    return (
        output,
        grad_input,
        new_first_down,
        new_second_down,
        new_down,
        new_first_up,
        new_second_up,
        new_up,
    )


def solution(mesh):
    in_specs = (
        P("exp", "seq", None),
        P("exp", "seq", None),
        P("exp"),
        P("exp", None),
        P("exp", "seq", None, None, None),
        P("exp", "seq", None, None, None),
        P(),
        P(),
        P(),
        P(),
        P(),
        P(),
        P("exp", None, None),
        P("exp", None, None),
        P("exp", None, None),
        P(None, None, "exp", None),
        P(None, None, "exp", None),
        P(None, None, "exp", None),
        P(None, None, None, "exp"),
        P(None, None, None, "exp"),
        P(None, None, None, "exp"),
    )
    out_specs = (
        P("exp", "seq", None),
        P("exp", "seq", None),
        P(None, None, "exp", None),
        P(None, None, "exp", None),
        P(None, None, "exp", None),
        P(None, None, None, "exp"),
        P(None, None, None, "exp"),
        P(None, None, None, "exp"),
    )
    return jax.shard_map(local, mesh=mesh, in_specs=in_specs, out_specs=out_specs, check_vma=False)
```
